32 devices in a mesh: ctx: 16 (over z, x, core), shard: 2 (over y).
Axes of the slice: x: 2, y: 2, z: 4, core: 2. Of those that a mesh axis runs over, the one named last changes fastest.
Arguments:
- tokens: bfloat16 [2, 2048, 768], P('shard', 'ctx'), may hold values from -6 to 6
- gain_one: bfloat16 [768], P('shard'), may hold values from 0.099609375 to 1.8984375
- w_qkv: bfloat16 [768, 2304], P('shard'), may hold values from -0.21875 to 0.21875
- w_out: bfloat16 [768, 768], P('shard'), may hold values from -6 to 6
- gain_two: bfloat16 [768], P('shard'), may hold values from 0.099609375 to 1.8984375
- w_in: bfloat16 [768, 2304], P('shard'), may hold values from -0.21875 to 0.21875
- w_down: bfloat16 [1152, 768], P('shard'), may hold values from -0.1875 to 0.1875
- cotangent: bfloat16 [2, 2048, 768], P('shard', 'ctx'), may hold values from -6 to 6
Outputs:
- result: float32 [2, 2048, 768], P('shard', 'ctx')
- grad_tokens: float32 [2, 2048, 768], P('shard', 'ctx')
- grad_gain_one: float32 [768], P('shard')
- grad_w_qkv: float32 [768, 2304], P('shard')
- grad_w_out: float32 [768, 768], P('shard')
- grad_gain_two: float32 [768], P('shard')
- grad_w_in: float32 [768, 2304], P('shard')
- grad_w_down: float32 [1152, 768], P('shard')
The draws below stay inside these ranges and needn't reach their ends.
All inputs are finite; a program needn't handle non-finite values.
Results may differ from the reference program's by a relative error of at most 0.024.
Values may be sent and summed in bfloat16 or wider, within the bound.
No kernel may reach another device: no remote copies, remote signals or barrier semaphores. Data moves between devices by JAX's collectives and lax.ppermute only.
A program may use at most 192 MiB of HBM per device.

```python
import math
import jax
import jax.numpy as jnp
from jax import lax

D = 768
HEADS = 12
HEAD_DIM = 64
FF = 1152
LENGTH = 2048
SEQS = 2


def steps_of(own_key, dims, pieces, low, high):
    def one(dim, blocks):
        heights = jax.random.uniform(jax.random.fold_in(jax.random.fold_in(own_key, 6), dim), (blocks,), jnp.float32, low / len(pieces), high / len(pieces))
        return jnp.repeat(jnp.exp(heights), dims[dim] // blocks).reshape((-1,) + (1,) * (len(dims) - dim - 1))

    level = one(*pieces[0])
    for cut in pieces[1:]:
        level = level * one(*cut)
    return level


def scatter_about(rng, shape, scale, limit, shards=(), kind=jnp.bfloat16):
    entries = scale * jax.random.normal(rng, shape, jnp.float32)
    if shards:
        entries = entries * steps_of(rng, shape, shards, -0.22, 0.18)
    return jnp.clip(entries, -limit, limit).astype(kind)


def setup_inputs(seed: int = 0) -> dict:
    splits = jax.random.split(jax.random.key(seed), 9)
    return {
        "tokens": scatter_about(splits[0], (SEQS, LENGTH, D), 1.0, 6.0, ((0, 2), (1, 16))),
        "gain_one": jnp.clip(1.0 + 0.18 * jax.random.normal(splits[1], (D,), jnp.float32), 0.099609375, 1.8984375).astype(jnp.bfloat16),
        "w_qkv": scatter_about(splits[2], (D, 3 * D), D ** -0.5, 0.21875, ((0, 2),)),
        "w_out": scatter_about(splits[3], (D, D), (max(1, D // 512)) ** -0.5, 6.0, ((0, 2),)),
        "gain_two": jnp.clip(1.0 + 0.18 * jax.random.normal(splits[4], (D,), jnp.float32), 0.099609375, 1.8984375).astype(jnp.bfloat16),
        "w_in": scatter_about(splits[5], (D, 2 * FF), D ** -0.5, 0.21875, ((0, 2),)),
        "w_down": scatter_about(splits[6], (FF, D), FF ** -0.5, 0.1875, ((0, 2),)),
        "cotangent": scatter_about(splits[7], (SEQS, LENGTH, D), 1.0, 6.0, ((0, 2), (1, 16))),
    }


EPS = 1e-05
THETA = 160000.0
HI = lax.Precision.HIGHEST

@jax.custom_vjp
def low(v):
    return lax.optimization_barrier(v.astype(jnp.bfloat16)).astype(jnp.float32)

@jax.custom_vjp
def low_back(v):
    return v

def low_keep(v):
    return (low(v), None)

def low_pass(kept, grad):
    return (grad,)

def back_keep(v):
    return (v, None)

def back_low(kept, grad):
    return (low(grad),)
low.defvjp(low_keep, low_pass)
low_back.defvjp(back_keep, back_low)

def matmul(left, right):
    return jnp.dot(left, right, precision=HI, preferred_element_type=jnp.float32)

def layer_norm(values, gain):
    mean = lax.optimization_barrier(jnp.mean(values, axis=-1, keepdims=True))
    centred = values - mean
    spread = lax.optimization_barrier(jnp.mean(centred * centred, axis=-1, keepdims=True))
    return centred * lax.rsqrt(spread + EPS) * gain

def rotary(length):
    half = HEAD_DIM // 2
    freq = THETA ** (-jnp.arange(half, dtype=jnp.float32) * (2.0 / HEAD_DIM))
    places = jnp.arange(length, dtype=jnp.int32).astype(jnp.float32)
    angle = places[:, None] * freq[None, :]
    angle = jnp.concatenate([angle, angle], axis=1)
    return (jnp.cos(angle), jnp.sin(angle))

def rotate(values, cosine, sine):
    half = HEAD_DIM // 2
    turned = jnp.concatenate([-values[..., half:], values[..., :half]], axis=-1)
    return values * cosine[:, None, :] + turned * sine[:, None, :]

def attention(query, key, value):
    length = query.shape[0]
    block = math.gcd(length, 512)
    factor = HEAD_DIM ** (-0.5)

    def one_block(rows_q):
        scores = low_back(jnp.einsum('qhd,khd->hqk', rows_q, key, precision=HI) * factor)
        probs = low(jax.nn.softmax(scores, axis=-1))
        return jnp.einsum('hqk,khd->qhd', probs, value, precision=HI)
    blocks = lax.map(jax.checkpoint(one_block), query.reshape(length // block, block, HEADS, HEAD_DIM))
    return blocks.reshape(length, HEADS * HEAD_DIM)

def sequence_layer(inputs, gain_one, w_qkv, w_out, gain_two, w_in, w_down):
    length = inputs.shape[0]
    h_one = low(layer_norm(inputs, gain_one))
    qkv = low_back(matmul(h_one, w_qkv)).reshape(length, 3, HEADS, HEAD_DIM)
    cosine, sine = rotary(length)
    query = low(rotate(qkv[:, 0], cosine, sine))
    key = low(rotate(qkv[:, 1], cosine, sine))
    value = low(qkv[:, 2])
    attended = low(low_back(attention(query, key, value)))
    middle = inputs + low_back(matmul(attended, w_out))
    h_two = low(layer_norm(middle, gain_two))
    gate_up = low_back(matmul(h_two, w_in))
    mixed = low(jax.nn.gelu(gate_up[:, :FF], approximate=False) * gate_up[:, FF:])
    return middle + low_back(matmul(mixed, w_down))

def reference(tokens, gain_one, w_qkv, w_out, gain_two, w_in, w_down, cotangent):
    params = (gain_one.astype(jnp.float32), w_qkv.astype(jnp.float32), w_out.astype(jnp.float32), gain_two.astype(jnp.float32), w_in.astype(jnp.float32), w_down.astype(jnp.float32))

    def forward(inputs, g_one, wq, wo, g_two, wi, wd):

        def step(carry, sequence):
            return (carry, jax.checkpoint(sequence_layer)(sequence, g_one, wq, wo, g_two, wi, wd))
        _, outputs = lax.scan(step, jnp.zeros((), jnp.float32), inputs)
        return outputs
    result, pullback = jax.vjp(forward, tokens.astype(jnp.float32), *params)
    grads = pullback(cotangent.astype(jnp.float32))
    return (result, grads[0], grads[1], grads[2], grads[3], grads[4], grads[5], grads[6])
```

```python
import functools
import math

import jax
import jax.numpy as jnp
from jax import lax
from jax.experimental import pallas as pl
from jax.experimental.pallas import tpu as pltpu
from jax.sharding import Mesh, PartitionSpec as P

D = 768
HEADS = 12
HEAD_DIM = 64
FF = 1152
EPS = 1e-05
THETA = 160000.0

TP = 4
GH = HEADS // TP
GW = GH * HEAD_DIM
WC = 640
CTX = ("zo", "z", "x", "core")
BF = jnp.bfloat16
F32 = jnp.float32
VMEM_LIMIT = 56 * 1024 * 1024

KEY_AT = ((0, 0), (0, 1), (1, 0))
VALUE_AT = ((1, 1), (2, 0), (2, 1))


def dot(a, b):
    return jnp.dot(a, b, preferred_element_type=F32)


def dot_nt(a, b):
    return lax.dot_general(a, b, (((1,), (1,)), ((), ())), preferred_element_type=F32)


def dot_tn(a, b):
    return lax.dot_general(a, b, (((0,), (0,)), ((), ())), preferred_element_type=F32)


def call(body, outs, n_smem, ins, scratch=(), any_ins=(), flops=0, bytes_accessed=0, name=None):
    specs = []
    for i in range(len(ins)):
        if i < n_smem:
            specs.append(pl.BlockSpec(memory_space=pltpu.SMEM))
        elif i in any_ins:
            specs.append(pl.BlockSpec(memory_space=pl.ANY))
        else:
            specs.append(pl.BlockSpec(memory_space=pltpu.VMEM))
    return pl.pallas_call(
        body,
        out_shape=[jax.ShapeDtypeStruct(s, t) for s, t in outs],
        in_specs=specs,
        out_specs=[pl.BlockSpec(memory_space=pltpu.VMEM)] * len(outs),
        scratch_shapes=list(scratch),
        compiler_params=pltpu.CompilerParams(vmem_limit_bytes=VMEM_LIMIT),
        cost_estimate=pl.CostEstimate(
            flops=flops, bytes_accessed=bytes_accessed, transcendentals=0
        ),
        name=name,
    )(*ins)


def normalise(values):
    mean = jnp.mean(values, axis=-1, keepdims=True)
    centred = values - mean
    spread = jnp.mean(centred * centred, axis=-1, keepdims=True)
    scale = lax.rsqrt(spread + EPS)
    return centred * scale, scale


def normalise_back(grad_unit, unit, scale):
    return scale * (
        grad_unit
        - jnp.mean(grad_unit, axis=-1, keepdims=True)
        - unit * jnp.mean(grad_unit * unit, axis=-1, keepdims=True)
    )


def turn(tile, cosine, signed_sine, first_half):
    swapped = jnp.where(first_half, pltpu.roll(tile, 96, 1), pltpu.roll(tile, 32, 1))
    return tile * cosine + swapped * signed_sine


def lane_masks(rows):
    lane = lax.broadcasted_iota(jnp.int32, (rows, 128), 1)
    return lax.rem(lane, 64) < 32, lane < 64


def front_kernel(n_w, offs, *refs):
    toks = refs[:TP]
    ws = refs[TP : TP + n_w]
    cos_ref, sin_ref, q_ref, kv_ref, h_ref, w_ref, gains_ref = refs[TP + n_w :]
    rows = toks[0].shape[0]
    part = ws[0].shape[0]
    for i, block in enumerate(ws):
        w_ref[pl.ds(pl.multiple_of(offs[i], part), part), :] = block[...]
    gains = w_ref[:, 512:640].astype(F32).T[64:72]
    gains_ref[...] = gains
    gain = gains[0:1]
    first, low = lane_masks(rows)
    for j in range(TP):
        at = slice(j * rows, (j + 1) * rows)
        unit, _ = normalise(toks[j][...].astype(F32))
        h = (unit * gain).astype(BF)
        h_ref[at, :] = h
        out = dot(h, w_ref[...])
        cosine, sine = cos_ref[at, :], sin_ref[at, :]
        key_a = turn(out[:, 0:128], cosine, sine, first)
        mixed = out[:, 128:256]
        key_b = jnp.where(low, turn(mixed, cosine, sine, first), mixed)
        kv_ref[at, 0:128] = key_a.astype(BF)
        kv_ref[at, 128:256] = key_b.astype(BF)
        kv_ref[at, 256:384] = out[:, 256:384].astype(BF)
        query_a = turn(out[:, 384:512], cosine, sine, first)
        query_b = jnp.where(low, turn(out[:, 512:640], cosine, sine, first), 0.0)
        factor = HEAD_DIM ** (-0.5)
        q_ref[at, 0:128] = (query_a * factor).astype(BF)
        q_ref[at, 128:256] = (query_b * factor).astype(BF)


def half_rows(values_t, head):
    at = head * HEAD_DIM
    rows = values_t[at : at + HEAD_DIM]
    zeros = jnp.zeros_like(rows)
    return jnp.concatenate([rows, zeros] if head % 2 == 0 else [zeros, rows], axis=0)


def forward_kernel(n_kv, q_ref, *refs):
    kvs = refs[:n_kv]
    att_ref, att_t_ref, lse_ref, kv_s, v_t, q_t = refs[n_kv:]
    rows = kvs[0].shape[0]
    block = math.gcd(rows, 256)
    for i, kv in enumerate(kvs):
        kv_s[i * rows : (i + 1) * rows, :] = kv[...]
        v_t[:, i * rows : (i + 1) * rows] = kv[:, 128:384].T
    q_t[...] = q_ref[...].T
    lse_ref[...] = jnp.zeros_like(lse_ref)
    for i in range(rows // block):
        at = slice(i * block, (i + 1) * block)
        for h in range(GH):
            tile = KEY_AT[h][0]
            keys = kv_s[:, tile * 128 : tile * 128 + 128]
            scores = dot(keys, half_rows(q_t[:, at], h))
            top = jnp.max(scores, axis=0, keepdims=True)
            weights = jnp.exp(scores - top)
            total = jnp.sum(weights, axis=0, keepdims=True)
            tile, half = VALUE_AT[h]
            values_t = v_t[(tile - 1) * 128 : tile * 128, :]
            out = dot(values_t, weights.astype(BF))[half * 64 : half * 64 + 64]
            att_t_ref[h * 64 : h * 64 + 64, at] = out / total
            lse_ref[h : h + 1, at] = top + jnp.log(total)
    att_ref[...] = att_t_ref[...].T.astype(BF)


def backward_kernel(n_kv, q_ref, *refs):
    kvs = refs[:n_kv]
    gas = refs[n_kv : n_kv + TP]
    att_t_ref, lse_ref, dkv_ref, dq_ref = refs[n_kv + TP : n_kv + TP + 4]
    kv_s, k_t, q_t, g_t, q_m, g_m, acc, dq_t = refs[n_kv + TP + 4 :]
    rows = kvs[0].shape[0]
    small = gas[0].shape[0]
    block = math.gcd(rows, 256)
    for i, kv in enumerate(kvs):
        kv_s[i * rows : (i + 1) * rows, :] = kv[...]
        k_t[:, i * rows : (i + 1) * rows] = kv[:, 0:256].T
    q_t[...] = q_ref[...].T
    _, low = lane_masks(small)
    for j in range(TP):
        at = slice(j * small, (j + 1) * small)
        g_t[:, at] = gas[j][...].T
        first, second = gas[j][:, 0:128], gas[j][:, 128:256].astype(F32)
        g_m[at, 0:128] = first
        g_m[at, 128:256] = jnp.where(low, second, 0.0).astype(BF)
        g_m[at, 256:384] = jnp.where(low, 0.0, second).astype(BF)
        both = q_ref[at, 0:128].astype(F32)
        q_m[at, 0:128] = jnp.where(low, both, 0.0).astype(BF)
        q_m[at, 128:256] = jnp.where(low, 0.0, both).astype(BF)
        q_m[at, 256:384] = q_ref[at, 128:256]
    dq_t[...] = jnp.zeros_like(dq_t)
    acc[...] = jnp.zeros_like(acc)
    for i in range(rows // block):
        at = slice(i * block, (i + 1) * block)
        for h in range(GH):
            ktile, khalf = KEY_AT[h]
            vtile = VALUE_AT[h][0]
            klanes = slice(ktile * 128, ktile * 128 + 128)
            vlanes = slice(vtile * 128, vtile * 128 + 128)
            scores = dot(kv_s[:, klanes], half_rows(q_t[:, at], h))
            probs = jnp.exp(scores - lse_ref[h : h + 1, at])
            grad_t = half_rows(g_t[:, at], h + 1)
            grad_probs = dot(kv_s[:, vlanes], grad_t)
            own = g_t[(h + 1) * 64 : (h + 2) * 64, at].astype(F32)
            inner = jnp.sum(
                own * att_t_ref[h * 64 : h * 64 + 64, at], axis=0, keepdims=True
            )
            grad_scores = (probs * (grad_probs - inner)).astype(BF)
            lanes = slice(h * 128, h * 128 + 128)
            acc[:, vlanes] += dot(probs.astype(BF), g_m[at, lanes])
            acc[:, klanes] += dot(grad_scores, q_m[at, lanes])
            part = dot(k_t[klanes, :], grad_scores)[khalf * 64 : khalf * 64 + 64]
            dq_t[h * 64 : h * 64 + 64, at] = part * HEAD_DIM ** (-0.5)
    dq_ref[...] = dq_t[...].T
    for i in range(n_kv):
        dkv_ref[i] = acc[i * rows : (i + 1) * rows, :].astype(BF)


def middle_kernel(n_out, n_in, n_down, offs, *refs):
    n_w = n_out + n_in + n_down
    atts = refs[:TP]
    tok_ref, cot_ref, gains_ref = refs[TP : TP + 3]
    ws = refs[TP + 3 : TP + 3 + n_w]
    rest = refs[TP + 3 + n_w :]
    result_ref, gmid_ref, gb_ref, h_ref, mixed_ref, ggu_ref, gain_ref = rest[:7]
    gatts = rest[7 : 7 + TP]
    w_out, w_in, w_down, sems = rest[7 + TP :]
    copies = []
    for i, block in enumerate(ws):
        target = w_out if i < n_out else (w_in if i < n_out + n_in else w_down)
        height = block.shape[0]
        at = pl.ds(pl.multiple_of(offs[i], math.gcd(height, 1024 * 9)), height)
        copies.append(pltpu.make_async_copy(block, target.at[at, :], sems.at[i]))
    for copy in copies:
        copy.start()
    starts = [pl.multiple_of(offs[n_w + j], GW) for j in range(TP)]
    for copy in copies[:n_out]:
        copy.wait()
    middle = tok_ref[...].astype(F32)
    for j in range(TP):
        middle += dot(atts[j][...], w_out[pl.ds(starts[j], GW), :])
    gain = gains_ref[1:2, :]
    unit, scale = normalise(middle)
    h = (unit * gain).astype(BF)
    h_ref[...] = h
    for copy in copies[n_out : n_out + n_in]:
        copy.wait()
    gate = dot(h, w_in[:, :FF])
    up = dot(h, w_in[:, FF:])
    phi = 0.5 * (1.0 + lax.erf(gate * math.sqrt(0.5)))
    active = gate * phi
    mixed = (active * up).astype(BF)
    mixed_ref[...] = mixed
    for copy in copies[n_out + n_in :]:
        copy.wait()
    grad_mixed = dot_nt(cot_ref[...], w_down[...])
    slope = phi + gate * (jnp.exp(-0.5 * gate * gate) * (1.0 / math.sqrt(2.0 * math.pi)))
    grad_gate = (grad_mixed * up * slope).astype(BF)
    grad_up = (grad_mixed * active).astype(BF)
    ggu_ref[:, :FF] = grad_gate
    ggu_ref[:, FF:] = grad_up
    grad_h = dot_nt(grad_gate, w_in[:, :FF]) + dot_nt(grad_up, w_in[:, FF:])
    gain_ref[...] = jnp.broadcast_to(
        jnp.sum(grad_h * unit, axis=0, keepdims=True), gain_ref.shape
    )
    grad_middle = cot_ref[...].astype(F32) + normalise_back(grad_h * gain, unit, scale)
    gmid_ref[...] = grad_middle
    gb = grad_middle.astype(BF)
    gb_ref[...] = gb
    for j in range(TP):
        part = dot_nt(gb, w_out[pl.ds(starts[j], GW), :])
        pad = jnp.zeros((part.shape[0], 256 - GW), F32)
        gatts[j][...] = jnp.concatenate([pad, part], axis=1).astype(BF)
    result_ref[...] = middle + dot(mixed, w_down[...])


def plan(shards):
    pieces = 4 * shards
    up16 = lambda n: -(-n // 16) * 16
    rows_d, rows_f = D // pieces, FF // pieces
    starts = [0, up16(rows_d), 2 * up16(rows_d), 3 * up16(rows_d)]
    starts.append(starts[-1] + up16(rows_f))
    starts.append(starts[-1] + up16(rows_d))
    total = -(-(starts[-1] + 16) // 64) * 64
    return pieces, rows_d, rows_f, starts, total


def ffn_grads_kernel(shards, groups, *refs):
    atts = refs[:TP]
    h_ref, ggu_ref, mixed_ref, cot_ref, gb_ref, gain_ref, out_ref = refs[TP:]
    pieces, rows_d, rows_f, starts, total = plan(shards)
    cot = cot_ref[...]
    h_t = h_ref[...].T
    for b in range(3):
        grad = dot(h_t, ggu_ref[:, b * D : (b + 1) * D]).astype(BF)
        for m in range(pieces):
            out_ref[m, starts[b] : starts[b] + rows_d, :] = grad[m * rows_d : (m + 1) * rows_d]
    grad = dot(mixed_ref[...].T, cot).astype(BF)
    for m in range(pieces):
        out_ref[m, starts[3] : starts[3] + rows_f, :] = grad[m * rows_f : (m + 1) * rows_f]
    gb = gb_ref[...]
    per = GW // rows_d
    for j in range(TP):
        grad = dot(atts[j][...].T, gb).astype(BF)
        for i in range(per):
            out_ref[groups[j] * per + i, starts[4] : starts[4] + rows_d, :] = grad[
                i * rows_d : (i + 1) * rows_d
            ]
    row = jnp.broadcast_to(gain_ref[0:1, :], (total - starts[5], D)).astype(BF)
    for m in range(pieces):
        out_ref[m, starts[5] :, :] = row


def qkv_grads_kernel(pieces, n_sum, *refs):
    parts = refs[:n_sum]
    dq_ref, cos_ref, sin_ref, h_ref, w_ref, grad_w_ref = refs[n_sum : n_sum + 6]
    outs = refs[n_sum + 6 : n_sum + 6 + TP]
    full = refs[n_sum + 6 + TP]
    rows = outs[0].shape[0]
    first, low = lane_masks(rows)
    for j in range(TP):
        at = slice(j * rows, (j + 1) * rows)
        cosine, sine = cos_ref[at, :], -sin_ref[at, :]
        tiles = []
        for t in range(3):
            total = parts[0][at, t * 128 : t * 128 + 128].astype(F32)
            for part in parts[1:]:
                total += part[at, t * 128 : t * 128 + 128].astype(F32)
            if t == 0:
                total = turn(total, cosine, sine, first)
            if t == 1:
                total = jnp.where(low, turn(total, cosine, sine, first), total)
            tiles.append(total)
        for t in range(2):
            tiles.append(turn(dq_ref[at, t * 128 : t * 128 + 128], cosine, sine, first))
        for t, tile in enumerate(tiles):
            tile = tile.astype(BF)
            full[at, t * 128 : t * 128 + 128] = tile
            outs[j][:, t * 128 : t * 128 + 128] = tile
    grad = dot(h_ref[...].T, full[...])
    w = w_ref[...].astype(F32)
    gain = w[:, 576:577]
    lane = lax.broadcasted_iota(jnp.int32, grad.shape, 1)
    by_gain = jnp.sum(grad * w, axis=1, keepdims=True) / gain
    grad = jnp.where(lane < 3 * GW, grad, by_gain).astype(BF)
    height = D // pieces
    for m in range(pieces):
        grad_w_ref[m] = grad[m * height : (m + 1) * height]


def tail_kernel(n_w, offs, *refs):
    grads = refs[:TP]
    tok_ref, gmid_ref, gains_ref = refs[TP : TP + 3]
    ws = refs[TP + 3 : TP + 3 + n_w]
    out_ref, w_all, sems = refs[TP + 3 + n_w :]
    copies = []
    for i, block in enumerate(ws):
        count, height = block.shape[:2]
        at = pl.ds(pl.multiple_of(offs[2 * i + 1], height), height)
        target = w_all.at[pl.ds(offs[2 * i], count), at, :]
        copies.append(pltpu.make_async_copy(block, target, sems.at[i]))
    for copy in copies:
        copy.start()
    unit, scale = normalise(tok_ref[...].astype(F32))
    for copy in copies:
        copy.wait()
    total = jnp.zeros(out_ref.shape, F32)
    for j in range(TP):
        total += dot_nt(grads[j][...], w_all[offs[2 * n_w + j]])
    grad_unit = total * gains_ref[0:1, :]
    out_ref[...] = gmid_ref[...] + normalise_back(grad_unit, unit, scale)


def ffn_unpack_kernel(shards, idx, *refs):
    blocks = refs[:4]
    in_ref, out_ref, down_ref, gain_ref, held = refs[4:]
    _, rows_d, rows_f, starts, total = plan(shards)
    quarter = total // TP
    z, x, c = idx[0], idx[1], idx[2]
    for cr in range(2):
        for xr in range(2):
            block = blocks[2 * cr + xr]
            for k in range(TP):
                at = pl.multiple_of(lax.rem(z - k + TP, TP) * quarter, quarter)
                held[pl.ds(at, quarter), :] = block[k].astype(F32)
            cc, xx = lax.rem(c + cr, 2), lax.rem(x + xr, 2)
            for b in range(3):
                in_ref[cc, xx, :, b * D : (b + 1) * D] = held[starts[b] : starts[b] + rows_d, :]
            down_ref[cc, xx] = held[starts[3] : starts[3] + rows_f, :]
            out_ref[cc, xx] = held[starts[4] : starts[4] + rows_d, :]
            if cr == 0 and xr == 0:
                gain_ref[...] = held[starts[5] : starts[5] + 8, :]


def qkv_unpack_kernel(idx, *refs):
    blocks = refs[:4]
    out_ref, gain_ref = refs[4:]
    z, x, c = idx[0], idx[1], idx[2]
    for cr in range(2):
        for xr in range(2):
            cc, xx = lax.rem(c + cr, 2), lax.rem(x + xr, 2)
            gain = None
            for g in range(TP):
                block = blocks[2 * cr + xr][lax.rem(z - g + TP, TP)].astype(F32)
                for source, place in ((0, 1), (1, 2), (2, 0)):
                    out_ref[cc, xx, :, place * D + g * GW : place * D + (g + 1) * GW] = block[
                        :, source * GW : (source + 1) * GW
                    ]
                tail = block[:, 512:640]
                gain = tail if gain is None else gain + tail
            gain_ref[cc, xx] = gain


def shift(value, axis, k):
    n = lax.axis_size(axis)
    return lax.ppermute(value, axis, [(i, (i + k) % n) for i in range(n)])


def gather(value, axis):
    return [value] + [shift(value, axis, k) for k in range(1, lax.axis_size(axis))]


def pick(value, index, dim):
    return lax.dynamic_index_in_dim(value, index, dim, keepdims=False)


def reduce_scatter(value, axis, dim):
    n, i = lax.axis_size(axis), lax.axis_index(axis)
    total = None
    for k in range(1, n):
        got = shift(pick(value, lax.rem(i + k, n), dim), axis, k).astype(F32)
        total = got if total is None else total + got
    own = pick(value, i, dim).astype(F32)
    return (own if total is None else own + total).astype(BF)


def sum_over(value, axis):
    total = value.astype(F32)
    for k in range(1, lax.axis_size(axis)):
        total = total + shift(value, axis, k).astype(F32)
    return total.astype(BF)


def fetch(weight):
    n, y, c = lax.axis_size("shard"), lax.axis_index("shard"), lax.axis_index("core")
    height = weight.shape[0]
    half = height // 2
    blocks = [(weight, y * height)]
    for k in range(1, n):
        start = lax.rem(y - k + n, n) * height
        if half % 16:
            blocks.append((shift(weight, "shard", k), start))
            continue
        mine = lax.dynamic_slice_in_dim(weight, c * half, half, 0)
        mine = shift(mine, "shard", k)
        blocks.append((mine, start + c * half))
        blocks.append((shift(mine, "core", 1), start + (1 - c) * half))
    return blocks


def per_device(tokens, gain_one, w_qkv, w_out, gain_two, w_in, w_down, cotangent):
    tok, cot = tokens[0], cotangent[0]
    rows = tok.shape[0]
    many = TP * rows
    zo, z = lax.axis_index("zo"), lax.axis_index("z")
    x, c, y = lax.axis_index("x"), lax.axis_index("core"), lax.axis_index("shard")
    shards = lax.axis_size("shard")
    part = w_qkv.shape[0]
    i32 = jnp.int32

    toks = gather(tok, "z")
    w_groups = w_qkv.reshape(part, 3, TP, GW).transpose(2, 0, 1, 3)
    gains_col = jnp.stack([gain_one, gain_two], axis=1)
    gains_col = jnp.broadcast_to(gains_col[None], (TP, part, 2))
    w_groups = jnp.concatenate(
        [
            w_groups[:, :, 1],
            w_groups[:, :, 2],
            w_groups[:, :, 0],
            gains_col,
            jnp.zeros((TP, part, WC - 3 * GW - 2), BF),
        ],
        axis=2,
    )
    w_own = pick(w_groups, z, 0)
    w_slices = gather(w_own, "shard")
    w_offs = jnp.stack([lax.rem(y - k + shards, shards) * part for k in range(shards)]).astype(i32)

    freq = THETA ** (-jnp.arange(HEAD_DIM // 2, dtype=F32) * (2.0 / HEAD_DIM))
    owners = lax.rem(z - jnp.arange(TP, dtype=i32) + TP, TP)
    first_places = (((zo * TP + owners) * 2 + x) * 2 + c) * rows
    places = (first_places[:, None] + jnp.arange(rows, dtype=i32)).reshape(many)
    angle = places.astype(F32)[:, None] * jnp.tile(freq, 4)[None, :]
    sign = jnp.where(jnp.arange(128) % 64 < 32, -1.0, 1.0).astype(F32)
    cosine, sine = jnp.cos(angle), jnp.sin(angle) * sign[None, :]

    query, kv, h_one, w_full, gains = call(
        functools.partial(front_kernel, shards),
        [
            ((many, 256), BF),
            ((many, 2 * GW), BF),
            ((many, D), BF),
            ((D, WC), BF),
            ((8, D), F32),
        ],
        1,
        [w_offs, *toks, *w_slices, cosine, sine],
        flops=2 * many * D * WC,
        bytes_accessed=5_000_000,
        name="front",
    )

    kvs = gather(kv, "zo")
    kvs = [b for k in range(2) for b in (kvs if k == 0 else [shift(v, "x", 1) for v in kvs])]
    kvs = kvs + [shift(v, "core", 1) for v in kvs]
    n_kv = len(kvs)
    keys = n_kv * many

    out_blocks = fetch(w_out)
    in_blocks = fetch(w_in)
    down_blocks = fetch(w_down)

    attended, attended_t, lse = call(
        functools.partial(forward_kernel, n_kv),
        [((many, GW), BF), ((GW, many), F32), ((8, many), F32)],
        0,
        [query, *kvs],
        scratch=[
            pltpu.VMEM((keys, 2 * GW), BF),
            pltpu.VMEM((256, keys), BF),
            pltpu.VMEM((256, many), BF),
        ],
        flops=4 * keys * many * 256 * GH,
        bytes_accessed=4_000_000,
        name="attention_forward",
    )
    att_blocks = attended.reshape(TP, rows, GW)
    atts = [att_blocks[0]] + [shift(att_blocks[k], "z", -k) for k in range(1, TP)]
    groups = lax.rem(z + jnp.arange(TP, dtype=i32), TP)

    blocks = out_blocks + in_blocks + down_blocks
    offs = jnp.concatenate(
        [jnp.stack([o for _, o in blocks]).astype(i32), groups * GW]
    )
    mid = call(
        functools.partial(middle_kernel, len(out_blocks), len(in_blocks), len(down_blocks)),
        [
            ((rows, D), F32),
            ((rows, D), F32),
            ((rows, D), BF),
            ((rows, D), BF),
            ((rows, FF), BF),
            ((rows, 2 * FF), BF),
            ((8, D), F32),
        ]
        + [((rows, 256), BF)] * TP,
        1,
        [offs, *atts, tok, cot, gains, *[b for b, _ in blocks]],
        scratch=[
            pltpu.VMEM((D, D), BF),
            pltpu.VMEM((D, 2 * FF), BF),
            pltpu.VMEM((FF, D), BF),
            pltpu.SemaphoreType.DMA((len(blocks),)),
        ],
        any_ins=range(1 + TP + 3, 1 + TP + 3 + len(blocks)),
        flops=2 * rows * (2 * D * D + 2 * D * 2 * FF + 2 * FF * D),
        bytes_accessed=14_000_000,
        name="feed_forward",
    )
    result, grad_middle, grad_branch, h_two, mixed, grad_gate_up, gain_two_row = mid[:7]
    gatts = mid[7:]
    gas = [gatts[0]] + [shift(gatts[k], "z", k) for k in range(1, TP)]

    pieces, rows_d, rows_f, _, total = plan(shards)
    (packed,) = call(
        functools.partial(ffn_grads_kernel, shards),
        [((pieces, total, D), BF)],
        1,
        [groups, *atts, h_two, grad_gate_up, mixed, cot, grad_branch, gain_two_row],
        flops=2 * rows * (D * 2 * FF + FF * D + D * D),
        bytes_accessed=10_000_000,
        name="ffn_weight_grads",
    )
    ffn = packed.reshape(shards, 2, 2, total, D)
    ffn = reduce_scatter(ffn, "core", 1)
    ffn = reduce_scatter(ffn, "shard", 0)
    ffn = reduce_scatter(ffn, "x", 0)
    ffn = reduce_scatter(ffn.reshape(TP, total // TP, D), "z", 0)
    ffn = sum_over(ffn, "zo")

    dkv, dq = call(
        functools.partial(backward_kernel, n_kv),
        [((n_kv, many, 2 * GW), BF), ((many, 256), F32)],
        0,
        [query, *kvs, *gas, attended_t, lse],
        scratch=[
            pltpu.VMEM((keys, 2 * GW), BF),
            pltpu.VMEM((256, keys), BF),
            pltpu.VMEM((256, many), BF),
            pltpu.VMEM((256, many), BF),
            pltpu.VMEM((many, 2 * GW), BF),
            pltpu.VMEM((many, 2 * GW), BF),
            pltpu.VMEM((keys, 2 * GW), F32),
            pltpu.VMEM((256, many), F32),
        ],
        flops=10 * keys * many * 256 * GH,
        bytes_accessed=8_000_000,
        name="attention_backward",
    )
    half = n_kv // 2
    got = shift(dkv[half:], "core", 1)
    summed = (dkv[:half].astype(F32) + got.astype(F32)).astype(BF)
    outer = half // 2
    keep, got = summed[:outer], shift(summed[outer:], "x", 1)
    if outer > 1:
        both = (keep.astype(F32) + got.astype(F32)).astype(BF)
        sums = [both[0]] + [shift(both[k], "zo", -k) for k in range(1, outer)]
    else:
        sums = [keep[0], got[0]]

    grads = call(
        functools.partial(qkv_grads_kernel, pieces, len(sums)),
        [((pieces, D // pieces, WC), BF)] + [((rows, WC), BF)] * TP,
        0,
        [*sums, dq, cosine, sine, h_one, w_full],
        scratch=[pltpu.VMEM((many, WC), BF)],
        flops=2 * many * D * WC,
        bytes_accessed=5_000_000,
        name="qkv_weight_grads",
    )
    gqkv = [grads[1]] + [shift(grads[1 + k], "z", -k) for k in range(1, TP)]

    wq = grads[0].reshape(shards, 2, 2, D // pieces, WC)
    wq = reduce_scatter(wq, "core", 1)
    wq = reduce_scatter(wq, "shard", 0)
    wq = reduce_scatter(wq, "x", 0)
    wq = sum_over(wq, "zo")

    w_parts = [(w_groups, 0, y * part)]
    for k in range(1, shards):
        start = lax.rem(y - k + shards, shards) * part
        mine = shift(lax.dynamic_slice_in_dim(w_groups, 2 * c, 2, 0), "shard", k)
        w_parts.append((mine, 2 * c, start))
        w_parts.append((shift(mine, "core", 1), 2 * (1 - c), start))
    tail_offs = jnp.concatenate(
        [jnp.stack([jnp.asarray(v, i32) for _, a, b in w_parts for v in (a, b)]), groups]
    )
    (grad_tokens,) = call(
        functools.partial(tail_kernel, len(w_parts)),
        [((rows, D), F32)],
        1,
        [tail_offs, *gqkv, tok, grad_middle, gains, *[w for w, _, _ in w_parts]],
        scratch=[
            pltpu.VMEM((TP, D, WC), BF),
            pltpu.SemaphoreType.DMA((len(w_parts),)),
        ],
        any_ins=range(1 + TP + 3, 1 + TP + 3 + len(w_parts)),
        flops=2 * rows * D * WC * TP,
        bytes_accessed=6_000_000,
        name="token_grads",
    )

    idx = jnp.stack([z, x, c]).astype(i32)
    ffn = jnp.stack(gather(ffn, "z"))
    ffn = gather(ffn, "x")
    ffn = ffn + [shift(v, "core", 1) for v in ffn]
    g_in, g_out, g_down, g_gain = call(
        functools.partial(ffn_unpack_kernel, shards),
        [
            ((2, 2, rows_d, 2 * FF), F32),
            ((2, 2, rows_d, D), F32),
            ((2, 2, rows_f, D), F32),
            ((8, D), F32),
        ],
        1,
        [idx, *ffn],
        scratch=[pltpu.VMEM((total, D), F32)],
        bytes_accessed=12_000_000,
        name="ffn_unpack",
    )
    grad_gain_two = lax.dynamic_slice_in_dim(g_gain[0], y * part, part, 0)

    wq = gather(wq, "x")
    wq = gather(jnp.stack(wq), "z")
    wq = jnp.stack(wq, axis=1)
    other = shift(wq, "core", 1)
    g_qkv, g_one = call(
        qkv_unpack_kernel,
        [((2, 2, rows_d, 3 * D), F32), ((2, 2, rows_d, 128), F32)],
        1,
        [idx, wq[0], wq[1], other[0], other[1]],
        bytes_accessed=6_000_000,
        name="qkv_unpack",
    )
    grad_gain_one = g_one[..., 64].reshape(part)

    return (
        result[None],
        grad_tokens[None],
        grad_gain_one,
        g_qkv.reshape(part, 3 * D),
        g_out.reshape(part, D),
        grad_gain_two,
        g_in.reshape(part, 2 * FF),
        g_down.reshape(w_down.shape[0], D),
    )


def solution(mesh):
    blocks = mesh.shape["ctx"]
    fine = Mesh(
        mesh.devices.reshape(blocks // (TP * 4), TP, 2, 2, mesh.shape["shard"]), CTX + ("shard",)
    )
    rows, split = P("shard", CTX, None), P("shard", None)
    return jax.shard_map(
        per_device,
        mesh=fine,
        in_specs=(rows, P("shard"), split, split, P("shard"), split, split, rows),
        out_specs=(rows, rows, P("shard"), split, split, P("shard"), split, split),
        check_vma=False,
    )
```

```python
import functools
import math

import jax
import jax.numpy as jnp
from jax import lax
from jax.experimental import pallas as pl
from jax.experimental.pallas import tpu as pltpu
from jax.sharding import Mesh, PartitionSpec as P

D = 768
HEADS = 12
HEAD_DIM = 64
FF = 1152
EPS = 1e-05
THETA = 160000.0

TP = 4
GH = HEADS // TP
GW = GH * HEAD_DIM
WC = 640
CTX = ("zo", "z", "x", "core")
BF = jnp.bfloat16
F32 = jnp.float32
VMEM_LIMIT = 56 * 1024 * 1024

KEY_AT = ((0, 0), (0, 1), (1, 0))
VALUE_AT = ((1, 1), (2, 0), (2, 1))


def dot(a, b):
    return jnp.dot(a, b, preferred_element_type=F32)


def dot_nt(a, b):
    return lax.dot_general(a, b, (((1,), (1,)), ((), ())), preferred_element_type=F32)


def dot_tn(a, b):
    return lax.dot_general(a, b, (((0,), (0,)), ((), ())), preferred_element_type=F32)


def call(body, outs, n_smem, ins, scratch=(), any_ins=(), name=None):
    specs = []
    for i in range(len(ins)):
        if i < n_smem:
            specs.append(pl.BlockSpec(memory_space=pltpu.SMEM))
        elif i in any_ins:
            specs.append(pl.BlockSpec(memory_space=pl.ANY))
        else:
            specs.append(pl.BlockSpec(memory_space=pltpu.VMEM))
    return pl.pallas_call(
        body,
        out_shape=[jax.ShapeDtypeStruct(s, t) for s, t in outs],
        in_specs=specs,
        out_specs=[pl.BlockSpec(memory_space=pltpu.VMEM)] * len(outs),
        scratch_shapes=list(scratch),
        compiler_params=pltpu.CompilerParams(vmem_limit_bytes=VMEM_LIMIT),
        cost_estimate=pl.CostEstimate(
            flops=1, bytes_accessed=1, transcendentals=0
        ),
        name=name,
    )(*ins)


def normalise(values):
    mean = jnp.mean(values, axis=-1, keepdims=True)
    centred = values - mean
    spread = jnp.mean(centred * centred, axis=-1, keepdims=True)
    scale = lax.rsqrt(spread + EPS)
    return centred * scale, scale


def normalise_back(grad_unit, unit, scale):
    return scale * (
        grad_unit
        - jnp.mean(grad_unit, axis=-1, keepdims=True)
        - unit * jnp.mean(grad_unit * unit, axis=-1, keepdims=True)
    )


def turn(tile, cosine, signed_sine, first_half):
    swapped = jnp.where(first_half, pltpu.roll(tile, 96, 1), pltpu.roll(tile, 32, 1))
    return tile * cosine + swapped * signed_sine


def lane_masks(rows):
    lane = lax.broadcasted_iota(jnp.int32, (rows, 128), 1)
    return lax.rem(lane, 64) < 32, lane < 64


def group_kernel(idx, w_ref, own_ref, half_ref):
    height = w_ref.shape[0]
    half = height // 2
    for g in range(TP):

        @pl.when(idx[0] == g)
        def _():
            parts = [w_ref[:, p * D + g * GW : p * D + (g + 1) * GW] for p in (1, 2, 0)]
            parts.append(jnp.zeros((height, WC - 3 * GW), BF))
            own_ref[...] = jnp.concatenate(parts, axis=1)

    half_ref[...] = own_ref[pl.ds(pl.multiple_of(idx[2] * half, half), half), :]


def pack_kernel(idx, out_ref, in_ref, down_ref, pack_ref):
    c = idx[2]
    half = out_ref.shape[0] // 2
    at = pl.ds(pl.multiple_of(c * half, half), half)
    pack_ref[0:half, :] = out_ref[at, :]
    for b in range(3):
        pack_ref[(1 + b) * half : (2 + b) * half, :] = in_ref[at, b * D : (b + 1) * D]
    count, step = down_half(down_ref.shape[0])
    at = pl.ds(pl.multiple_of(c * step, 16), count)
    pack_ref[4 * half :, :] = down_ref[at, :]


def down_half(height):
    count = -(-height // 32) * 16
    return count, height - count


def front_kernel(shards, idx, *refs):
    toks = refs[:TP]
    n_w = 2 * shards - 1
    ws = refs[TP : TP + n_w]
    gain_refs = refs[TP + n_w : TP + n_w + shards]
    cos_ref, sin_ref, q_ref, kv_ref, h_ref, w_ref, gains_ref = refs[TP + n_w + shards :]
    c, y = idx[2], idx[3]
    rows = toks[0].shape[0]
    part = ws[0].shape[0]
    half = part // 2
    gains_ref[...] = jnp.zeros_like(gains_ref)
    for k in range(shards):
        start = lax.rem(y - k + shards, shards) * part
        at = pl.ds(pl.multiple_of(start, part), part)
        if k == 0:
            w_ref[at, :] = ws[0][...]
            continue
        at = pl.ds(pl.multiple_of(start + c * half, half), half)
        w_ref[at, :] = ws[2 * k - 1][...]
        at = pl.ds(pl.multiple_of(start + (1 - c) * half, half), half)
        w_ref[at, :] = ws[2 * k][...]
    for s in range(shards):

        @pl.when(y == s)
        def _():
            for k in range(shards):
                start = (s - k) % shards * part
                gains_ref[0:2, start : start + part] = gain_refs[k][...].astype(F32)

    gain = gains_ref[0:1, :]
    first, low = lane_masks(rows)
    for j in range(TP):
        at = slice(j * rows, (j + 1) * rows)
        unit, _ = normalise(toks[j][...].astype(F32))
        h = (unit * gain).astype(BF)
        h_ref[at, :] = h
        out = dot(h, w_ref[...])
        cosine, sine = cos_ref[at, :], sin_ref[at, :]
        key_a = turn(out[:, 0:128], cosine, sine, first)
        mixed = out[:, 128:256]
        key_b = jnp.where(low, turn(mixed, cosine, sine, first), mixed)
        kv_ref[at, 0:128] = key_a.astype(BF)
        kv_ref[at, 128:256] = key_b.astype(BF)
        kv_ref[at, 256:384] = out[:, 256:384].astype(BF)
        query_a = turn(out[:, 384:512], cosine, sine, first)
        query_b = jnp.where(low, turn(out[:, 512:640], cosine, sine, first), 0.0)
        factor = HEAD_DIM ** (-0.5)
        q_ref[at, 0:128] = (query_a * factor).astype(BF)
        q_ref[at, 128:256] = (query_b * factor).astype(BF)


def half_rows(values_t, head):
    at = head * HEAD_DIM
    rows = values_t[at : at + HEAD_DIM]
    zeros = jnp.zeros_like(rows)
    return jnp.concatenate([rows, zeros] if head % 2 == 0 else [zeros, rows], axis=0)


def forward_kernel(n_kv, q_ref, *refs):
    kvs = refs[:n_kv]
    atts = refs[n_kv : n_kv + TP]
    att_t_ref, lse_ref, kv_s, v_t, q_t = refs[n_kv + TP :]
    rows = kvs[0].shape[0]
    block = math.gcd(rows, 256)
    for i, kv in enumerate(kvs):
        kv_s[i * rows : (i + 1) * rows, :] = kv[...]
        v_t[:, i * rows : (i + 1) * rows] = kv[:, 128:384].T
    q_t[...] = q_ref[...].T
    lse_ref[...] = jnp.zeros_like(lse_ref)
    for i in range(rows // block):
        at = slice(i * block, (i + 1) * block)
        for h in range(GH):
            tile = KEY_AT[h][0]
            keys = kv_s[:, tile * 128 : tile * 128 + 128]
            scores = dot(keys, half_rows(q_t[:, at], h))
            top = jnp.max(scores, axis=0, keepdims=True)
            weights = jnp.exp(scores - top)
            total = jnp.sum(weights, axis=0, keepdims=True)
            tile, half = VALUE_AT[h]
            values_t = v_t[(tile - 1) * 128 : tile * 128, :]
            out = dot(values_t, weights.astype(BF))[half * 64 : half * 64 + 64]
            att_t_ref[h * 64 : h * 64 + 64, at] = out / total
            lse_ref[h : h + 1, at] = top + jnp.log(total)
    small = rows // TP
    for j in range(TP):
        atts[j][...] = att_t_ref[:, j * small : (j + 1) * small].T.astype(BF)


def backward_kernel(n_kv, q_ref, *refs):
    kvs = refs[:n_kv]
    gas = refs[n_kv : n_kv + TP]
    att_t_ref, lse_ref = refs[n_kv + TP : n_kv + TP + 2]
    tables = refs[n_kv + TP + 2 : n_kv + TP + 4]
    keep_ref, send_ref, dq_ref = refs[n_kv + TP + 4 : n_kv + TP + 7]
    kv_s, k_t, q_t, g_t, q_m, g_m, acc, dq_t = refs[n_kv + TP + 7 :]
    rows = kvs[0].shape[0]
    small = gas[0].shape[0]
    block = math.gcd(rows, 256)
    for i, kv in enumerate(kvs):
        kv_s[i * rows : (i + 1) * rows, :] = kv[...]
        k_t[:, i * rows : (i + 1) * rows] = kv[:, 0:256].T
    q_t[...] = q_ref[...].T
    _, low = lane_masks(small)
    for j in range(TP):
        at = slice(j * small, (j + 1) * small)
        g_t[:, at] = gas[j][...].T
        first, second = gas[j][:, 0:128], gas[j][:, 128:256].astype(F32)
        g_m[at, 0:128] = first
        g_m[at, 128:256] = jnp.where(low, second, 0.0).astype(BF)
        g_m[at, 256:384] = jnp.where(low, 0.0, second).astype(BF)
        both = q_ref[at, 0:128].astype(F32)
        q_m[at, 0:128] = jnp.where(low, both, 0.0).astype(BF)
        q_m[at, 128:256] = jnp.where(low, 0.0, both).astype(BF)
        q_m[at, 256:384] = q_ref[at, 128:256]
    dq_t[...] = jnp.zeros_like(dq_t)
    acc[...] = jnp.zeros_like(acc)
    for i in range(rows // block):
        at = slice(i * block, (i + 1) * block)
        for h in range(GH):
            ktile, khalf = KEY_AT[h]
            vtile = VALUE_AT[h][0]
            klanes = slice(ktile * 128, ktile * 128 + 128)
            vlanes = slice(vtile * 128, vtile * 128 + 128)
            scores = dot(kv_s[:, klanes], half_rows(q_t[:, at], h))
            probs = jnp.exp(scores - lse_ref[h : h + 1, at])
            grad_t = half_rows(g_t[:, at], h + 1)
            grad_probs = dot(kv_s[:, vlanes], grad_t)
            own = g_t[(h + 1) * 64 : (h + 2) * 64, at].astype(F32)
            inner = jnp.sum(
                own * att_t_ref[h * 64 : h * 64 + 64, at], axis=0, keepdims=True
            )
            grad_scores = (probs * (grad_probs - inner)).astype(BF)
            lanes = slice(h * 128, h * 128 + 128)
            acc[:, vlanes] += dot(probs.astype(BF), g_m[at, lanes])
            acc[:, klanes] += dot(grad_scores, q_m[at, lanes])
            part = dot(k_t[klanes, :], grad_scores)[khalf * 64 : khalf * 64 + 64]
            dq_t[h * 64 : h * 64 + 64, at] = part * HEAD_DIM ** (-0.5)
    first, low = lane_masks(rows)
    cosine, sine = tables[0][0:rows, :], -tables[1][0:rows, :]
    grad_q = dq_t[...].T
    for t in range(2):
        lanes = slice(t * 128, t * 128 + 128)
        dq_ref[:, lanes] = turn(grad_q[:, lanes], cosine, sine, first).astype(BF)
    for i in range(n_kv):
        at = slice(i * rows, (i + 1) * rows)
        cosine, sine = tables[0][at, :], -tables[1][at, :]
        target = keep_ref if i < n_kv // 2 else send_ref
        block = i % (n_kv // 2)
        grad = acc[at, 0:128]
        target[block, :, 0:128] = turn(grad, cosine, sine, first).astype(BF)
        grad = acc[at, 128:256]
        grad = jnp.where(low, turn(grad, cosine, sine, first), grad)
        target[block, :, 128:256] = grad.astype(BF)
        target[block, :, 256:384] = acc[at, 256:384].astype(BF)


ACT_H, ACT_MIX, ACT_GU, ACT_GB, ACT_ATT, ACT_COT, ACT_ALL = (
    0, D, D + FF, D + 3 * FF, 2 * D + 3 * FF, 3 * D + 3 * FF, 4 * D + 3 * FF
)


def middle_kernel(n_packs, idx, *refs):
    atts = refs[:TP]
    tok_ref, cot_ref, gains_ref, out_own, in_own, down_own = refs[TP : TP + 6]
    packs = refs[TP + 6 : TP + 6 + n_packs]
    rest = refs[TP + 6 + n_packs :]
    result_ref, gmid_ref, act_ref, gain_ref = rest[:4]
    gatts = rest[4 : 4 + TP]
    w_out, w_in, w_down, sems = rest[4 + TP :]
    half = out_own.shape[0] // 2
    count, step = down_half(down_own.shape[0])

    def rows(start, height):
        return pl.ds(pl.multiple_of(start, 16), height)

    z, c, y = idx[0], idx[2], idx[3]
    shards = n_packs // 2 + 1
    own, own_down = y * 2 * half, y * down_own.shape[0]
    outs = [pltpu.make_async_copy(out_own, w_out.at[rows(own, 2 * half), :], sems.at[0])]
    ins = [pltpu.make_async_copy(in_own, w_in.at[rows(own, 2 * half), :], sems.at[1])]
    target = w_down.at[rows(own_down, down_own.shape[0]), :]
    downs = [pltpu.make_async_copy(down_own, target, sems.at[2])]
    for i, pack in enumerate(packs):
        shard = lax.rem(y - (i // 2 + 1) + shards, shards)
        core = 1 - c if i % 2 else c
        at = rows((shard * 2 + core) * half, half)
        source = pack.at[0:half, :]
        outs.append(pltpu.make_async_copy(source, w_out.at[at, :], sems.at[3 + 5 * i]))
        for b in range(3):
            source = pack.at[(1 + b) * half : (2 + b) * half, :]
            target = w_in.at[at, b * D : (b + 1) * D]
            ins.append(pltpu.make_async_copy(source, target, sems.at[4 + 5 * i + b]))
        at = rows(shard * down_own.shape[0] + core * step, count)
        source = pack.at[4 * half : 4 * half + count, :]
        downs.append(pltpu.make_async_copy(source, w_down.at[at, :], sems.at[7 + 5 * i]))
    apart = 2 * count == down_own.shape[0]
    for copy in outs + ins + (downs if apart else downs[:1]):
        copy.start()
    starts = [pl.multiple_of(lax.rem(z + j, TP) * GW, GW) for j in range(TP)]
    for copy in outs:
        copy.wait()
    middle = tok_ref[...].astype(F32)
    for j in range(TP):
        middle += dot(atts[j][...], w_out[pl.ds(starts[j], GW), :])
        act_ref[:, ACT_ATT + j * GW : ACT_ATT + (j + 1) * GW] = atts[j][...]
    gain = gains_ref[1:2, :]
    unit, scale = normalise(middle)
    h = (unit * gain).astype(BF)
    act_ref[:, ACT_H : ACT_H + D] = h
    for copy in ins:
        copy.wait()
    gate = dot(h, w_in[:, :FF])
    up = dot(h, w_in[:, FF:])
    phi = 0.5 * (1.0 + lax.erf(gate * math.sqrt(0.5)))
    active = gate * phi
    mixed = (active * up).astype(BF)
    act_ref[:, ACT_MIX : ACT_MIX + FF] = mixed
    for i, copy in enumerate(downs):
        if i and not apart:
            copy.start()
        copy.wait()
    grad_mixed = dot_nt(cot_ref[...], w_down[...])
    slope = phi + gate * (jnp.exp(-0.5 * gate * gate) * (1.0 / math.sqrt(2.0 * math.pi)))
    grad_gate = (grad_mixed * up * slope).astype(BF)
    grad_up = (grad_mixed * active).astype(BF)
    act_ref[:, ACT_GU : ACT_GU + FF] = grad_gate
    act_ref[:, ACT_GU + FF : ACT_GU + 2 * FF] = grad_up
    grad_h = dot_nt(grad_gate, w_in[:, :FF]) + dot_nt(grad_up, w_in[:, FF:])
    gain_ref[...] = jnp.broadcast_to(
        jnp.sum(grad_h * unit, axis=0, keepdims=True), gain_ref.shape
    )
    grad_middle = cot_ref[...].astype(F32) + normalise_back(grad_h * gain, unit, scale)
    gmid_ref[...] = grad_middle
    gb = grad_middle.astype(BF)
    act_ref[:, ACT_GB : ACT_GB + D] = gb
    act_ref[:, ACT_COT : ACT_COT + D] = cot_ref[...]
    for j in range(TP):
        part = dot_nt(gb, w_out[pl.ds(starts[j], GW), :])
        pad = jnp.zeros((part.shape[0], 256 - GW), F32)
        gatts[j][...] = jnp.concatenate([pad, part], axis=1).astype(BF)
    result_ref[...] = middle + dot(mixed, w_down[...])


def up16(n):
    return -(-n // 16) * 16


def plan(shards):
    rows_d, rows_f = D // (4 * shards), FF // (4 * shards)
    return rows_d, rows_f, up16(rows_d), up16(rows_f)


def ffn_grads_kernel(shards, idx, own, got, gain_ref, *refs):
    ins = refs[:shards]
    others = refs[shards : shards + 2]
    h_t, mixed_t, att_t, right = refs[shards + 2 :]
    z, x, c, y = idx[0], idx[1], idx[2], idx[3]
    rows_d, rows_f, pad_d, pad_f = plan(shards)
    n = own.shape[0]
    pieces, per = 4 * shards, GW // rows_d
    for i, act in enumerate((own, got)):
        at = slice(i * n, (i + 1) * n)
        h = act[:, ACT_H : ACT_H + D].T
        mixed = act[:, ACT_MIX : ACT_MIX + FF].T
        att = act[:, ACT_ATT : ACT_ATT + D].T
        for m in range(pieces):
            h_t[m, 0:rows_d, at] = h[m * rows_d : (m + 1) * rows_d]
            mixed_t[m, 0:rows_f, at] = mixed[m * rows_f : (m + 1) * rows_f]
            att_t[m, 0:rows_d, at] = att[m * rows_d : (m + 1) * rows_d]
        right[at, 0 : 2 * FF] = act[:, ACT_GU : ACT_GU + 2 * FF]
        right[at, 2 * FF : 2 * FF + D] = act[:, ACT_GB : ACT_GB + D]
        right[at, 2 * FF + D :] = act[:, ACT_COT : ACT_COT + D]
    for k in range(shards):
        piece = (lax.rem(y + k, shards) * 2 + c) * 2
        left = h_t[pl.ds(piece, 2)].reshape(2 * pad_d, 2 * n)
        grad = dot(left, right[:, 0 : 2 * FF]).astype(BF)
        for xx in range(2):
            for t in range(2 * FF // 128):
                ins[k][xx, t * pad_d : t * pad_d + rows_d, :] = grad[
                    xx * pad_d : xx * pad_d + rows_d, t * 128 : t * 128 + 128
                ]
    gain = jnp.broadcast_to(gain_ref[0:1, :], (16, D)).astype(BF)
    high = pad_f + pad_d + 16
    for xr in range(2):
        for s in range(shards):
            piece = (s * 2 + c) * 2 + lax.rem(x + xr, 2)
            turned = lax.rem(piece // per - z + TP, TP) * per + lax.rem(piece, per)
            down = dot(mixed_t[piece], right[:, 2 * FF + D :]).astype(BF)
            out = dot(att_t[turned], right[:, 2 * FF : 2 * FF + D]).astype(BF)
            for t in range(D // 128):
                lanes = slice(t * 128, t * 128 + 128)
                base = t * high
                others[xr][s, base : base + pad_f, :] = down[:, lanes]
                base += pad_f
                others[xr][s, base : base + pad_d, :] = out[:, lanes]
                base += pad_d
                others[xr][s, base : base + 16, :] = gain[:, lanes]


def qkv_grads_kernel(shards, n_kv, idx, *refs):
    hs = refs[:n_kv]
    keep_ref, send_ref, dq_ref, w_ref, gains_ref, mine_ref, other_ref = refs[n_kv:]
    c = idx[2]
    total = None
    for i in range(n_kv):
        grads = (keep_ref if i < n_kv // 2 else send_ref)[i % (n_kv // 2)]
        part = dot(grads.T, hs[i][...])
        total = part if total is None else total + part
    grad = jnp.concatenate([total, dot(dq_ref[...].T, hs[0][...])], axis=0).T
    w = w_ref[...].astype(F32)
    gain = gains_ref[...].T[:, 0:1]
    lane = lax.broadcasted_iota(jnp.int32, grad.shape, 1)
    by_gain = jnp.sum(grad * w, axis=1, keepdims=True) / gain
    grad = jnp.where(lane < 3 * GW, grad, by_gain).astype(BF)
    height = plan(shards)[0]
    for s in range(shards):
        for cc in range(2):
            block = (s * 2 + cc) * 2 * height
            for xx in range(2):
                part = grad[block + xx * height : block + (xx + 1) * height]

                @pl.when(c == cc)
                def _():
                    mine_ref[s, xx] = part

                @pl.when(c != cc)
                def _():
                    other_ref[s, xx] = part


def combine_kernel(n_sum, idx, *refs):
    parts = refs[:n_sum]
    dq_ref, w_ref, out_ref = refs[n_sum:]
    rows = out_ref.shape[2]
    for j in range(TP):
        at = slice(j * rows, (j + 1) * rows)
        total = parts[0][at, :].astype(F32)
        for part in parts[1:]:
            total += part[at, :].astype(F32)
        grad = jnp.concatenate([total.astype(BF), dq_ref[at, :]], axis=1)
        owner = lax.rem(idx[0] - j + TP, TP)
        out_ref[owner // 2, lax.rem(owner, 2)] = dot_nt(grad, w_ref[...]).astype(BF)


def tail_kernel(n_sum, *refs):
    tok_ref, gmid_ref, gains_ref, out_ref = refs[n_sum:]
    unit, scale = normalise(tok_ref[...].astype(F32))
    total = refs[0][...].astype(F32)
    for grad in refs[1:n_sum]:
        total += grad[...].astype(F32)
    grad_unit = total * gains_ref[0:1, :]
    out_ref[...] = gmid_ref[...] + normalise_back(grad_unit, unit, scale)


def place_z(z, k):
    return lax.rem(z // 2 + k % 2, 2) * 2 + lax.rem(lax.rem(z, 2) + k // 2, 2)


def in_unpack_kernel(shards, idx, own, got, in_ref, held):
    rows_d, _, pad_d, _ = plan(shards)
    size = held.shape[0] // TP
    z, x, c = idx[0], idx[1], idx[2]
    for cr in range(2):
        for xr in range(2):
            for k in range(TP):
                at = pl.ds(pl.multiple_of(place_z(z, k) * size, size), size)
                held[at, :] = (got if cr else own)[xr, k].astype(F32)
            cc, xx = lax.rem(c + cr, 2), lax.rem(x + xr, 2)
            for t in range(2 * FF // 128):
                base = t * pad_d
                in_ref[cc, xx, :, t * 128 : t * 128 + 128] = held[base : base + rows_d, :]


def rest_unpack_kernel(shards, idx, own, got, out_ref, down_ref, gain_ref, held, gain_all):
    rows_d, rows_f, pad_d, pad_f = plan(shards)
    high = pad_f + pad_d + 16
    size = held.shape[0] // TP
    z, x, c = idx[0], idx[1], idx[2]
    gains = []
    for cr in range(2):
        for xr in range(2):
            for k in range(TP):
                at = pl.ds(pl.multiple_of(place_z(z, k) * size, size), size)
                held[at, :] = (got if cr else own)[xr, k].astype(F32)
            cc, xx = lax.rem(c + cr, 2), lax.rem(x + xr, 2)
            for t in range(D // 128):
                lanes = slice(t * 128, t * 128 + 128)
                base = t * high
                down_ref[cc, xx, :, lanes] = held[base : base + rows_f, :]
                base += pad_f
                out_ref[cc, xx, :, lanes] = held[base : base + rows_d, :]
                base += pad_d
                if xr == 0:
                    gains.append(held[base : base + 8, :])
    for t in range(D // 128):
        gain_all[:, t * 128 : t * 128 + 128] = gains[t] + gains[t + D // 128]
    part = gain_ref.shape[1]
    for s in range(shards):

        @pl.when(idx[3] == s)
        def _():
            gain_ref[...] = gain_all[0:1, s * part : (s + 1) * part]


def qkv_unpack_kernel(idx, own, got, out_ref, gain_ref, gain_s):
    z, x, c = idx[0], idx[1], idx[2]
    for cr in range(2):
        for xr in range(2):
            cc, xx = lax.rem(c + cr, 2), lax.rem(x + xr, 2)
            gain = None
            for g in range(TP):
                k = 2 * lax.rem(g % 2 + z, 2) + lax.rem(g // 2 + z // 2, 2)
                block = (got if cr else own)[xr, k].astype(F32)
                for source, place in ((0, 1), (1, 2), (2, 0)):
                    out_ref[cc, xx, :, place * D + g * GW : place * D + (g + 1) * GW] = block[
                        :, source * GW : (source + 1) * GW
                    ]
                tail = block[:, 512:640]
                gain = tail if gain is None else gain + tail
            height = gain.shape[0]
            at = pl.multiple_of((cc * 2 + xx) * height, height)
            gain_s[pl.ds(at, height), :] = gain
    gain_ref[...] = gain_s[...].T[64:65]


def shift(value, axis, k):
    n = lax.axis_size(axis)
    return lax.ppermute(value, axis, [(i, (i + k) % n) for i in range(n)])


def gather(value, axis):
    return [value] + [shift(value, axis, k) for k in range(1, lax.axis_size(axis))]


def pick(value, index, dim):
    return lax.dynamic_index_in_dim(value, index, dim, keepdims=False)


def reduce_step(order, terms, axis, dim):
    n, i = lax.axis_size(axis), lax.axis_index(axis)
    got = []
    for k in range(1, n):
        got.append(shift(order.add([pick(t, lax.rem(i + k, n), dim) for t in terms]), axis, k))
    return [pick(t, i, dim) for t in terms] + got


def add(terms):
    total = terms[0].astype(F32)
    for term in terms[1:]:
        total = total + term.astype(F32)
    return total.astype(BF)


def swap_z(value, bit):
    return lax.ppermute(value, "z", [(i, i ^ bit) for i in range(TP)])


def reduce_z(order, terms, bit):
    z = lax.axis_index("z")
    i, dim = (z % 2, 1) if bit == 1 else (z // 2, 0)
    got = swap_z(order.add([pick(t, 1 - i, dim) for t in terms]), bit)
    return [pick(t, i, dim) for t in terms] + [got]


def gather_z(value, bit):
    got = swap_z(value, bit)
    return jnp.stack([value, got]) if bit == 2 else jnp.concatenate([value, got])


def sum_over(value, axis):
    return add([value] + [shift(value, axis, k) for k in range(1, lax.axis_size(axis))])


def after(value, *others):
    return lax.optimization_barrier((value, *others))[0]


class Order:
    def __init__(self):
        self.last = None

    def __call__(self, values):
        if self.last is None:
            return values
        return lax.optimization_barrier((values, self.last))[0]

    def add(self, terms):
        total = add(self(terms))
        self.last = total
        return total

    def run(self, body, outs, n_smem, ins, **more):
        got = call(body, outs, n_smem, self(list(ins)), **more)
        self.last = got[0]
        return got


def per_device(tokens, gain_one, w_qkv, w_out, gain_two, w_in, w_down, cotangent):
    tok, cot = tokens[0], cotangent[0]
    rows = tok.shape[0]
    many = TP * rows
    zo, z = lax.axis_index("zo"), lax.axis_index("z")
    x, c, y = lax.axis_index("x"), lax.axis_index("core"), lax.axis_index("shard")
    outer, shards = lax.axis_size("zo"), lax.axis_size("shard")
    part = w_qkv.shape[0]
    n_kv = 4 * outer
    keys = n_kv * many
    rows_d, rows_f, pad_d, pad_f = plan(shards)
    high_in, high = 2 * FF // 128 * pad_d, D // 128 * (pad_f + pad_d + 16)
    i32 = jnp.int32
    idx = jnp.stack([z, x, c, y]).astype(i32)
    order = Order()

    toks = gather(tok, "z")
    w_own, w_mine = order.run(
        group_kernel,
        [((part, WC), BF), ((part // 2, WC), BF)],
        1,
        [idx, w_qkv],
        name="group_columns",
    )
    gains_own = jnp.stack([gain_one, gain_two])
    gain_parts = gather(gains_own, "shard")
    w_slices = [w_own]
    for k in range(1, shards):
        w_slices.append(shift(w_mine, "shard", k))
        w_slices.append(shift(w_slices[-1], "core", 1))
    (pack,) = order.run(
        pack_kernel,
        [((2 * part + down_half(w_down.shape[0])[0], D), BF)],
        1,
        [idx, w_out, w_in, w_down],
        name="pack_weights",
    )
    packs = [shift(pack, "shard", k) for k in range(1, shards)]

    freq = THETA ** (-jnp.arange(HEAD_DIM // 2, dtype=F32) * (2.0 / HEAD_DIM))
    owners = lax.rem(z - jnp.arange(TP, dtype=i32) + TP, TP)
    places = []
    for cr in range(2):
        for xr in range(2):
            for zr in range(outer):
                zz = lax.rem(zo - zr + outer, outer)
                place = ((zz * TP + owners) * 2 + lax.rem(x + xr, 2)) * 2 + lax.rem(c + cr, 2)
                places.append(place)
    places = jnp.concatenate(places) * rows
    places = (places[:, None] + jnp.arange(rows, dtype=i32)).reshape(keys)
    angle = places.astype(F32)[:, None] * jnp.tile(freq, 4)[None, :]
    sign = jnp.where(jnp.arange(128) % 64 < 32, -1.0, 1.0).astype(F32)
    cosine, sine = jnp.cos(angle), jnp.sin(angle) * sign[None, :]

    query, kv, h_one, w_full, gains = order.run(
        functools.partial(front_kernel, shards),
        [
            ((many, 256), BF),
            ((many, 2 * GW), BF),
            ((many, D), BF),
            ((D, WC), BF),
            ((8, D), F32),
        ],
        1,
        [idx, *toks, *w_slices, *gain_parts, cosine, sine],
        name="front",
    )

    near = gather(kv, "zo")
    near = near + [shift(v, "x", 1) for v in near]
    kvs = near + [shift(v, "core", 1) for v in near]
    h_near = gather(after(h_one, near[-1]), "zo")
    h_near = h_near + [shift(v, "x", 1) for v in h_near]
    att = order.run(
        functools.partial(forward_kernel, n_kv),
        [((rows, GW), BF)] * TP + [((GW, many), F32), ((8, many), F32)],
        0,
        [query, *kvs],
        scratch=[
            pltpu.VMEM((keys, 2 * GW), BF),
            pltpu.VMEM((256, keys), BF),
            pltpu.VMEM((256, many), BF),
        ],
        name="attention_forward",
    )
    att_blocks, (attended_t, lse) = att[:TP], att[TP:]
    atts = [att_blocks[0]] + [shift(att_blocks[k], "z", -k) for k in range(1, TP)]

    packs = [after(p, lse) for p in packs]
    both = [v for p in packs for v in (p, shift(p, "core", 1))]
    mid = order.run(
        functools.partial(middle_kernel, len(both)),
        [((rows, D), F32), ((rows, D), F32), ((rows, ACT_ALL), BF), ((8, D), F32)]
        + [((rows, 256), BF)] * TP,
        1,
        [idx, *atts, tok, cot, gains, w_out, w_in, w_down, *both],
        scratch=[
            pltpu.VMEM((D, D), BF),
            pltpu.VMEM((D, 2 * FF), BF),
            pltpu.VMEM((FF, D), BF),
            pltpu.SemaphoreType.DMA((3 + 5 * len(both),)),
        ],
        any_ins=range(1 + TP + 3, 1 + TP + 6 + len(both)),
        name="feed_forward",
    )
    result, grad_middle, act, gain_two_row = mid[:4]
    act = after(act, *h_near)
    gatts = mid[4:]
    gas = [gatts[0]] + [shift(gatts[k], "z", k) for k in range(1, TP)]

    ffn = order.run(
        functools.partial(ffn_grads_kernel, shards),
        [((2, high_in, 128), BF)] * shards + [((shards, high, 128), BF)] * 2,
        1,
        [idx, act, shift(act, "core", 1), gain_two_row],
        scratch=[
            pltpu.VMEM((4 * shards, pad_d, 2 * rows), BF),
            pltpu.VMEM((4 * shards, pad_f, 2 * rows), BF),
            pltpu.VMEM((4 * shards, pad_d, 2 * rows), BF),
            pltpu.VMEM((2 * rows, 2 * FF + 2 * D), BF),
        ],
        name="ffn_weight_grads",
    )
    f_in = [ffn[0]] + [shift(ffn[k], "shard", k) for k in range(1, shards)]
    f_rest = [ffn[shards], shift(ffn[shards + 1], "x", 1)]
    hs = h_near + [shift(after(v, ffn[0]), "core", 1) for v in h_near]

    dkv_keep, dkv_send, dq = order.run(
        functools.partial(backward_kernel, n_kv),
        [((n_kv // 2, many, 2 * GW), BF)] * 2 + [((many, 256), BF)],
        0,
        [query, *kvs, *gas, attended_t, lse, cosine, sine],
        scratch=[
            pltpu.VMEM((keys, 2 * GW), BF),
            pltpu.VMEM((256, keys), BF),
            pltpu.VMEM((256, many), BF),
            pltpu.VMEM((256, many), BF),
            pltpu.VMEM((many, 2 * GW), BF),
            pltpu.VMEM((many, 2 * GW), BF),
            pltpu.VMEM((keys, 2 * GW), F32),
            pltpu.VMEM((256, many), F32),
        ],
        name="attention_backward",
    )
    mine, other = order.run(
        functools.partial(qkv_grads_kernel, shards, n_kv),
        [((shards, 2, rows_d, WC), BF)] * 2,
        1,
        [idx, *hs, dkv_keep, dkv_send, dq, w_full, gains],
        name="qkv_weight_grads",
    )
    terms = [dkv_keep, shift(after(dkv_send, mine), "core", 1)]
    wq = [mine, shift(after(other, *f_in, *f_rest), "core", 1)]
    terms = [t.reshape(2, outer, many, 2 * GW) for t in terms]
    got = shift(order.add([t[1] for t in terms]), "x", 1)
    terms = [t[0] for t in terms] + [got]

    f_in = reduce_step(order, f_in, "x", 0)
    f_rest = reduce_step(order, f_rest, "shard", 0)
    wq = reduce_step(order, wq, "shard", 0)
    wq = reduce_step(order, wq, "x", 0)

    if outer > 1:
        total = order.add(terms)
        sums = [total[0]] + [shift(total[k], "zo", -k) for k in range(1, outer)]
    else:
        sums = [t[0] for t in terms]
    (gh,) = order.run(
        functools.partial(combine_kernel, len(sums)),
        [((2, 2, rows, D), BF)],
        1,
        [idx, *sums, dq, w_full],
        name="h_one_grads",
    )
    gh = reduce_z(order, [gh], 1)
    f_rest = reduce_z(order, [order.add(f_rest).reshape(2, 2, high // TP, 128)], 1)
    f_in = reduce_z(order, [order.add(f_in).reshape(2, 2, high_in // TP, 128)], 1)
    wq = gather_z(sum_over(order.add(wq), "zo"), 2)
    gh = reduce_z(order, gh, 2)
    wq = gather_z(wq, 1)
    f_rest = reduce_z(order, f_rest, 2)
    f_in = reduce_z(order, f_in, 2)
    wq = jnp.stack(gather(wq, "x"))
    f_rest = gather_z(sum_over(order.add(f_rest), "zo"), 2)
    f_in = gather_z(sum_over(order.add(f_in), "zo"), 2)
    (grad_tokens,) = order.run(
        functools.partial(tail_kernel, len(gh)),
        [((rows, D), F32)],
        0,
        [*gh, tok, grad_middle, gains],
        name="token_grads",
    )
    f_rest = gather_z(after(f_rest, gh[-1]), 1)
    f_in = gather_z(after(f_in, gh[-1]), 1)
    wq_got = shift(wq, "core", 1)
    f_rest = jnp.stack(gather(f_rest, "x"))
    f_in = jnp.stack(gather(f_in, "x"))

    g_qkv, grad_gain_one = order.run(
        qkv_unpack_kernel,
        [((2, 2, rows_d, 3 * D), F32), ((1, part), F32)],
        1,
        [idx, wq, wq_got],
        scratch=[pltpu.VMEM((part, 128), F32)],
        name="qkv_unpack",
    )
    g_out, g_down, grad_gain_two = order.run(
        functools.partial(rest_unpack_kernel, shards),
        [
            ((2, 2, rows_d, D), F32),
            ((2, 2, rows_f, D), F32),
            ((1, part), F32),
        ],
        1,
        [idx, f_rest, shift(f_rest, "core", 1)],
        scratch=[pltpu.VMEM((high, 128), F32), pltpu.VMEM((8, D), F32)],
        name="w_down_w_out_unpack",
    )
    (g_in,) = order.run(
        functools.partial(in_unpack_kernel, shards),
        [((2, 2, rows_d, 2 * FF), F32)],
        1,
        [idx, f_in, shift(f_in, "core", 1)],
        scratch=[pltpu.VMEM((high_in, 128), F32)],
        name="w_in_unpack",
    )

    return (
        result[None],
        grad_tokens[None],
        grad_gain_one.reshape(part),
        g_qkv.reshape(part, 3 * D),
        g_out.reshape(part, D),
        grad_gain_two.reshape(part),
        g_in.reshape(part, 2 * FF),
        g_down.reshape(w_down.shape[0], D),
    )


def solution(mesh):
    blocks = mesh.shape["ctx"]
    fine = Mesh(
        mesh.devices.reshape(blocks // (TP * 4), TP, 2, 2, mesh.shape["shard"]), CTX + ("shard",)
    )
    rows, split = P("shard", CTX, None), P("shard", None)
    return jax.shard_map(
        per_device,
        mesh=fine,
        in_specs=(rows, P("shard"), split, split, P("shard"), split, split, rows),
        out_specs=(rows, rows, P("shard"), split, split, P("shard"), split, split),
        check_vma=False,
    )
```

```python
import functools
import math

import jax
import jax.numpy as jnp
from jax import lax
from jax.experimental import pallas as pl
from jax.experimental.pallas import tpu as pltpu
from jax.sharding import Mesh, PartitionSpec as P

D = 768
HEADS = 12
HEAD_DIM = 64
FF = 1152
EPS = 1e-05
THETA = 160000.0

TP = 4
GH = HEADS // TP
GW = GH * HEAD_DIM
WC = 640
CTX = ("zo", "z", "x", "core")
BF = jnp.bfloat16
F32 = jnp.float32
VMEM_LIMIT = 56 * 1024 * 1024

KEY_AT = ((0, 0), (0, 1), (1, 0))
VALUE_AT = ((1, 1), (2, 0), (2, 1))


def dot(a, b):
    return jnp.dot(a, b, preferred_element_type=F32)


def dot_nt(a, b):
    return lax.dot_general(a, b, (((1,), (1,)), ((), ())), preferred_element_type=F32)


def dot_tn(a, b):
    return lax.dot_general(a, b, (((0,), (0,)), ((), ())), preferred_element_type=F32)


def call(body, outs, n_smem, ins, scratch=(), any_ins=(), name=None):
    specs = []
    for i in range(len(ins)):
        if i < n_smem:
            specs.append(pl.BlockSpec(memory_space=pltpu.SMEM))
        elif i in any_ins:
            specs.append(pl.BlockSpec(memory_space=pl.ANY))
        else:
            specs.append(pl.BlockSpec(memory_space=pltpu.VMEM))
    return pl.pallas_call(
        body,
        out_shape=[jax.ShapeDtypeStruct(s, t) for s, t in outs],
        in_specs=specs,
        out_specs=[pl.BlockSpec(memory_space=pltpu.VMEM)] * len(outs),
        scratch_shapes=list(scratch),
        compiler_params=pltpu.CompilerParams(vmem_limit_bytes=VMEM_LIMIT),
        cost_estimate=pl.CostEstimate(
            flops=1, bytes_accessed=1, transcendentals=0
        ),
        name=name,
    )(*ins)


def normalise(values):
    mean = jnp.mean(values, axis=-1, keepdims=True)
    centred = values - mean
    spread = jnp.mean(centred * centred, axis=-1, keepdims=True)
    scale = lax.rsqrt(spread + EPS)
    return centred * scale, scale


def normalise_back(grad_unit, unit, scale):
    return scale * (
        grad_unit
        - jnp.mean(grad_unit, axis=-1, keepdims=True)
        - unit * jnp.mean(grad_unit * unit, axis=-1, keepdims=True)
    )


def turn(tile, cosine, signed_sine, first_half):
    swapped = jnp.where(first_half, pltpu.roll(tile, 96, 1), pltpu.roll(tile, 32, 1))
    return tile * cosine + swapped * signed_sine


def lane_masks(rows):
    lane = lax.broadcasted_iota(jnp.int32, (rows, 128), 1)
    return lax.rem(lane, 64) < 32, lane < 64


def group_kernel(idx, w_ref, one_ref, two_ref, own_ref, half_ref):
    height = w_ref.shape[0]
    half = height // 2
    for g in range(TP):

        @pl.when(idx[0] == g)
        def _():
            parts = [w_ref[:, p * D + g * GW : p * D + (g + 1) * GW] for p in (1, 2, 0)]
            parts.append(jnp.zeros((height, WC - 3 * GW), BF))
            own_ref[...] = jnp.concatenate(parts, axis=1)

    half_ref[0:half, :] = own_ref[pl.ds(pl.multiple_of(idx[2] * half, half), half), :]
    half_ref[half:, :] = jnp.zeros((16, WC), BF)
    half_ref[half : half + 1, 0:height] = one_ref[...].reshape(1, height)
    half_ref[half + 1 : half + 2, 0:height] = two_ref[...].reshape(1, height)


def pack_kernel(idx, out_ref, in_ref, down_ref, pack_ref):
    c = idx[2]
    half = out_ref.shape[0] // 2
    at = pl.ds(pl.multiple_of(c * half, half), half)
    pack_ref[0:half, :] = out_ref[at, :]
    for b in range(3):
        pack_ref[(1 + b) * half : (2 + b) * half, :] = in_ref[at, b * D : (b + 1) * D]
    count, step = down_half(down_ref.shape[0])
    at = pl.ds(pl.multiple_of(c * step, 16), count)
    pack_ref[4 * half :, :] = down_ref[at, :]


def down_half(height):
    count = -(-height // 32) * 16
    return count, height - count


def front_kernel(shards, idx, *refs):
    toks = refs[:TP]
    n_w = 2 * shards - 1
    ws = refs[TP : TP + n_w]
    mine, cos_ref, sin_ref, q_ref, kv_ref, h_ref, w_ref, gains_ref = refs[TP + n_w :]
    c, y = idx[2], idx[3]
    rows = toks[0].shape[0]
    part = ws[0].shape[0]
    half = part // 2
    gains_ref[...] = jnp.zeros_like(gains_ref)
    for k in range(shards):
        start = lax.rem(y - k + shards, shards) * part
        at = pl.ds(pl.multiple_of(start, part), part)
        if k == 0:
            w_ref[at, :] = ws[0][...]
            continue
        at = pl.ds(pl.multiple_of(start + c * half, half), half)
        w_ref[at, :] = ws[2 * k - 1][0:half]
        at = pl.ds(pl.multiple_of(start + (1 - c) * half, half), half)
        w_ref[at, :] = ws[2 * k][0:half]
    for s in range(shards):

        @pl.when(y == s)
        def _():
            for k in range(shards):
                start = (s - k) % shards * part
                gains = (ws[2 * k - 1] if k else mine)[half : half + 2, 0:part]
                gains_ref[0:2, start : start + part] = gains.astype(F32)

    gain = gains_ref[0:1, :]
    first, low = lane_masks(rows)
    for j in range(TP):
        at = slice(j * rows, (j + 1) * rows)
        unit, _ = normalise(toks[j][...].astype(F32))
        h = (unit * gain).astype(BF)
        h_ref[at, :] = h
        out = dot(h, w_ref[...])
        cosine, sine = cos_ref[at, :], sin_ref[at, :]
        key_a = turn(out[:, 0:128], cosine, sine, first)
        mixed = out[:, 128:256]
        key_b = jnp.where(low, turn(mixed, cosine, sine, first), mixed)
        kv_ref[at, 0:128] = key_a.astype(BF)
        kv_ref[at, 128:256] = key_b.astype(BF)
        kv_ref[at, 256:384] = out[:, 256:384].astype(BF)
        query_a = turn(out[:, 384:512], cosine, sine, first)
        query_b = jnp.where(low, turn(out[:, 512:640], cosine, sine, first), 0.0)
        factor = HEAD_DIM ** (-0.5)
        q_ref[at, 0:128] = (query_a * factor).astype(BF)
        q_ref[at, 128:256] = (query_b * factor).astype(BF)


def half_rows(values_t, head):
    at = head * HEAD_DIM
    rows = values_t[at : at + HEAD_DIM]
    zeros = jnp.zeros_like(rows)
    return jnp.concatenate([rows, zeros] if head % 2 == 0 else [zeros, rows], axis=0)


def forward_kernel(n_kv, last, q_ref, *refs):
    kvs = refs[:n_kv]
    if last:
        before_ref, before_lse = refs[n_kv : n_kv + 2]
        atts = refs[n_kv + 2 : n_kv + 2 + TP]
    att_t_ref, lse_ref, kv_s, v_t, q_t = refs[-5:]
    rows = kvs[0].shape[0]
    block = math.gcd(rows, 256)
    for i, kv in enumerate(kvs):
        kv_s[i * rows : (i + 1) * rows, :] = kv[...]
        v_t[:, i * rows : (i + 1) * rows] = kv[:, 128:384].T
    q_t[...] = q_ref[...].T
    lse_ref[...] = jnp.zeros_like(lse_ref)
    for i in range(rows // block):
        at = slice(i * block, (i + 1) * block)
        for h in range(GH):
            tile = KEY_AT[h][0]
            keys = kv_s[:, tile * 128 : tile * 128 + 128]
            scores = dot(keys, half_rows(q_t[:, at], h))
            top = jnp.max(scores, axis=0, keepdims=True)
            weights = jnp.exp(scores - top)
            total = jnp.sum(weights, axis=0, keepdims=True)
            tile, half = VALUE_AT[h]
            values_t = v_t[(tile - 1) * 128 : tile * 128, :]
            out = dot(values_t, weights.astype(BF))[half * 64 : half * 64 + 64]
            head = slice(h * 64, h * 64 + 64)
            if last:
                old = before_lse[h : h + 1, at]
                high = jnp.maximum(old, top)
                share, own = jnp.exp(old - high), jnp.exp(top - high)
                total = total * own + share
                out = out * own + before_ref[head, at] * share
                top = high
            att_t_ref[head, at] = out / total
            lse_ref[h : h + 1, at] = top + jnp.log(total)
    if last:
        small = rows // TP
        for j in range(TP):
            atts[j][...] = att_t_ref[:, j * small : (j + 1) * small].T.astype(BF)


def backward_kernel(n_kv, q_ref, *refs):
    kvs = refs[:n_kv]
    gas = refs[n_kv : n_kv + TP]
    att_t_ref, lse_ref = refs[n_kv + TP : n_kv + TP + 2]
    tables = refs[n_kv + TP + 2 : n_kv + TP + 4]
    keep_ref, send_ref, dq_ref = refs[n_kv + TP + 4 : n_kv + TP + 7]
    kv_s, k_t, q_t, g_t, q_m, g_m, acc, dq_t = refs[n_kv + TP + 7 :]
    rows = kvs[0].shape[0]
    small = gas[0].shape[0]
    block = math.gcd(rows, 256)
    for i, kv in enumerate(kvs):
        kv_s[i * rows : (i + 1) * rows, :] = kv[...]
        k_t[:, i * rows : (i + 1) * rows] = kv[:, 0:256].T
    q_t[...] = q_ref[...].T
    _, low = lane_masks(small)
    for j in range(TP):
        at = slice(j * small, (j + 1) * small)
        g_t[:, at] = gas[j][...].T
        first, second = gas[j][:, 0:128], gas[j][:, 128:256].astype(F32)
        g_m[at, 0:128] = first
        g_m[at, 128:256] = jnp.where(low, second, 0.0).astype(BF)
        g_m[at, 256:384] = jnp.where(low, 0.0, second).astype(BF)
        both = q_ref[at, 0:128].astype(F32)
        q_m[at, 0:128] = jnp.where(low, both, 0.0).astype(BF)
        q_m[at, 128:256] = jnp.where(low, 0.0, both).astype(BF)
        q_m[at, 256:384] = q_ref[at, 128:256]
    dq_t[...] = jnp.zeros_like(dq_t)
    acc[...] = jnp.zeros_like(acc)
    for i in range(rows // block):
        at = slice(i * block, (i + 1) * block)
        for h in range(GH):
            ktile, khalf = KEY_AT[h]
            vtile = VALUE_AT[h][0]
            klanes = slice(ktile * 128, ktile * 128 + 128)
            vlanes = slice(vtile * 128, vtile * 128 + 128)
            scores = dot(kv_s[:, klanes], half_rows(q_t[:, at], h))
            probs = jnp.exp(scores - lse_ref[h : h + 1, at])
            grad_t = half_rows(g_t[:, at], h + 1)
            grad_probs = dot(kv_s[:, vlanes], grad_t)
            own = g_t[(h + 1) * 64 : (h + 2) * 64, at].astype(F32)
            inner = jnp.sum(
                own * att_t_ref[h * 64 : h * 64 + 64, at], axis=0, keepdims=True
            )
            grad_scores = (probs * (grad_probs - inner)).astype(BF)
            lanes = slice(h * 128, h * 128 + 128)
            acc[:, vlanes] += dot(probs.astype(BF), g_m[at, lanes])
            acc[:, klanes] += dot(grad_scores, q_m[at, lanes])
            part = dot(k_t[klanes, :], grad_scores)[khalf * 64 : khalf * 64 + 64]
            dq_t[h * 64 : h * 64 + 64, at] = part * HEAD_DIM ** (-0.5)
    first, low = lane_masks(rows)
    cosine, sine = tables[0][0:rows, :], -tables[1][0:rows, :]
    grad_q = dq_t[...].T
    for t in range(2):
        lanes = slice(t * 128, t * 128 + 128)
        dq_ref[:, lanes] = turn(grad_q[:, lanes], cosine, sine, first).astype(BF)
    for i in range(n_kv):
        at = slice(i * rows, (i + 1) * rows)
        cosine, sine = tables[0][at, :], -tables[1][at, :]
        target = keep_ref if i < n_kv // 2 else send_ref
        block = i % (n_kv // 2)
        grad = acc[at, 0:128]
        target[block, :, 0:128] = turn(grad, cosine, sine, first).astype(BF)
        grad = acc[at, 128:256]
        grad = jnp.where(low, turn(grad, cosine, sine, first), grad)
        target[block, :, 128:256] = grad.astype(BF)
        target[block, :, 256:384] = acc[at, 256:384].astype(BF)


ACT_H, ACT_MIX, ACT_GU, ACT_GB, ACT_ATT, ACT_COT, ACT_ALL = (
    0, D, D + FF, D + 3 * FF, 2 * D + 3 * FF, 3 * D + 3 * FF, 4 * D + 3 * FF
)


def middle_kernel(n_packs, idx, *refs):
    atts = refs[:TP]
    tok_ref, cot_ref, gains_ref, out_own, in_own, down_own = refs[TP : TP + 6]
    packs = refs[TP + 6 : TP + 6 + n_packs]
    rest = refs[TP + 6 + n_packs :]
    result_ref, gmid_ref, act_ref, gain_ref = rest[:4]
    gatts = rest[4 : 4 + TP]
    w_out, w_in, w_down, sems = rest[4 + TP :]
    half = out_own.shape[0] // 2
    count, step = down_half(down_own.shape[0])

    def rows(start, height):
        return pl.ds(pl.multiple_of(start, 16), height)

    z, c, y = idx[0], idx[2], idx[3]
    shards = n_packs // 2 + 1
    own, own_down = y * 2 * half, y * down_own.shape[0]
    outs = [pltpu.make_async_copy(out_own, w_out.at[rows(own, 2 * half), :], sems.at[0])]
    ins = [pltpu.make_async_copy(in_own, w_in.at[rows(own, 2 * half), :], sems.at[1])]
    target = w_down.at[rows(own_down, down_own.shape[0]), :]
    downs = [pltpu.make_async_copy(down_own, target, sems.at[2])]
    for i, pack in enumerate(packs):
        shard = lax.rem(y - (i // 2 + 1) + shards, shards)
        core = 1 - c if i % 2 else c
        at = rows((shard * 2 + core) * half, half)
        source = pack.at[0:half, :]
        outs.append(pltpu.make_async_copy(source, w_out.at[at, :], sems.at[3 + 5 * i]))
        for b in range(3):
            source = pack.at[(1 + b) * half : (2 + b) * half, :]
            target = w_in.at[at, b * D : (b + 1) * D]
            ins.append(pltpu.make_async_copy(source, target, sems.at[4 + 5 * i + b]))
        at = rows(shard * down_own.shape[0] + core * step, count)
        source = pack.at[4 * half : 4 * half + count, :]
        downs.append(pltpu.make_async_copy(source, w_down.at[at, :], sems.at[7 + 5 * i]))
    apart = 2 * count == down_own.shape[0]
    for copy in outs + ins + (downs if apart else downs[:1]):
        copy.start()
    starts = [pl.multiple_of(lax.rem(z + j, TP) * GW, GW) for j in range(TP)]
    for copy in outs:
        copy.wait()
    middle = tok_ref[...].astype(F32)
    for j in range(TP):
        middle += dot(atts[j][...], w_out[pl.ds(starts[j], GW), :])
        act_ref[:, ACT_ATT + j * GW : ACT_ATT + (j + 1) * GW] = atts[j][...]
    gain = gains_ref[1:2, :]
    unit, scale = normalise(middle)
    h = (unit * gain).astype(BF)
    act_ref[:, ACT_H : ACT_H + D] = h
    for copy in ins:
        copy.wait()
    gate = dot(h, w_in[:, :FF])
    up = dot(h, w_in[:, FF:])
    phi = 0.5 * (1.0 + lax.erf(gate * math.sqrt(0.5)))
    active = gate * phi
    mixed = (active * up).astype(BF)
    act_ref[:, ACT_MIX : ACT_MIX + FF] = mixed
    for i, copy in enumerate(downs):
        if i and not apart:
            copy.start()
        copy.wait()
    grad_mixed = dot_nt(cot_ref[...], w_down[...])
    slope = phi + gate * (jnp.exp(-0.5 * gate * gate) * (1.0 / math.sqrt(2.0 * math.pi)))
    grad_gate = (grad_mixed * up * slope).astype(BF)
    grad_up = (grad_mixed * active).astype(BF)
    act_ref[:, ACT_GU : ACT_GU + FF] = grad_gate
    act_ref[:, ACT_GU + FF : ACT_GU + 2 * FF] = grad_up
    grad_h = dot_nt(grad_gate, w_in[:, :FF]) + dot_nt(grad_up, w_in[:, FF:])
    gain_ref[...] = jnp.broadcast_to(
        jnp.sum(grad_h * unit, axis=0, keepdims=True), gain_ref.shape
    )
    grad_middle = cot_ref[...].astype(F32) + normalise_back(grad_h * gain, unit, scale)
    gmid_ref[...] = grad_middle
    gb = grad_middle.astype(BF)
    act_ref[:, ACT_GB : ACT_GB + D] = gb
    act_ref[:, ACT_COT : ACT_COT + D] = cot_ref[...]
    for j in range(TP):
        part = dot_nt(gb, w_out[pl.ds(starts[j], GW), :])
        pad = jnp.zeros((part.shape[0], 256 - GW), F32)
        gatts[j][...] = jnp.concatenate([pad, part], axis=1).astype(BF)
    result_ref[...] = middle + dot(mixed, w_down[...])


def up16(n):
    return -(-n // 16) * 16


def plan(shards):
    rows_d, rows_f = D // (4 * shards), FF // (4 * shards)
    return rows_d, rows_f, up16(rows_d), up16(rows_f)


def ffn_grads_kernel(shards, idx, own, got, gain_ref, *refs):
    ins = refs[:shards]
    mine_ref, other_ref = refs[shards : shards + 2]
    h_t, mixed_t, att_t, right = refs[shards + 2 :]
    z, x, c, y = idx[0], idx[1], idx[2], idx[3]
    rows_d, rows_f, pad_d, pad_f = plan(shards)
    n = own.shape[0]
    pieces, per = 4 * shards, GW // rows_d
    for i, act in enumerate((own, got)):
        at = slice(i * n, (i + 1) * n)
        h = act[:, ACT_H : ACT_H + D].T
        mixed = act[:, ACT_MIX : ACT_MIX + FF].T
        att = act[:, ACT_ATT : ACT_ATT + D].T
        for m in range(pieces):
            h_t[m, 0:rows_d, at] = h[m * rows_d : (m + 1) * rows_d]
            mixed_t[m, 0:rows_f, at] = mixed[m * rows_f : (m + 1) * rows_f]
            att_t[m, 0:rows_d, at] = att[m * rows_d : (m + 1) * rows_d]
        right[at, 0 : 2 * FF] = act[:, ACT_GU : ACT_GU + 2 * FF]
        right[at, 2 * FF : 2 * FF + D] = act[:, ACT_GB : ACT_GB + D]
        right[at, 2 * FF + D :] = act[:, ACT_COT : ACT_COT + D]
    for k in range(shards):
        piece = (lax.rem(y + k, shards) * 2 + c) * 2
        left = h_t[pl.ds(piece, 2)].reshape(2 * pad_d, 2 * n)
        grad = dot(left, right[:, 0 : 2 * FF]).astype(BF)
        for xx in range(2):
            for t in range(2 * FF // 128):
                ins[k][xx, t * pad_d : t * pad_d + rows_d, :] = grad[
                    xx * pad_d : xx * pad_d + rows_d, t * 128 : t * 128 + 128
                ]
    high = mine_ref.shape[3] * TP
    gain = jnp.broadcast_to(gain_ref[0:1, :], (high - pad_f - pad_d, D)).astype(BF)
    for xx in range(2):
        for s in range(shards):
            piece = (s * 2 + c) * 2 + xx
            turned = lax.rem(piece // per - z + TP, TP) * per + lax.rem(piece, per)
            down = dot(mixed_t[piece], right[:, 2 * FF + D :]).astype(BF)
            out = dot(att_t[turned], right[:, 2 * FF : 2 * FF + D]).astype(BF)
            both = jnp.concatenate([down, out, gain], axis=0)
            for q in range(TP):
                chunk = both[q * (high // TP) : (q + 1) * (high // TP)]

                @pl.when(lax.rem(z, 2) == q % 2)
                def _():
                    mine_ref[q // 2, s, xx] = chunk

                @pl.when(lax.rem(z, 2) != q % 2)
                def _():
                    other_ref[q // 2, s, xx] = chunk


def qkv_grads_kernel(shards, n_kv, idx, *refs):
    hs = refs[:n_kv]
    keep_ref, send_ref, dq_ref, w_ref, gains_ref, mine_ref, other_ref = refs[n_kv:]
    c = idx[2]
    total = None
    for i in range(n_kv):
        grads = (keep_ref if i < n_kv // 2 else send_ref)[i % (n_kv // 2)]
        part = dot(grads.T, hs[i][...])
        total = part if total is None else total + part
    grad = jnp.concatenate([total, dot(dq_ref[...].T, hs[0][...])], axis=0).T
    gain = gains_ref[...].T[:, 0:1]
    lane = lax.broadcasted_iota(jnp.int32, grad.shape, 1)
    by_gain = jnp.sum(grad * w_ref[...].astype(F32), axis=1, keepdims=True) / gain
    grad = jnp.where(lane < 3 * GW, grad, by_gain).astype(BF)
    height = plan(shards)[0]
    for s in range(shards):
        for cc in range(2):
            block = (s * 2 + cc) * 2 * height
            for xx in range(2):
                part = grad[block + xx * height : block + (xx + 1) * height]

                @pl.when(c == cc)
                def _():
                    mine_ref[s, xx] = part

                @pl.when(c != cc)
                def _():
                    other_ref[s, xx] = part


def h_one_grads_kernel(n_sum, idx, *refs):
    parts = refs[:n_sum]
    dq_ref, w_ref, gh_mine, gh_other = refs[n_sum:]
    rows = gh_mine.shape[1]
    for j in range(TP):
        at = slice(j * rows, (j + 1) * rows)
        total = parts[0][0, at, :].astype(F32)
        for part in parts[1:]:
            total += part[0, at, :].astype(F32)
        grad = jnp.concatenate([total.astype(BF), dq_ref[at, :]], axis=1)
        owner = lax.rem(idx[0] - j + TP, TP)
        target = gh_other if j % 2 else gh_mine
        target[owner // 2] = dot_nt(grad, w_ref[...]).astype(BF)


def tail_kernel(n_sum, idx, *refs):
    tok_ref, gmid_ref, gains_ref, out_ref = refs[n_sum:]
    unit, scale = normalise(tok_ref[...].astype(F32))
    total = 0.0
    for grad in refs[:n_sum]:
        grad = grad[idx[0] // 2] if len(grad.shape) == 3 else grad[...]
        total += grad.astype(F32)
    grad_unit = total * gains_ref[0:1, :]
    out_ref[...] = gmid_ref[...] + normalise_back(grad_unit, unit, scale)


def place_z(z, k):
    return lax.rem(z // 2 + k % 2, 2) * 2 + lax.rem(lax.rem(z, 2) + k // 2, 2)


def in_unpack_kernel(shards, idx, own, got, in_ref, held):
    rows_d, _, pad_d, _ = plan(shards)
    size = held.shape[0] // TP
    z, x, c = idx[0], idx[1], idx[2]
    for cr in range(2):
        for xr in range(2):
            for k in range(TP):
                at = pl.ds(pl.multiple_of(place_z(z, k) * size, size), size)
                held[at, :] = (got if cr else own)[xr, k].astype(F32)
            cc, xx = lax.rem(c + cr, 2), lax.rem(x + xr, 2)
            for t in range(2 * FF // 128):
                base = t * pad_d
                in_ref[cc, xx, :, t * 128 : t * 128 + 128] = held[base : base + rows_d, :]


def rest_unpack_kernel(shards, idx, own, got, out_ref, down_ref, gain_ref, held):
    rows_d, rows_f, pad_d, pad_f = plan(shards)
    size = held.shape[0] // TP
    z, x, c = idx[0], idx[1], idx[2]
    gain = None
    for cr in range(2):
        for xr in range(2):
            for k in range(TP):
                at = pl.ds(pl.multiple_of(place_z(z, k) * size, size), size)
                held[at, :] = (got if cr else own)[xr, k].astype(F32)
            cc, xx = lax.rem(c + cr, 2), lax.rem(x + xr, 2)
            down_ref[cc, xx] = held[0:rows_f, :]
            out_ref[cc, xx] = held[pad_f : pad_f + rows_d, :]
            if xr == 0:
                row = held[pad_f + pad_d : pad_f + pad_d + 8, :]
                gain = row if gain is None else gain + row
    part = gain_ref.shape[0]
    for s in range(shards):

        @pl.when(idx[3] == s)
        def _():
            gain_ref[...] = gain[0:1, s * part : (s + 1) * part].reshape(part)


def qkv_unpack_kernel(idx, own, got, out_ref, gain_ref, gain_s):
    z, x, c = idx[0], idx[1], idx[2]
    for cr in range(2):
        for xr in range(2):
            cc, xx = lax.rem(c + cr, 2), lax.rem(x + xr, 2)
            gain = None
            for g in range(TP):
                k = 2 * lax.rem(g % 2 + z, 2) + lax.rem(g // 2 + z // 2, 2)
                block = (got if cr else own)[xr, k].astype(F32)
                for source, place in ((0, 1), (1, 2), (2, 0)):
                    out_ref[cc, xx, :, place * D + g * GW : place * D + (g + 1) * GW] = block[
                        :, source * GW : (source + 1) * GW
                    ]
                tail = block[:, 512:640]
                gain = tail if gain is None else gain + tail
            height = gain.shape[0]
            at = pl.multiple_of((cc * 2 + xx) * height, height)
            gain_s[pl.ds(at, height), :] = gain
    gain_ref[...] = gain_s[...].T[64:65].reshape(gain_ref.shape)


def shift(value, axis, k):
    n = lax.axis_size(axis)
    return lax.ppermute(value, axis, [(i, (i + k) % n) for i in range(n)])


def gather(value, axis):
    return [value] + [shift(value, axis, k) for k in range(1, lax.axis_size(axis))]


def pick(value, index, dim):
    return lax.dynamic_index_in_dim(value, index, dim, keepdims=False)


def term(value, *views):
    return (value, views)


def take(index, dim):
    return lambda value: pick(value, index, dim)


def reshaped(*shape):
    return lambda value: value.reshape(shape)


def viewed(terms, view):
    return [(value, views + (view,)) for value, views in terms]


def reduce_step(order, terms, axis, dim):
    n, i = lax.axis_size(axis), lax.axis_index(axis)
    got = []
    for k in range(1, n):
        part = order.add(viewed(terms, take(lax.rem(i + k, n), dim)))
        got.append(term(shift(part, axis, k)))
    return viewed(terms, take(i, dim)) + got


def add(values):
    total = values[0].astype(F32)
    for value in values[1:]:
        total = total + value.astype(F32)
    return total.astype(BF)


def swap_z(value, bit):
    return lax.ppermute(value, "z", [(i, i ^ bit) for i in range(TP)])


def reduce_z(order, terms, bit):
    z = lax.axis_index("z")
    i, dim = (z % 2, 1) if bit == 1 else (z // 2, 0)
    part = order.add(viewed(terms, take(1 - i, dim)))
    return viewed(terms, take(i, dim)) + [term(swap_z(part, bit))]


def gather_z(order, value, bit):
    value = order.step(value)
    got = swap_z(value, bit)
    return jnp.stack([value, got]) if bit == 2 else jnp.concatenate([value, got])


def sum_over(value, axis):
    return add([value] + [shift(value, axis, k) for k in range(1, lax.axis_size(axis))])


def after(value, *others):
    return lax.optimization_barrier((value, *others))[0]


class Order:
    def __init__(self):
        self.last = None

    def __call__(self, values):
        if self.last is None:
            return values
        return lax.optimization_barrier((values, self.last))[0]

    def step(self, value):
        self.last = self(value)
        return self.last

    def add(self, terms):
        values = []
        for value, (_, views) in zip(self([t[0] for t in terms]), terms):
            for view in views:
                value = view(value)
            values.append(value)
        self.last = add(values)
        return self.last

    def run(self, body, outs, n_smem, ins, **more):
        got = call(body, outs, n_smem, self(list(ins)), **more)
        self.last = got[0]
        return got


def per_device(tokens, gain_one, w_qkv, w_out, gain_two, w_in, w_down, cotangent):
    tok, cot = tokens[0], cotangent[0]
    rows = tok.shape[0]
    many = TP * rows
    zo, z = lax.axis_index("zo"), lax.axis_index("z")
    x, c, y = lax.axis_index("x"), lax.axis_index("core"), lax.axis_index("shard")
    outer, shards = lax.axis_size("zo"), lax.axis_size("shard")
    part = w_qkv.shape[0]
    n_kv = 4 * outer
    keys = n_kv * many
    rows_d, rows_f, pad_d, pad_f = plan(shards)
    high_in, high = 2 * FF // 128 * pad_d, -(-(pad_f + pad_d + 16) // 64) * 64
    i32 = jnp.int32
    idx = jnp.stack([z, x, c, y]).astype(i32)
    order = Order()

    toks = gather(tok, "z")
    w_own, w_mine = order.run(
        group_kernel,
        [((part, WC), BF), ((part // 2 + 16, WC), BF)],
        1,
        [idx, w_qkv, gain_one, gain_two],
        name="group_columns",
    )
    w_slices = [w_own]
    for k in range(1, shards):
        w_slices.append(shift(w_mine, "shard", k))
        w_slices.append(shift(w_slices[-1], "core", 1))
    (pack,) = order.run(
        pack_kernel,
        [((2 * part + down_half(w_down.shape[0])[0], D), BF)],
        1,
        [idx, w_out, w_in, w_down],
        name="pack_weights",
    )
    packs = [shift(pack, "shard", k) for k in range(1, shards)]

    freq = THETA ** (-jnp.arange(HEAD_DIM // 2, dtype=F32) * (2.0 / HEAD_DIM))
    owners = lax.rem(z - jnp.arange(TP, dtype=i32) + TP, TP)
    places = []
    for cr in range(2):
        for xr in range(2):
            for zr in range(outer):
                zz = lax.rem(zo - zr + outer, outer)
                place = ((zz * TP + owners) * 2 + lax.rem(x + xr, 2)) * 2 + lax.rem(c + cr, 2)
                places.append(place)
    first_place = jnp.concatenate(places) * rows
    freq = jnp.tile(freq, 4)[None, :]
    sign = jnp.where(jnp.arange(128) % 64 < 32, -1.0, 1.0).astype(F32)
    start = first_place.astype(F32)[:, None] * freq
    step = jnp.arange(rows, dtype=i32).astype(F32)[:, None] * freq
    cos_a, sin_a = jnp.cos(start)[:, None], jnp.sin(start)[:, None]
    cos_b, sin_b = jnp.cos(step)[None], jnp.sin(step)[None]
    cosine = (cos_a * cos_b - sin_a * sin_b).reshape(keys, 128)
    sine = ((sin_a * cos_b + cos_a * sin_b) * sign).reshape(keys, 128)

    query, kv, h_one, w_full, gains = order.run(
        functools.partial(front_kernel, shards),
        [
            ((many, 256), BF),
            ((many, 2 * GW), BF),
            ((many, D), BF),
            ((D, WC), BF),
            ((8, D), F32),
        ],
        1,
        [idx, *toks, *w_slices, w_mine, cosine, sine],
        name="front",
    )

    near = gather(kv, "zo")
    near = near + [shift(v, "x", 1) for v in near]
    kv_core = shift(kv, "core", 1)
    close = (0, n_kv // 2)
    far = [i for i in range(n_kv) if i not in close]
    scratch = lambda count: [
        pltpu.VMEM((count * many, 2 * GW), BF),
        pltpu.VMEM((256, count * many), BF),
        pltpu.VMEM((256, many), BF),
    ]
    first = order.run(
        functools.partial(forward_kernel, 2, False),
        [((GW, many), F32), ((8, many), F32)],
        0,
        [query, kv, kv_core],
        scratch=scratch(2),
        name="attention_forward_near",
    )
    kvs = near + [kv_core] + [shift(after(v, *first), "core", 1) for v in near[1:]]
    att = order.run(
        functools.partial(forward_kernel, len(far), True),
        [((rows, GW), BF)] * TP + [((GW, many), F32), ((8, many), F32)],
        0,
        [query, *[kvs[i] for i in far], *first],
        scratch=scratch(len(far)),
        name="attention_forward_far",
    )
    att_blocks, (attended_t, lse) = att[:TP], att[TP:]
    h_near = gather(after(h_one, lse), "zo")
    h_near = h_near + [shift(v, "x", 1) for v in h_near]
    h_core = shift(after(h_one, lse), "core", 1)
    atts = [att_blocks[0]] + [shift(att_blocks[k], "z", -k) for k in range(1, TP)]

    packs = [after(p, lse) for p in packs]
    both = [v for p in packs for v in (p, shift(p, "core", 1))]
    mid = order.run(
        functools.partial(middle_kernel, len(both)),
        [((rows, D), F32), ((rows, D), F32), ((rows, ACT_ALL), BF), ((8, D), F32)]
        + [((rows, 256), BF)] * TP,
        1,
        [idx, *atts, tok, cot, after(gains, h_core), w_out, w_in, w_down, *both],
        scratch=[
            pltpu.VMEM((D, D), BF),
            pltpu.VMEM((D, 2 * FF), BF),
            pltpu.VMEM((FF, D), BF),
            pltpu.SemaphoreType.DMA((3 + 5 * len(both),)),
        ],
        any_ins=range(1 + TP + 3, 1 + TP + 6 + len(both)),
        name="feed_forward",
    )
    result, grad_middle, act, gain_two_row = mid[:4]
    act = after(act, *h_near)
    gatts = mid[4:]
    gas = [gatts[0]] + [shift(gatts[k], "z", k) for k in range(1, TP)]

    hs = h_near + [h_core] + [shift(after(v, result), "core", 1) for v in h_near[1:]]
    gain_two_row = after(gain_two_row, *hs)
    ffn = order.run(
        functools.partial(ffn_grads_kernel, shards),
        [((2, high_in, 128), BF)] * shards
        + [((2, shards, 2, high // TP, D), BF)] * 2,
        1,
        [idx, act, shift(act, "core", 1), gain_two_row],
        scratch=[
            pltpu.VMEM((4 * shards, pad_d, 2 * rows), BF),
            pltpu.VMEM((4 * shards, pad_f, 2 * rows), BF),
            pltpu.VMEM((4 * shards, pad_d, 2 * rows), BF),
            pltpu.VMEM((2 * rows, 2 * FF + 2 * D), BF),
        ],
        name="ffn_weight_grads",
    )
    f_in = [term(ffn[0])]
    f_in += [term(shift(after(ffn[k], *gas), "shard", k)) for k in range(1, shards)]
    f_rest = [term(ffn[shards]), term(swap_z(after(ffn[shards + 1], *gas), 1))]

    dkv_keep, dkv_send, dq = order.run(
        functools.partial(backward_kernel, n_kv),
        [((n_kv // 2, many, 2 * GW), BF)] * 2 + [((many, 256), BF)],
        0,
        [query, *kvs, *gas, attended_t, lse, cosine, sine],
        scratch=[
            pltpu.VMEM((keys, 2 * GW), BF),
            pltpu.VMEM((256, keys), BF),
            pltpu.VMEM((256, many), BF),
            pltpu.VMEM((256, many), BF),
            pltpu.VMEM((many, 2 * GW), BF),
            pltpu.VMEM((many, 2 * GW), BF),
            pltpu.VMEM((keys, 2 * GW), F32),
            pltpu.VMEM((256, many), F32),
        ],
        name="attention_backward",
    )
    mine, other = order.run(
        functools.partial(qkv_grads_kernel, shards, n_kv),
        [((shards, 2, rows_d, WC), BF)] * 2,
        1,
        [idx, *hs, dkv_keep, dkv_send, dq, w_full, gains],
        name="qkv_weight_grads",
    )
    first_got = [t[0] for t in f_in[1:] + f_rest[1:]]
    mine, other, *_ = lax.optimization_barrier((mine, other, *first_got))
    order.last = mine
    terms = [term(dkv_keep), term(shift(after(dkv_send, mine), "core", 1))]
    terms = viewed(terms, reshaped(2, outer, many, 2 * GW))
    wq = [term(mine), term(shift(other, "core", 1))]

    def pair(value):
        return jnp.stack([value, shift(order.step(value), "x", 1)])

    f_in = reduce_step(order, f_in, "x", 0)
    f_rest = reduce_z(order, f_rest, 2)
    wq = reduce_step(order, wq, "shard", 0)
    got = shift(order.add(viewed(terms, take(1, 0))), "x", 1)
    terms = viewed(terms, take(0, 0)) + [term(got)]
    wq = reduce_step(order, wq, "x", 0)
    if outer > 1:
        total = order.add(terms)
        sums = [total[0:1]] + [shift(total[k : k + 1], "zo", -k) for k in range(1, outer)]
    else:
        sums = [
            dkv_keep.reshape(2, many, 2 * GW),
            terms[1][0].reshape(2, many, 2 * GW),
            got.reshape(1, many, 2 * GW),
        ]
    gh, gh_other = order.run(
        functools.partial(h_one_grads_kernel, len(sums)),
        [((2, rows, D), BF)] * 2,
        1,
        [idx, *sums, dq, w_full],
        name="h_one_grads",
    )
    gh = [term(gh), term(swap_z(gh_other, 1))]
    f_in = reduce_z(order, viewed(f_in, reshaped(2, 2, high_in // TP, 128)), 1)
    f_rest = reduce_step(order, f_rest, "shard", 0)
    wq = gather_z(order, sum_over(order.add(wq), "zo"), 2)

    f_in = reduce_z(order, f_in, 2)
    f_rest = reduce_step(order, f_rest, "x", 0)
    wq = gather_z(order, wq, 1)
    gh = reduce_z(order, gh, 2)

    f_in = gather_z(order, sum_over(order.add(f_in), "zo"), 2)
    f_rest = gather_z(order, sum_over(order.add(f_rest), "zo"), 2)
    wq = pair(wq)

    f_rest = gather_z(order, f_rest, 1)
    f_in = gather_z(order, f_in, 1)
    (grad_tokens,) = order.run(
        functools.partial(tail_kernel, len(gh)),
        [((rows, D), F32)],
        1,
        [idx, *[t[0] for t in gh], tok, grad_middle, gains],
        name="token_grads",
    )
    wq = order.step(wq)
    wq_got = shift(wq, "core", 1)

    f_rest = pair(f_rest)
    f_in = pair(f_in)
    f_rest = order.step(f_rest)
    f_rest_got = shift(f_rest, "core", 1)
    f_in = order.step(f_in)
    f_in_got = shift(f_in, "core", 1)
    g_qkv, grad_gain_one = order.run(
        qkv_unpack_kernel,
        [((2, 2, rows_d, 3 * D), F32), ((part,), F32)],
        1,
        [idx, wq, wq_got],
        scratch=[pltpu.VMEM((part, 128), F32)],
        name="qkv_unpack",
    )
    g_out, g_down, grad_gain_two = order.run(
        functools.partial(rest_unpack_kernel, shards),
        [
            ((2, 2, rows_d, D), F32),
            ((2, 2, rows_f, D), F32),
            ((part,), F32),
        ],
        1,
        [idx, f_rest, f_rest_got],
        scratch=[pltpu.VMEM((high, D), F32)],
        name="w_down_w_out_unpack",
    )
    (g_in,) = order.run(
        functools.partial(in_unpack_kernel, shards),
        [((2, 2, rows_d, 2 * FF), F32)],
        1,
        [idx, f_in, f_in_got],
        scratch=[pltpu.VMEM((high_in, 128), F32)],
        name="w_in_unpack",
    )

    return (
        result[None],
        grad_tokens[None],
        grad_gain_one,
        g_qkv.reshape(part, 3 * D),
        g_out.reshape(part, D),
        grad_gain_two,
        g_in.reshape(part, 2 * FF),
        g_down.reshape(w_down.shape[0], D),
    )


def solution(mesh):
    blocks = mesh.shape["ctx"]
    fine = Mesh(
        mesh.devices.reshape(blocks // (TP * 4), TP, 2, 2, mesh.shape["shard"]), CTX + ("shard",)
    )
    rows, split = P("shard", CTX, None), P("shard", None)
    return jax.shard_map(
        per_device,
        mesh=fine,
        in_specs=(rows, P("shard"), split, split, P("shard"), split, split, rows),
        out_specs=(rows, rows, P("shard"), split, split, P("shard"), split, split),
        check_vma=False,
    )
```

```python
import functools
import math

import jax
import jax.numpy as jnp
from jax import lax
from jax.experimental import pallas as pl
from jax.experimental.pallas import tpu as pltpu
from jax.sharding import Mesh, PartitionSpec as P

D = 768
HEADS = 12
HEAD_DIM = 64
FF = 1152
EPS = 1e-05
THETA = 160000.0

TP = 4
GH = HEADS // TP
GW = GH * HEAD_DIM
WC = 640
CTX = ("zo", "z", "x", "core")
BF = jnp.bfloat16
F32 = jnp.float32
VMEM_LIMIT = 32 * 1024 * 1024

KEY_AT = ((0, 0), (0, 1), (1, 0))
VALUE_AT = ((1, 1), (2, 0), (2, 1))


def dot(a, b):
    return jnp.dot(a, b, preferred_element_type=F32)


def dot_nt(a, b):
    return lax.dot_general(a, b, (((1,), (1,)), ((), ())), preferred_element_type=F32)


def dot_tn(a, b):
    return lax.dot_general(a, b, (((0,), (0,)), ((), ())), preferred_element_type=F32)


def call(body, outs, n_smem, ins, scratch=(), any_ins=(), hbm_ins=(), hbm_outs=(), name=None):
    specs, values = [], []
    for i, value in enumerate(ins):
        space = pltpu.SMEM if i < n_smem else (pl.ANY if i in any_ins else pltpu.VMEM)
        if i in hbm_ins:
            value = pltpu.with_memory_space_constraint(value, pltpu.HBM)
        specs.append(pl.BlockSpec(memory_space=space))
        values.append(value)
    shapes = []
    for i, (shape, kind) in enumerate(outs):
        shapes.append(pltpu.HBM(shape, kind) if i in hbm_outs else jax.ShapeDtypeStruct(shape, kind))
    return pl.pallas_call(
        body,
        out_shape=shapes,
        in_specs=specs,
        out_specs=[pl.BlockSpec(memory_space=pltpu.VMEM)] * len(outs),
        scratch_shapes=list(scratch),
        compiler_params=pltpu.CompilerParams(vmem_limit_bytes=VMEM_LIMIT),
        cost_estimate=pl.CostEstimate(flops=1, bytes_accessed=1, transcendentals=0),
        name=name,
    )(*values)


def normalise(values):
    mean = jnp.mean(values, axis=-1, keepdims=True)
    centred = values - mean
    spread = jnp.mean(centred * centred, axis=-1, keepdims=True)
    scale = lax.rsqrt(spread + EPS)
    return centred * scale, scale


def normalise_back(grad_unit, unit, scale):
    return scale * (
        grad_unit
        - jnp.mean(grad_unit, axis=-1, keepdims=True)
        - unit * jnp.mean(grad_unit * unit, axis=-1, keepdims=True)
    )


def turn(tile, cosine, signed_sine, first_half):
    swapped = jnp.where(first_half, pltpu.roll(tile, 96, 1), pltpu.roll(tile, 32, 1))
    return tile * cosine + swapped * signed_sine


def lane_masks(rows):
    lane = lax.broadcasted_iota(jnp.int32, (rows, 128), 1)
    return lax.rem(lane, 64) < 32, lane < 64


def group_kernel(idx, w_ref, one_ref, two_ref, own_ref, half_ref):
    height = w_ref.shape[0]
    half = height // 2
    for g in range(TP):

        @pl.when(idx[0] == g)
        def _():
            parts = [w_ref[:, p * D + g * GW : p * D + (g + 1) * GW] for p in (1, 2, 0)]
            parts.append(jnp.zeros((height, WC - 3 * GW), BF))
            own_ref[...] = jnp.concatenate(parts, axis=1)

    half_ref[0:half, :] = own_ref[pl.ds(pl.multiple_of(idx[2] * half, half), half), :]
    half_ref[half:, :] = jnp.zeros((16, WC), BF)
    half_ref[half : half + 1, 0:height] = one_ref[...].reshape(1, height)
    half_ref[half + 1 : half + 2, 0:height] = two_ref[...].reshape(1, height)


def pack_kernel(idx, out_ref, in_ref, down_ref, pack_ref, pack_down):
    c = idx[2]
    half = out_ref.shape[0] // 2
    at = pl.ds(pl.multiple_of(c * half, half), half)
    pack_ref[0:half, :] = out_ref[at, :]
    for b in range(3):
        pack_ref[(1 + b) * half : (2 + b) * half, :] = in_ref[at, b * D : (b + 1) * D]
    count, step = down_half(down_ref.shape[0])
    quarter, hop = down_half(count)
    at = pl.multiple_of(c * step + lax.rem(idx[0], 2) * hop, 16)
    pack_down[...] = down_ref[pl.ds(at, quarter), :]


def down_half(height):
    count = -(-height // 32) * 16
    return count, height - count


def front_kernel(shards, idx, *refs):
    toks = refs[:TP]
    n_w = 2 * shards - 1
    ws = refs[TP : TP + n_w]
    mine, cos_ref, sin_ref, q_ref, kv_ref, h_ref, w_ref, gains_ref = refs[TP + n_w :]
    c, y = idx[2], idx[3]
    rows = toks[0].shape[0]
    part = ws[0].shape[0]
    half = part // 2
    gains_ref[...] = jnp.zeros_like(gains_ref)
    for k in range(shards):
        start = lax.rem(y - k + shards, shards) * part
        at = pl.ds(pl.multiple_of(start, part), part)
        if k == 0:
            w_ref[at, :] = ws[0][...]
            continue
        at = pl.ds(pl.multiple_of(start + c * half, half), half)
        w_ref[at, :] = ws[2 * k - 1][0:half]
        at = pl.ds(pl.multiple_of(start + (1 - c) * half, half), half)
        w_ref[at, :] = ws[2 * k][0:half]
    for s in range(shards):

        @pl.when(y == s)
        def _():
            for k in range(shards):
                start = (s - k) % shards * part
                gains = (ws[2 * k - 1] if k else mine)[half : half + 2, 0:part]
                gains_ref[0:2, start : start + part] = gains.astype(F32)

    gain = gains_ref[0:1, :]
    first, low = lane_masks(rows)
    for j in range(TP):
        at = slice(j * rows, (j + 1) * rows)
        unit, _ = normalise(toks[j][...].astype(F32))
        h = (unit * gain).astype(BF)
        h_ref[at, :] = h
        out = dot(h, w_ref[...])
        cosine, sine = cos_ref[at, :], sin_ref[at, :]
        key_a = turn(out[:, 0:128], cosine, sine, first)
        mixed = out[:, 128:256]
        key_b = jnp.where(low, turn(mixed, cosine, sine, first), mixed)
        kv_ref[at, 0:128] = key_a.astype(BF)
        kv_ref[at, 128:256] = key_b.astype(BF)
        kv_ref[at, 256:384] = out[:, 256:384].astype(BF)
        query_a = turn(out[:, 384:512], cosine, sine, first)
        query_b = jnp.where(low, turn(out[:, 512:640], cosine, sine, first), 0.0)
        factor = HEAD_DIM ** (-0.5)
        q_ref[at, 0:128] = (query_a * factor).astype(BF)
        q_ref[at, 128:256] = (query_b * factor).astype(BF)


def half_rows(values_t, head):
    at = head * HEAD_DIM
    rows = values_t[at : at + HEAD_DIM]
    zeros = jnp.zeros_like(rows)
    return jnp.concatenate([rows, zeros] if head % 2 == 0 else [zeros, rows], axis=0)


def forward_kernel(n_kv, last, q_ref, *refs):
    kvs = refs[:n_kv]
    if last:
        before_ref, before_lse = refs[n_kv : n_kv + 2]
        atts = refs[n_kv + 2 : n_kv + 2 + TP]
    att_t_ref, lse_ref, kv_s, v_t, q_t = refs[-5:]
    rows = kvs[0].shape[0]
    block = math.gcd(rows, 256)
    for i, kv in enumerate(kvs):
        kv_s[i * rows : (i + 1) * rows, :] = kv[...]
        v_t[:, i * rows : (i + 1) * rows] = kv[:, 128:384].T
    q_t[...] = q_ref[...].T
    lse_ref[...] = jnp.zeros_like(lse_ref)
    for i in range(rows // block):
        at = slice(i * block, (i + 1) * block)
        for h in range(GH):
            tile = KEY_AT[h][0]
            keys = kv_s[:, tile * 128 : tile * 128 + 128]
            scores = dot(keys, half_rows(q_t[:, at], h))
            top = jnp.max(scores, axis=0, keepdims=True)
            weights = jnp.exp(scores - top)
            total = jnp.sum(weights, axis=0, keepdims=True)
            tile, half = VALUE_AT[h]
            values_t = v_t[(tile - 1) * 128 : tile * 128, :]
            out = dot(values_t, weights.astype(BF))[half * 64 : half * 64 + 64]
            head = slice(h * 64, h * 64 + 64)
            if last:
                old = before_lse[h : h + 1, at]
                high = jnp.maximum(old, top)
                share, own = jnp.exp(old - high), jnp.exp(top - high)
                total = total * own + share
                out = out * own + before_ref[head, at] * share
                top = high
            att_t_ref[head, at] = out / total
            lse_ref[h : h + 1, at] = top + jnp.log(total)
    if last:
        small = rows // TP
        for j in range(TP):
            atts[j][...] = att_t_ref[:, j * small : (j + 1) * small].T.astype(BF)


def backward_kernel(n_kv, q_ref, *refs):
    kvs = refs[:n_kv]
    gas = refs[n_kv : n_kv + TP]
    att_t_ref, lse_ref = refs[n_kv + TP : n_kv + TP + 2]
    tables = refs[n_kv + TP + 2 : n_kv + TP + 4]
    keep_ref, send_ref, dq_ref = refs[n_kv + TP + 4 : n_kv + TP + 7]
    kv_s, k_t, q_t, g_t, q_m, g_m, acc, dq_t = refs[n_kv + TP + 7 :]
    rows = kvs[0].shape[0]
    small = gas[0].shape[0]
    block = math.gcd(rows, 256)
    for i, kv in enumerate(kvs):
        kv_s[i * rows : (i + 1) * rows, :] = kv[...]
        k_t[:, i * rows : (i + 1) * rows] = kv[:, 0:256].T
    q_t[...] = q_ref[...].T
    _, low = lane_masks(small)
    for j in range(TP):
        at = slice(j * small, (j + 1) * small)
        g_t[:, at] = gas[j][...].T
        first, second = gas[j][:, 0:128], gas[j][:, 128:256].astype(F32)
        g_m[at, 0:128] = first
        g_m[at, 128:256] = jnp.where(low, second, 0.0).astype(BF)
        g_m[at, 256:384] = jnp.where(low, 0.0, second).astype(BF)
        both = q_ref[at, 0:128].astype(F32)
        q_m[at, 0:128] = jnp.where(low, both, 0.0).astype(BF)
        q_m[at, 128:256] = jnp.where(low, 0.0, both).astype(BF)
        q_m[at, 256:384] = q_ref[at, 128:256]
    dq_t[...] = jnp.zeros_like(dq_t)
    acc[...] = jnp.zeros_like(acc)
    for i in range(rows // block):
        at = slice(i * block, (i + 1) * block)
        for h in range(GH):
            ktile, khalf = KEY_AT[h]
            vtile = VALUE_AT[h][0]
            klanes = slice(ktile * 128, ktile * 128 + 128)
            vlanes = slice(vtile * 128, vtile * 128 + 128)
            scores = dot(kv_s[:, klanes], half_rows(q_t[:, at], h))
            probs = jnp.exp(scores - lse_ref[h : h + 1, at])
            grad_t = half_rows(g_t[:, at], h + 1)
            grad_probs = dot(kv_s[:, vlanes], grad_t)
            own = g_t[(h + 1) * 64 : (h + 2) * 64, at].astype(F32)
            inner = jnp.sum(
                own * att_t_ref[h * 64 : h * 64 + 64, at], axis=0, keepdims=True
            )
            grad_scores = (probs * (grad_probs - inner)).astype(BF)
            lanes = slice(h * 128, h * 128 + 128)
            acc[:, vlanes] += dot(probs.astype(BF), g_m[at, lanes])
            acc[:, klanes] += dot(grad_scores, q_m[at, lanes])
            part = dot(k_t[klanes, :], grad_scores)[khalf * 64 : khalf * 64 + 64]
            dq_t[h * 64 : h * 64 + 64, at] = part * HEAD_DIM ** (-0.5)
    first, low = lane_masks(rows)
    cosine, sine = tables[0][0:rows, :], -tables[1][0:rows, :]
    grad_q = dq_t[...].T
    for t in range(2):
        lanes = slice(t * 128, t * 128 + 128)
        dq_ref[:, lanes] = turn(grad_q[:, lanes], cosine, sine, first).astype(BF)
    for i in range(n_kv):
        at = slice(i * rows, (i + 1) * rows)
        cosine, sine = tables[0][at, :], -tables[1][at, :]
        target = keep_ref if i < n_kv // 2 else send_ref
        block = i % (n_kv // 2)
        grad = acc[at, 0:128]
        target[block, :, 0:128] = turn(grad, cosine, sine, first).astype(BF)
        grad = acc[at, 128:256]
        grad = jnp.where(low, turn(grad, cosine, sine, first), grad)
        target[block, :, 128:256] = grad.astype(BF)
        target[block, :, 256:384] = acc[at, 256:384].astype(BF)


ACT_H, ACT_MIX, ACT_GU, ACT_GB, ACT_ATT, ACT_COT, ACT_ALL = (
    0, D, D + FF, D + 3 * FF, 2 * D + 3 * FF, 3 * D + 3 * FF, 4 * D + 3 * FF
)


def middle_kernel(n_packs, idx, *refs):
    atts = refs[:TP]
    tok_ref, cot_ref, gains_ref, out_own, in_own, down_own = refs[TP : TP + 6]
    packs = refs[TP + 6 : TP + 6 + n_packs]
    down_packs = refs[TP + 6 + n_packs : TP + 6 + 2 * n_packs]
    rest = refs[TP + 6 + 2 * n_packs :]
    result_ref, gmid_ref, act_ref, gain_ref = rest[:4]
    gatts = rest[4 : 4 + TP]
    w_out, w_in, w_down, sems = rest[4 + TP :]
    half = out_own.shape[0] // 2
    count, step = down_half(down_own.shape[0])

    def rows(start, height):
        return pl.ds(pl.multiple_of(start, 16), height)

    z, c, y = idx[0], idx[2], idx[3]
    shards = n_packs // 2 + 1
    own, own_down = y * 2 * half, y * down_own.shape[0]
    outs = [pltpu.make_async_copy(out_own, w_out.at[rows(own, 2 * half), :], sems.at[0])]
    ins = [pltpu.make_async_copy(in_own, w_in.at[rows(own, 2 * half), :], sems.at[1])]
    target = w_down.at[rows(own_down, down_own.shape[0]), :]
    downs = [pltpu.make_async_copy(down_own, target, sems.at[2])]
    for i, pack in enumerate(packs):
        shard = lax.rem(y - (i // 2 + 1) + shards, shards)
        core = 1 - c if i % 2 else c
        at = rows((shard * 2 + core) * half, half)
        source = pack.at[0:half, :]
        outs.append(pltpu.make_async_copy(source, w_out.at[at, :], sems.at[3 + 6 * i]))
        for b in range(3):
            source = pack.at[(1 + b) * half : (2 + b) * half, :]
            target = w_in.at[at, b * D : (b + 1) * D]
            ins.append(pltpu.make_async_copy(source, target, sems.at[4 + 6 * i + b]))
        quarter, hop = down_half(count)
        for b in range(2):
            parity = lax.rem(z + b, 2)
            at = rows(shard * down_own.shape[0] + core * step + parity * hop, quarter)
            source = down_packs[i].at[b]
            downs.append(pltpu.make_async_copy(source, w_down.at[at, :], sems.at[7 + 6 * i + b]))
    apart = 4 * down_half(count)[0] == down_own.shape[0]
    for copy in outs + ins + (downs if apart else downs[:1]):
        copy.start()
    starts = [pl.multiple_of(lax.rem(z + j, TP) * GW, GW) for j in range(TP)]
    for copy in outs:
        copy.wait()
    middle = tok_ref[...].astype(F32)
    for j in range(TP):
        middle += dot(atts[j][...], w_out[pl.ds(starts[j], GW), :])
        act_ref[:, ACT_ATT + j * GW : ACT_ATT + (j + 1) * GW] = atts[j][...]
    gain = gains_ref[1:2, :]
    unit, scale = normalise(middle)
    h = (unit * gain).astype(BF)
    act_ref[:, ACT_H : ACT_H + D] = h
    for copy in ins:
        copy.wait()
    gate = dot(h, w_in[:, :FF])
    up = dot(h, w_in[:, FF:])
    phi = 0.5 * (1.0 + lax.erf(gate * math.sqrt(0.5)))
    active = gate * phi
    mixed = (active * up).astype(BF)
    act_ref[:, ACT_MIX : ACT_MIX + FF] = mixed
    for i, copy in enumerate(downs):
        if i and not apart:
            copy.start()
        copy.wait()
    grad_mixed = dot_nt(cot_ref[...], w_down[...])
    slope = phi + gate * (jnp.exp(-0.5 * gate * gate) * (1.0 / math.sqrt(2.0 * math.pi)))
    grad_gate = (grad_mixed * up * slope).astype(BF)
    grad_up = (grad_mixed * active).astype(BF)
    act_ref[:, ACT_GU : ACT_GU + FF] = grad_gate
    act_ref[:, ACT_GU + FF : ACT_GU + 2 * FF] = grad_up
    grad_h = dot_nt(grad_gate, w_in[:, :FF]) + dot_nt(grad_up, w_in[:, FF:])
    gain_ref[...] = jnp.broadcast_to(
        jnp.sum(grad_h * unit, axis=0, keepdims=True), gain_ref.shape
    )
    grad_middle = cot_ref[...].astype(F32) + normalise_back(grad_h * gain, unit, scale)
    gmid_ref[...] = grad_middle
    gb = grad_middle.astype(BF)
    act_ref[:, ACT_GB : ACT_GB + D] = gb
    act_ref[:, ACT_COT : ACT_COT + D] = cot_ref[...]
    for j in range(TP):
        part = dot_nt(gb, w_out[pl.ds(starts[j], GW), :])
        pad = jnp.zeros((part.shape[0], 256 - GW), F32)
        gatts[j][...] = jnp.concatenate([pad, part], axis=1).astype(BF)
    result_ref[...] = middle + dot(mixed, w_down[...])


def up16(n):
    return -(-n // 16) * 16


def plan(shards):
    rows_d, rows_f = D // (4 * shards), FF // (4 * shards)
    return rows_d, rows_f, up16(rows_d), up16(rows_f)


def ffn_grads_kernel(shards, idx, own, got, gain_ref, *refs):
    ins = refs[:shards]
    mine_ref, other_ref = refs[shards : shards + 2]
    h_t, mixed_t, att_t, right = refs[shards + 2 :]
    z, x, c, y = idx[0], idx[1], idx[2], idx[3]
    rows_d, rows_f, pad_d, pad_f = plan(shards)
    n = own.shape[0]
    pieces, per = 4 * shards, GW // rows_d
    for i, act in enumerate((own, got)):
        at = slice(i * n, (i + 1) * n)
        h = act[:, ACT_H : ACT_H + D].T
        mixed = act[:, ACT_MIX : ACT_MIX + FF].T
        att = act[:, ACT_ATT : ACT_ATT + D].T
        for m in range(pieces):
            h_t[m, 0:rows_d, at] = h[m * rows_d : (m + 1) * rows_d]
            mixed_t[m, 0:rows_f, at] = mixed[m * rows_f : (m + 1) * rows_f]
            att_t[m, 0:rows_d, at] = att[m * rows_d : (m + 1) * rows_d]
        right[at, 0 : 2 * FF] = act[:, ACT_GU : ACT_GU + 2 * FF]
        right[at, 2 * FF : 2 * FF + D] = act[:, ACT_GB : ACT_GB + D]
        right[at, 2 * FF + D :] = act[:, ACT_COT : ACT_COT + D]
    for k in range(shards):
        piece = (lax.rem(y + k, shards) * 2 + c) * 2
        left = h_t[pl.ds(piece, 2)].reshape(2 * pad_d, 2 * n)
        grad = dot(left, right[:, 0 : 2 * FF]).astype(BF)
        for xx in range(2):
            for t in range(2 * FF // 128):
                ins[k][xx, t * pad_d : t * pad_d + rows_d, :] = grad[
                    xx * pad_d : xx * pad_d + rows_d, t * 128 : t * 128 + 128
                ]
    high = mine_ref.shape[1]
    gain = jnp.broadcast_to(gain_ref[0:1, :], (high - pad_f - pad_d, D)).astype(BF)
    for xx in range(2):
        for s in range(shards):
            piece = (s * 2 + c) * 2 + xx
            turned = lax.rem(piece // per - z + TP, TP) * per + lax.rem(piece, per)
            down = dot(mixed_t[piece], right[:, 2 * FF + D :]).astype(BF)
            out = dot(att_t[turned], right[:, 2 * FF : 2 * FF + D]).astype(BF)
            both = jnp.concatenate([down, out, gain], axis=0)

            @pl.when(x == xx)
            def _():
                mine_ref[s] = both

            @pl.when(x != xx)
            def _():
                other_ref[s] = both


def qkv_grads_kernel(shards, n_kv, idx, *refs):
    hs = refs[:n_kv]
    keep_ref, send_ref, dq_ref, w_ref, gains_ref, mine_ref, other_ref = refs[n_kv:]
    c = idx[2]
    total = None
    for i in range(n_kv):
        grads = (keep_ref if i < n_kv // 2 else send_ref)[i % (n_kv // 2)]
        part = dot(grads.T, hs[i][...])
        total = part if total is None else total + part
    grad = jnp.concatenate([total, dot(dq_ref[...].T, hs[0][...])], axis=0).T
    gain = gains_ref[...].T[:, 0:1]
    lane = lax.broadcasted_iota(jnp.int32, grad.shape, 1)
    by_gain = jnp.sum(grad * w_ref[...].astype(F32), axis=1, keepdims=True) / gain
    grad = jnp.where(lane < 3 * GW, grad, by_gain).astype(BF)
    height = plan(shards)[0]
    for s in range(shards):
        for cc in range(2):
            block = (s * 2 + cc) * 2 * height
            for xx in range(2):
                part = grad[block + xx * height : block + (xx + 1) * height]

                @pl.when(c == cc)
                def _():
                    mine_ref[s, xx] = part

                @pl.when(c != cc)
                def _():
                    other_ref[s, xx] = part


def h_one_grads_kernel(n_sum, idx, *refs):
    parts = refs[:n_sum]
    dq_ref, w_ref, gh_mine, gh_other = refs[n_sum:]
    rows = gh_mine.shape[1]
    for j in range(TP):
        at = slice(j * rows, (j + 1) * rows)
        total = parts[0][0, at, :].astype(F32)
        for part in parts[1:]:
            total += part[0, at, :].astype(F32)
        grad = jnp.concatenate([total.astype(BF), dq_ref[at, :]], axis=1)
        owner = lax.rem(idx[0] - j + TP, TP)
        target = gh_other if j % 2 else gh_mine
        target[owner // 2] = dot_nt(grad, w_ref[...]).astype(BF)


def tail_kernel(n_sum, idx, *refs):
    tok_ref, gmid_ref, gains_ref, out_ref = refs[n_sum:]
    unit, scale = normalise(tok_ref[...].astype(F32))
    total = 0.0
    for grad in refs[:n_sum]:
        grad = grad[idx[0] // 2] if len(grad.shape) == 3 else grad[...]
        total += grad.astype(F32)
    grad_unit = total * gains_ref[0:1, :]
    out_ref[...] = gmid_ref[...] + normalise_back(grad_unit, unit, scale)


def place_z(z, k):
    return lax.rem(z // 2 + k % 2, 2) * 2 + lax.rem(lax.rem(z, 2) + k // 2, 2)


def in_unpack_kernel(shards, idx, own, got, in_ref, held):
    rows_d, _, pad_d, _ = plan(shards)
    size = held.shape[0] // TP
    z, x, c = idx[0], idx[1], idx[2]
    for cr in range(2):
        for xr in range(2):
            for k in range(TP):
                at = pl.ds(pl.multiple_of(place_z(z, k) * size, size), size)
                held[at, :] = (got if cr else own)[xr, k].astype(F32)
            cc, xx = lax.rem(c + cr, 2), lax.rem(x + xr, 2)
            for t in range(2 * FF // 128):
                base = t * pad_d
                in_ref[cc, xx, :, t * 128 : t * 128 + 128] = held[base : base + rows_d, :]


def rest_unpack_kernel(shards, idx, own, got, out_ref, down_ref, gain_ref, held):
    rows_d, rows_f, pad_d, pad_f = plan(shards)
    size = held.shape[0] // TP
    z, x, c = idx[0], idx[1], idx[2]
    gain = None
    for cr in range(2):
        for xr in range(2):
            for k in range(TP):
                at = pl.ds(pl.multiple_of(place_z(z, k) * size, size), size)
                held[at, :] = (got if cr else own)[xr, k].astype(F32)
            cc, xx = lax.rem(c + cr, 2), lax.rem(x + xr, 2)
            down_ref[cc, xx] = held[0:rows_f, :]
            out_ref[cc, xx] = held[pad_f : pad_f + rows_d, :]
            if xr == 0:
                row = held[pad_f + pad_d : pad_f + pad_d + 8, :]
                gain = row if gain is None else gain + row
    part = gain_ref.shape[0]
    for s in range(shards):

        @pl.when(idx[3] == s)
        def _():
            gain_ref[...] = gain[0:1, s * part : (s + 1) * part].reshape(part)


def qkv_unpack_kernel(idx, own, got, out_ref, gain_ref, gain_s):
    z, x, c = idx[0], idx[1], idx[2]
    for cr in range(2):
        for xr in range(2):
            cc, xx = lax.rem(c + cr, 2), lax.rem(x + xr, 2)
            gain = None
            for g in range(TP):
                k = 2 * lax.rem(g % 2 + z, 2) + lax.rem(g // 2 + z // 2, 2)
                block = (got if cr else own)[xr, k].astype(F32)
                for source, place in ((0, 1), (1, 2), (2, 0)):
                    out_ref[cc, xx, :, place * D + g * GW : place * D + (g + 1) * GW] = block[
                        :, source * GW : (source + 1) * GW
                    ]
                tail = block[:, 512:640]
                gain = tail if gain is None else gain + tail
            height = gain.shape[0]
            at = pl.multiple_of((cc * 2 + xx) * height, height)
            gain_s[pl.ds(at, height), :] = gain
    gain_ref[...] = gain_s[...].T[64:65].reshape(gain_ref.shape)


def shift(value, axis, k):
    n = lax.axis_size(axis)
    return lax.ppermute(value, axis, [(i, (i + k) % n) for i in range(n)])


def gather(value, axis):
    return [value] + [shift(value, axis, k) for k in range(1, lax.axis_size(axis))]


def pick(value, index, dim):
    return lax.dynamic_index_in_dim(value, index, dim, keepdims=False)


def term(value, *views):
    return (value, views)


def take(index, dim):
    return lambda value: pick(value, index, dim)


def reshaped(*shape):
    return lambda value: value.reshape(shape)


def viewed(terms, view):
    return [(value, views + (view,)) for value, views in terms]


def reduce_step(order, terms, axis, dim):
    n, i = lax.axis_size(axis), lax.axis_index(axis)
    total = order.add(terms)
    got = [term(shift(pick(total, lax.rem(i + k, n), dim), axis, k)) for k in range(1, n)]
    return [term(pick(total, i, dim))] + got


def add(values):
    total = values[0].astype(F32)
    for value in values[1:]:
        total = total + value.astype(F32)
    return total.astype(BF)


def swap_z(value, bit):
    return lax.ppermute(value, "z", [(i, i ^ bit) for i in range(TP)])


def reduce_z(order, terms, bit):
    z = lax.axis_index("z")
    i, dim = (z % 2, 1) if bit == 1 else (z // 2, 0)
    total = order.add(terms)
    return [term(pick(total, i, dim)), term(swap_z(pick(total, 1 - i, dim), bit))]


def gather_z(order, value, bit):
    value = order.step(value)
    got = swap_z(value, bit)
    return jnp.stack([value, got]) if bit == 2 else jnp.concatenate([value, got])


def sum_over(value, axis):
    return add([value] + [shift(value, axis, k) for k in range(1, lax.axis_size(axis))])


def after(value, *others):
    return lax.optimization_barrier((value, *others))[0]


class Order:
    def __init__(self):
        self.last = None

    def __call__(self, values):
        if self.last is None:
            return values
        return lax.optimization_barrier((values, self.last))[0]

    def step(self, value):
        self.last = self(value)
        return self.last

    def add(self, terms):
        values = []
        for value, (_, views) in zip(self([t[0] for t in terms]), terms):
            for view in views:
                value = view(value)
            values.append(value)
        self.last = add(values)
        return self.last

    def run(self, body, outs, n_smem, ins, **more):
        got = call(body, outs, n_smem, self(list(ins)), **more)
        self.last = got[0]
        return got


def per_device(tokens, gain_one, w_qkv, w_out, gain_two, w_in, w_down, cotangent):
    tok, cot = tokens[0], cotangent[0]
    rows = tok.shape[0]
    many = TP * rows
    zo, z = lax.axis_index("zo"), lax.axis_index("z")
    x, c, y = lax.axis_index("x"), lax.axis_index("core"), lax.axis_index("shard")
    outer, shards = lax.axis_size("zo"), lax.axis_size("shard")
    part = w_qkv.shape[0]
    n_kv = 4 * outer
    keys = n_kv * many
    rows_d, rows_f, pad_d, pad_f = plan(shards)
    high_in, high = 2 * FF // 128 * pad_d, -(-(pad_f + pad_d + 16) // 64) * 64
    i32 = jnp.int32
    idx = jnp.stack([z, x, c, y]).astype(i32)
    order = Order()

    toks = gather(tok, "z")
    w_own, w_mine = order.run(
        group_kernel,
        [((part, WC), BF), ((part // 2 + 16, WC), BF)],
        1,
        [idx, w_qkv, gain_one, gain_two],
        hbm_ins=(1, 2, 3),
        name="group_columns",
    )
    w_slices = [w_own]
    for k in range(1, shards):
        w_slices.append(shift(w_mine, "shard", k))
        w_slices.append(shift(w_slices[-1], "core", 1))
    pack, pack_down = order.run(
        pack_kernel,
        [((2 * part, D), BF), ((down_half(down_half(w_down.shape[0])[0])[0], D), BF)],
        1,
        [idx, w_out, w_in, w_down],
        hbm_ins=(1, 2, 3),
        name="pack_weights",
    )
    downs = [shift(pack_down, "shard", k) for k in range(1, shards)]
    packs = [shift(pack, "shard", k) for k in range(1, shards)]

    freq = THETA ** (-jnp.arange(HEAD_DIM // 2, dtype=F32) * (2.0 / HEAD_DIM))
    owners = lax.rem(z - jnp.arange(TP, dtype=i32) + TP, TP)
    places = []
    for cr in range(2):
        for xr in range(2):
            for zr in range(outer):
                zz = lax.rem(zo - zr + outer, outer)
                place = ((zz * TP + owners) * 2 + lax.rem(x + xr, 2)) * 2 + lax.rem(c + cr, 2)
                places.append(place)
    first_place = jnp.concatenate(places) * rows
    freq = jnp.tile(freq, 4)[None, :]
    sign = jnp.where(jnp.arange(128) % 64 < 32, -1.0, 1.0).astype(F32)
    start = first_place.astype(F32)[:, None] * freq
    step = jnp.arange(rows, dtype=i32).astype(F32)[:, None] * freq
    cos_a, sin_a = jnp.cos(start)[:, None], jnp.sin(start)[:, None]
    cos_b, sin_b = jnp.cos(step)[None], jnp.sin(step)[None]
    cosine = (cos_a * cos_b - sin_a * sin_b).reshape(keys, 128)
    sine = ((sin_a * cos_b + cos_a * sin_b) * sign).reshape(keys, 128)

    query, kv, h_one, w_full, gains = order.run(
        functools.partial(front_kernel, shards),
        [
            ((many, 256), BF),
            ((many, 2 * GW), BF),
            ((many, D), BF),
            ((D, WC), BF),
            ((8, D), F32),
        ],
        1,
        [idx, *toks, *w_slices, w_mine, cosine, sine],
        hbm_ins=range(1, 1 + TP + len(w_slices) + 3),
        hbm_outs=(2, 3, 4),
        name="front",
    )

    near = gather(kv, "zo")
    near = near + [shift(v, "x", 1) for v in near]
    kv_core = shift(kv, "core", 1)
    close = (0, n_kv // 2)
    far = [i for i in range(n_kv) if i not in close]
    scratch = lambda count: [
        pltpu.VMEM((count * many, 2 * GW), BF),
        pltpu.VMEM((256, count * many), BF),
        pltpu.VMEM((256, many), BF),
    ]
    first = order.run(
        functools.partial(forward_kernel, 2, False),
        [((GW, many), F32), ((8, many), F32)],
        0,
        [query, kv, kv_core],
        scratch=scratch(2),
        name="attention_forward_near",
    )
    kvs = near + [kv_core] + [shift(after(v, *first), "core", 1) for v in near[1:]]
    downs = [jnp.stack([v, swap_z(v, 1)]) for v in downs]
    both_down = [v for p in downs for v in (p, shift(p, "core", 1))]
    first = [first[0], after(first[1], *both_down)]
    att = order.run(
        functools.partial(forward_kernel, len(far), True),
        [((rows, GW), BF)] * TP + [((GW, many), F32), ((8, many), F32)],
        0,
        [query, *[kvs[i] for i in far], *first],
        scratch=scratch(len(far)),
        hbm_outs=(TP, TP + 1),
        name="attention_forward_far",
    )
    att_blocks, (attended_t, lse) = att[:TP], att[TP:]
    h_near = gather(after(h_one, lse), "zo")
    h_near = h_near + [shift(v, "x", 1) for v in h_near]
    h_core = shift(after(h_one, lse), "core", 1)
    atts = [att_blocks[0]] + [shift(att_blocks[k], "z", -k) for k in range(1, TP)]

    packs = [after(p, lse) for p in packs]
    both = [v for p in packs for v in (p, shift(p, "core", 1))]
    mid = order.run(
        functools.partial(middle_kernel, len(both)),
        [((rows, D), F32), ((rows, D), F32), ((rows, ACT_ALL), BF), ((8, D), F32)]
        + [((rows, 256), BF)] * TP,
        1,
        [idx, *atts, tok, cot, after(gains, h_core), w_out, w_in, w_down, *both, *both_down],
        scratch=[
            pltpu.VMEM((D, D), BF),
            pltpu.VMEM((D, 2 * FF), BF),
            pltpu.VMEM((FF, D), BF),
            pltpu.SemaphoreType.DMA((3 + 6 * len(both),)),
        ],
        any_ins=range(1 + TP + 3, 1 + TP + 6 + 2 * len(both)),
        hbm_ins=(1 + TP, 2 + TP, 3 + TP),
        hbm_outs=(0, 1, 3),
        name="feed_forward",
    )
    result, grad_middle, act, gain_two_row = mid[:4]
    act = after(act, *h_near)
    gatts = mid[4:]
    gas = [gatts[0]] + [shift(gatts[k], "z", k) for k in range(1, TP)]

    hs = h_near + [h_core] + [shift(after(v, result), "core", 1) for v in h_near[1:]]
    gain_two_row = after(gain_two_row, *hs)
    ffn = order.run(
        functools.partial(ffn_grads_kernel, shards),
        [((2, high_in, 128), BF)] * shards
        + [((shards, high, D), BF)] * 2,
        1,
        [idx, act, shift(act, "core", 1), gain_two_row],
        scratch=[
            pltpu.VMEM((4 * shards, pad_d, 2 * rows), BF),
            pltpu.VMEM((4 * shards, pad_f, 2 * rows), BF),
            pltpu.VMEM((4 * shards, pad_d, 2 * rows), BF),
            pltpu.VMEM((2 * rows, 2 * FF + 2 * D), BF),
        ],
        hbm_outs=range(shards + 2),
        name="ffn_weight_grads",
    )
    f_in = [term(ffn[0])]
    f_in += [term(shift(after(ffn[k], *gas), "shard", k)) for k in range(1, shards)]
    f_rest = [term(ffn[shards]), term(shift(after(ffn[shards + 1], *gas), "x", 1))]

    dkv_keep, dkv_send, dq = order.run(
        functools.partial(backward_kernel, n_kv),
        [((n_kv // 2, many, 2 * GW), BF)] * 2 + [((many, 256), BF)],
        0,
        [query, *kvs, *gas, attended_t, lse, cosine, sine],
        scratch=[
            pltpu.VMEM((keys, 2 * GW), BF),
            pltpu.VMEM((256, keys), BF),
            pltpu.VMEM((256, many), BF),
            pltpu.VMEM((256, many), BF),
            pltpu.VMEM((many, 2 * GW), BF),
            pltpu.VMEM((many, 2 * GW), BF),
            pltpu.VMEM((keys, 2 * GW), F32),
            pltpu.VMEM((256, many), F32),
        ],
        hbm_ins=range(0, 1 + n_kv + TP + 4),
        name="attention_backward",
    )
    mine, other = order.run(
        functools.partial(qkv_grads_kernel, shards, n_kv),
        [((shards, 2, rows_d, WC), BF)] * 2,
        1,
        [idx, *hs, dkv_keep, dkv_send, dq, w_full, gains],
        hbm_ins=range(1, 1 + n_kv),
        name="qkv_weight_grads",
    )
    first_got = [t[0] for t in f_in[1:] + f_rest[1:]]
    mine, other, *_ = lax.optimization_barrier((mine, other, *first_got))
    order.last = mine
    terms = [term(dkv_keep), term(shift(after(dkv_send, mine), "core", 1))]
    terms = viewed(terms, reshaped(2, outer, many, 2 * GW))
    wq = [term(mine), term(shift(other, "core", 1))]

    def pair(value):
        return jnp.stack([value, shift(order.step(value), "x", 1)])

    f_in = reduce_step(order, f_in, "x", 0)
    f_rest = reduce_step(order, f_rest, "shard", 0)
    wq = reduce_step(order, wq, "shard", 0)
    f_in = reduce_z(order, viewed(f_in, reshaped(2, 2, high_in // TP, 128)), 1)
    f_rest = reduce_z(order, viewed(f_rest, reshaped(2, 2, high // TP, D)), 1)
    got = shift(order.add(viewed(terms, take(1, 0))), "x", 1)
    terms = viewed(terms, take(0, 0)) + [term(got)]
    wq = reduce_step(order, wq, "x", 0)
    f_in = reduce_z(order, f_in, 2)
    f_rest = reduce_z(order, f_rest, 2)
    wq = gather_z(order, sum_over(order.add(wq), "zo"), 2)
    f_in = gather_z(order, sum_over(order.add(f_in), "zo"), 2)
    f_rest = gather_z(order, sum_over(order.add(f_rest), "zo"), 2)

    if outer > 1:
        total = order.add(terms)
        sums = [total[0:1]] + [shift(total[k : k + 1], "zo", -k) for k in range(1, outer)]
    else:
        sums = [
            dkv_keep.reshape(2, many, 2 * GW),
            terms[1][0].reshape(2, many, 2 * GW),
            got.reshape(1, many, 2 * GW),
        ]
    gh, gh_other = order.run(
        functools.partial(h_one_grads_kernel, len(sums)),
        [((2, rows, D), BF)] * 2,
        1,
        [idx, *sums, dq, w_full],
        name="h_one_grads",
    )
    wq = gather_z(order, wq, 1)
    f_in = gather_z(order, f_in, 1)
    f_rest = gather_z(order, f_rest, 1)
    wq = pair(wq)
    f_in = pair(f_in)
    gh = [term(gh), term(swap_z(order(gh_other), 1))]
    wq = order.step(wq)
    wq_got = shift(wq, "core", 1)
    f_rest = pair(f_rest)
    g_qkv, grad_gain_one = order.run(
        qkv_unpack_kernel,
        [((2, 2, rows_d, 3 * D), F32), ((part,), F32)],
        1,
        [idx, wq, wq_got],
        scratch=[pltpu.VMEM((part, 128), F32)],
        name="qkv_unpack",
    )
    gh = reduce_z(order, gh, 2)
    f_in = order.step(f_in)
    f_in_got = shift(f_in, "core", 1)
    f_rest = order.step(f_rest)
    f_rest_got = shift(f_rest, "core", 1)
    (g_in,) = order.run(
        functools.partial(in_unpack_kernel, shards),
        [((2, 2, rows_d, 2 * FF), F32)],
        1,
        [idx, f_in, f_in_got],
        scratch=[pltpu.VMEM((high_in, 128), F32)],
        name="w_in_unpack",
    )
    g_out, g_down, grad_gain_two = order.run(
        functools.partial(rest_unpack_kernel, shards),
        [
            ((2, 2, rows_d, D), F32),
            ((2, 2, rows_f, D), F32),
            ((part,), F32),
        ],
        1,
        [idx, f_rest, f_rest_got],
        scratch=[pltpu.VMEM((high, D), F32)],
        name="w_down_w_out_unpack",
    )
    (grad_tokens,) = order.run(
        functools.partial(tail_kernel, len(gh)),
        [((rows, D), F32)],
        1,
        [idx, *[t[0] for t in gh], tok, grad_middle, gains],
        name="token_grads",
    )

    return (
        result[None],
        grad_tokens[None],
        grad_gain_one,
        g_qkv.reshape(part, 3 * D),
        g_out.reshape(part, D),
        grad_gain_two,
        g_in.reshape(part, 2 * FF),
        g_down.reshape(w_down.shape[0], D),
    )


def solution(mesh):
    blocks = mesh.shape["ctx"]
    fine = Mesh(
        mesh.devices.reshape(blocks // (TP * 4), TP, 2, 2, mesh.shape["shard"]), CTX + ("shard",)
    )
    rows, split = P("shard", CTX, None), P("shard", None)
    return jax.shard_map(
        per_device,
        mesh=fine,
        in_specs=(rows, P("shard"), split, split, P("shard"), split, split, rows),
        out_specs=(rows, rows, P("shard"), split, split, P("shard"), split, split),
        check_vma=False,
    )
```

```python
import functools
import math

import jax
import jax.numpy as jnp
from jax import lax
from jax.experimental import pallas as pl
from jax.experimental.pallas import tpu as pltpu
from jax.sharding import Mesh, PartitionSpec as P

D = 768
HEADS = 12
HEAD_DIM = 64
FF = 1152
EPS = 1e-05
THETA = 160000.0

TP = 4
GH = HEADS // TP
GW = GH * HEAD_DIM
WC = 640
CTX = ("zo", "z", "x", "core")
BF = jnp.bfloat16
F32 = jnp.float32
VMEM_LIMIT = 32 * 1024 * 1024

KEY_AT = ((0, 0), (0, 1), (1, 0))
VALUE_AT = ((1, 1), (2, 0), (2, 1))


def dot(a, b):
    return jnp.dot(a, b, preferred_element_type=F32)


def dot_nt(a, b):
    return lax.dot_general(a, b, (((1,), (1,)), ((), ())), preferred_element_type=F32)


def dot_tn(a, b):
    return lax.dot_general(a, b, (((0,), (0,)), ((), ())), preferred_element_type=F32)


def call(body, outs, n_smem, ins, scratch=(), any_ins=(), hbm_ins=(), hbm_outs=(), name=None):
    specs, values = [], []
    for i, value in enumerate(ins):
        space = pltpu.SMEM if i < n_smem else (pl.ANY if i in any_ins else pltpu.VMEM)
        if i in hbm_ins:
            value = pltpu.with_memory_space_constraint(value, pltpu.HBM)
        specs.append(pl.BlockSpec(memory_space=space))
        values.append(value)
    shapes = []
    for i, (shape, kind) in enumerate(outs):
        shapes.append(pltpu.HBM(shape, kind) if i in hbm_outs else jax.ShapeDtypeStruct(shape, kind))
    return pl.pallas_call(
        body,
        out_shape=shapes,
        in_specs=specs,
        out_specs=[pl.BlockSpec(memory_space=pltpu.VMEM)] * len(outs),
        scratch_shapes=list(scratch),
        compiler_params=pltpu.CompilerParams(vmem_limit_bytes=VMEM_LIMIT),
        cost_estimate=pl.CostEstimate(flops=1, bytes_accessed=1, transcendentals=0),
        name=name,
    )(*values)


def normalise(values):
    mean = jnp.mean(values, axis=-1, keepdims=True)
    centred = values - mean
    spread = jnp.mean(centred * centred, axis=-1, keepdims=True)
    scale = lax.rsqrt(spread + EPS)
    return centred * scale, scale


def normalise_back(grad_unit, unit, scale):
    return scale * (
        grad_unit
        - jnp.mean(grad_unit, axis=-1, keepdims=True)
        - unit * jnp.mean(grad_unit * unit, axis=-1, keepdims=True)
    )


def turn(tile, cosine, signed_sine, first_half):
    swapped = jnp.where(first_half, pltpu.roll(tile, 96, 1), pltpu.roll(tile, 32, 1))
    return tile * cosine + swapped * signed_sine


def lane_masks(rows):
    lane = lax.broadcasted_iota(jnp.int32, (rows, 128), 1)
    return lax.rem(lane, 64) < 32, lane < 64


def group_kernel(idx, w_ref, one_ref, two_ref, own_ref, half_ref):
    height = w_ref.shape[0]
    half = height // 2
    for g in range(TP):

        @pl.when(idx[0] == g)
        def _():
            parts = [w_ref[:, p * D + g * GW : p * D + (g + 1) * GW] for p in (1, 2, 0)]
            parts.append(jnp.zeros((height, WC - 3 * GW), BF))
            own_ref[...] = jnp.concatenate(parts, axis=1)

    half_ref[0:half, :] = own_ref[pl.ds(pl.multiple_of(idx[2] * half, half), half), :]
    half_ref[half:, :] = jnp.zeros((16, WC), BF)
    half_ref[half : half + 1, 0:height] = one_ref[...].reshape(1, height)
    half_ref[half + 1 : half + 2, 0:height] = two_ref[...].reshape(1, height)


def pack_kernel(idx, out_ref, in_ref, down_ref, pack_ref, pack_down):
    c = idx[2]
    half = out_ref.shape[0] // 2
    at = pl.ds(pl.multiple_of(c * half, half), half)
    pack_ref[0:half, :] = out_ref[at, :]
    for b in range(3):
        pack_ref[(1 + b) * half : (2 + b) * half, :] = in_ref[at, b * D : (b + 1) * D]
    count, step = down_half(down_ref.shape[0])
    quarter, hop = down_half(count)
    at = pl.multiple_of(c * step + lax.rem(idx[0], 2) * hop, 16)
    pack_down[...] = down_ref[pl.ds(at, quarter), :]


def down_half(height):
    count = -(-height // 32) * 16
    return count, height - count


def front_kernel(shards, idx, *refs):
    toks = refs[:TP]
    n_w = 2 * shards - 1
    ws = refs[TP : TP + n_w]
    mine, cos_ref, sin_ref, q_ref, kv_ref, h_ref, w_ref, gains_ref = refs[TP + n_w :]
    c, y = idx[2], idx[3]
    rows = toks[0].shape[0]
    part = ws[0].shape[0]
    half = part // 2
    gains_ref[...] = jnp.zeros_like(gains_ref)
    for k in range(shards):
        start = lax.rem(y - k + shards, shards) * part
        at = pl.ds(pl.multiple_of(start, part), part)
        if k == 0:
            w_ref[at, :] = ws[0][...]
            continue
        at = pl.ds(pl.multiple_of(start + c * half, half), half)
        w_ref[at, :] = ws[2 * k - 1][0:half]
        at = pl.ds(pl.multiple_of(start + (1 - c) * half, half), half)
        w_ref[at, :] = ws[2 * k][0:half]
    for s in range(shards):

        @pl.when(y == s)
        def _():
            for k in range(shards):
                start = (s - k) % shards * part
                gains = (ws[2 * k - 1] if k else mine)[half : half + 2, 0:part]
                gains_ref[0:2, start : start + part] = gains.astype(F32)

    gain = gains_ref[0:1, :]
    first, low = lane_masks(rows)
    for j in range(TP):
        at = slice(j * rows, (j + 1) * rows)
        unit, _ = normalise(toks[j][...].astype(F32))
        h = (unit * gain).astype(BF)
        h_ref[at, :] = h
        out = dot(h, w_ref[...])
        cosine, sine = cos_ref[at, :], sin_ref[at, :]
        key_a = turn(out[:, 0:128], cosine, sine, first)
        mixed = out[:, 128:256]
        key_b = jnp.where(low, turn(mixed, cosine, sine, first), mixed)
        kv_ref[at, 0:128] = key_a.astype(BF)
        kv_ref[at, 128:256] = key_b.astype(BF)
        kv_ref[at, 256:384] = out[:, 256:384].astype(BF)
        query_a = turn(out[:, 384:512], cosine, sine, first)
        query_b = jnp.where(low, turn(out[:, 512:640], cosine, sine, first), 0.0)
        factor = HEAD_DIM ** (-0.5)
        q_ref[at, 0:128] = (query_a * factor).astype(BF)
        q_ref[at, 128:256] = (query_b * factor).astype(BF)


def half_rows(values_t, head):
    at = head * HEAD_DIM
    rows = values_t[at : at + HEAD_DIM]
    zeros = jnp.zeros_like(rows)
    return jnp.concatenate([rows, zeros] if head % 2 == 0 else [zeros, rows], axis=0)


def forward_kernel(n_kv, last, q_ref, *refs):
    kvs = refs[:n_kv]
    if last:
        before_ref, before_lse = refs[n_kv : n_kv + 2]
        atts = refs[n_kv + 2 : n_kv + 2 + TP]
    att_t_ref, lse_ref, kv_s, v_t, q_t = refs[-5:]
    rows = kvs[0].shape[0]
    block = math.gcd(rows, 256)
    for i, kv in enumerate(kvs):
        kv_s[i * rows : (i + 1) * rows, :] = kv[...]
        v_t[:, i * rows : (i + 1) * rows] = kv[:, 128:384].T
    q_t[...] = q_ref[...].T
    lse_ref[...] = jnp.zeros_like(lse_ref)
    for i in range(rows // block):
        at = slice(i * block, (i + 1) * block)
        for h in range(GH):
            tile = KEY_AT[h][0]
            keys = kv_s[:, tile * 128 : tile * 128 + 128]
            scores = dot(keys, half_rows(q_t[:, at], h))
            top = jnp.max(scores, axis=0, keepdims=True)
            weights = jnp.exp(scores - top)
            total = jnp.sum(weights, axis=0, keepdims=True)
            tile, half = VALUE_AT[h]
            values_t = v_t[(tile - 1) * 128 : tile * 128, :]
            out = dot(values_t, weights.astype(BF))[half * 64 : half * 64 + 64]
            head = slice(h * 64, h * 64 + 64)
            if last:
                old = before_lse[h : h + 1, at]
                high = jnp.maximum(old, top)
                share, own = jnp.exp(old - high), jnp.exp(top - high)
                total = total * own + share
                out = out * own + before_ref[head, at] * share
                top = high
            att_t_ref[head, at] = out / total
            lse_ref[h : h + 1, at] = top + jnp.log(total)
    if last:
        small = rows // TP
        for j in range(TP):
            atts[j][...] = att_t_ref[:, j * small : (j + 1) * small].T.astype(BF)


def backward_kernel(n_kv, q_ref, *refs):
    kvs = refs[:n_kv]
    gas = refs[n_kv : n_kv + TP]
    att_t_ref, lse_ref = refs[n_kv + TP : n_kv + TP + 2]
    tables = refs[n_kv + TP + 2 : n_kv + TP + 4]
    keep_ref, send_ref, dq_ref = refs[n_kv + TP + 4 : n_kv + TP + 7]
    kv_s, k_t, q_t, g_t, q_m, g_m, acc, dq_t = refs[n_kv + TP + 7 :]
    rows = kvs[0].shape[0]
    small = gas[0].shape[0]
    block = math.gcd(rows, 256)
    for i, kv in enumerate(kvs):
        kv_s[i * rows : (i + 1) * rows, :] = kv[...]
        k_t[:, i * rows : (i + 1) * rows] = kv[:, 0:256].T
    q_t[...] = q_ref[...].T
    _, low = lane_masks(small)
    for j in range(TP):
        at = slice(j * small, (j + 1) * small)
        g_t[:, at] = gas[j][...].T
        first, second = gas[j][:, 0:128], gas[j][:, 128:256].astype(F32)
        g_m[at, 0:128] = first
        g_m[at, 128:256] = jnp.where(low, second, 0.0).astype(BF)
        g_m[at, 256:384] = jnp.where(low, 0.0, second).astype(BF)
        both = q_ref[at, 0:128].astype(F32)
        q_m[at, 0:128] = jnp.where(low, both, 0.0).astype(BF)
        q_m[at, 128:256] = jnp.where(low, 0.0, both).astype(BF)
        q_m[at, 256:384] = q_ref[at, 128:256]
    dq_t[...] = jnp.zeros_like(dq_t)
    acc[...] = jnp.zeros_like(acc)
    for i in range(rows // block):
        at = slice(i * block, (i + 1) * block)
        for h in range(GH):
            ktile, khalf = KEY_AT[h]
            vtile = VALUE_AT[h][0]
            klanes = slice(ktile * 128, ktile * 128 + 128)
            vlanes = slice(vtile * 128, vtile * 128 + 128)
            scores = dot(kv_s[:, klanes], half_rows(q_t[:, at], h))
            probs = jnp.exp(scores - lse_ref[h : h + 1, at])
            grad_t = half_rows(g_t[:, at], h + 1)
            grad_probs = dot(kv_s[:, vlanes], grad_t)
            own = g_t[(h + 1) * 64 : (h + 2) * 64, at].astype(F32)
            inner = jnp.sum(
                own * att_t_ref[h * 64 : h * 64 + 64, at], axis=0, keepdims=True
            )
            grad_scores = (probs * (grad_probs - inner)).astype(BF)
            lanes = slice(h * 128, h * 128 + 128)
            acc[:, vlanes] += dot(probs.astype(BF), g_m[at, lanes])
            acc[:, klanes] += dot(grad_scores, q_m[at, lanes])
            part = dot(k_t[klanes, :], grad_scores)[khalf * 64 : khalf * 64 + 64]
            dq_t[h * 64 : h * 64 + 64, at] = part * HEAD_DIM ** (-0.5)
    first, low = lane_masks(rows)
    cosine, sine = tables[0][0:rows, :], -tables[1][0:rows, :]
    grad_q = dq_t[...].T
    for t in range(2):
        lanes = slice(t * 128, t * 128 + 128)
        dq_ref[:, lanes] = turn(grad_q[:, lanes], cosine, sine, first).astype(BF)
    for i in range(n_kv):
        at = slice(i * rows, (i + 1) * rows)
        cosine, sine = tables[0][at, :], -tables[1][at, :]
        target = keep_ref if i < n_kv // 2 else send_ref
        block = i % (n_kv // 2)
        grad = acc[at, 0:128]
        target[block, :, 0:128] = turn(grad, cosine, sine, first).astype(BF)
        grad = acc[at, 128:256]
        grad = jnp.where(low, turn(grad, cosine, sine, first), grad)
        target[block, :, 128:256] = grad.astype(BF)
        target[block, :, 256:384] = acc[at, 256:384].astype(BF)


ACT_H, ACT_MIX, ACT_GU, ACT_GB, ACT_ATT, ACT_COT, ACT_ALL = (
    0, D, D + FF, D + 3 * FF, 2 * D + 3 * FF, 3 * D + 3 * FF, 4 * D + 3 * FF
)


def middle_kernel(n_packs, idx, *refs):
    atts = refs[:TP]
    tok_ref, cot_ref, gains_ref, out_own, in_own, down_own = refs[TP : TP + 6]
    packs = refs[TP + 6 : TP + 6 + n_packs]
    down_packs = refs[TP + 6 + n_packs : TP + 6 + 2 * n_packs]
    rest = refs[TP + 6 + 2 * n_packs :]
    result_ref, gmid_ref, act_ref, gain_ref = rest[:4]
    gatts = rest[4 : 4 + TP]
    w_out, w_in, w_down, sems = rest[4 + TP :]
    half = out_own.shape[0] // 2
    count, step = down_half(down_own.shape[0])

    def rows(start, height):
        return pl.ds(pl.multiple_of(start, 16), height)

    z, c, y = idx[0], idx[2], idx[3]
    shards = n_packs // 2 + 1
    own, own_down = y * 2 * half, y * down_own.shape[0]
    outs = [pltpu.make_async_copy(out_own, w_out.at[rows(own, 2 * half), :], sems.at[0])]
    ins = [pltpu.make_async_copy(in_own, w_in.at[rows(own, 2 * half), :], sems.at[1])]
    target = w_down.at[rows(own_down, down_own.shape[0]), :]
    downs = [pltpu.make_async_copy(down_own, target, sems.at[2])]
    for i, pack in enumerate(packs):
        shard = lax.rem(y - (i // 2 + 1) + shards, shards)
        core = 1 - c if i % 2 else c
        at = rows((shard * 2 + core) * half, half)
        source = pack.at[0:half, :]
        outs.append(pltpu.make_async_copy(source, w_out.at[at, :], sems.at[3 + 6 * i]))
        for b in range(3):
            source = pack.at[(1 + b) * half : (2 + b) * half, :]
            target = w_in.at[at, b * D : (b + 1) * D]
            ins.append(pltpu.make_async_copy(source, target, sems.at[4 + 6 * i + b]))
        quarter, hop = down_half(count)
        for b in range(2):
            parity = lax.rem(z + b, 2)
            at = rows(shard * down_own.shape[0] + core * step + parity * hop, quarter)
            source = down_packs[i].at[b]
            downs.append(pltpu.make_async_copy(source, w_down.at[at, :], sems.at[7 + 6 * i + b]))
    apart = 4 * down_half(count)[0] == down_own.shape[0]
    for copy in outs + ins + (downs if apart else downs[:1]):
        copy.start()
    starts = [pl.multiple_of(lax.rem(z + j, TP) * GW, GW) for j in range(TP)]
    for copy in outs:
        copy.wait()
    middle = tok_ref[...].astype(F32)
    for j in range(TP):
        middle += dot(atts[j][...], w_out[pl.ds(starts[j], GW), :])
        act_ref[:, ACT_ATT + j * GW : ACT_ATT + (j + 1) * GW] = atts[j][...]
    gain = gains_ref[1:2, :]
    unit, scale = normalise(middle)
    h = (unit * gain).astype(BF)
    act_ref[:, ACT_H : ACT_H + D] = h
    for copy in ins:
        copy.wait()
    gate = dot(h, w_in[:, :FF])
    up = dot(h, w_in[:, FF:])
    phi = 0.5 * (1.0 + lax.erf(gate * math.sqrt(0.5)))
    active = gate * phi
    mixed = (active * up).astype(BF)
    act_ref[:, ACT_MIX : ACT_MIX + FF] = mixed
    for i, copy in enumerate(downs):
        if i and not apart:
            copy.start()
        copy.wait()
    grad_mixed = dot_nt(cot_ref[...], w_down[...])
    slope = phi + gate * (jnp.exp(-0.5 * gate * gate) * (1.0 / math.sqrt(2.0 * math.pi)))
    grad_gate = (grad_mixed * up * slope).astype(BF)
    grad_up = (grad_mixed * active).astype(BF)
    act_ref[:, ACT_GU : ACT_GU + FF] = grad_gate
    act_ref[:, ACT_GU + FF : ACT_GU + 2 * FF] = grad_up
    grad_h = dot_nt(grad_gate, w_in[:, :FF]) + dot_nt(grad_up, w_in[:, FF:])
    gain_ref[...] = jnp.broadcast_to(
        jnp.sum(grad_h * unit, axis=0, keepdims=True), gain_ref.shape
    )
    grad_middle = cot_ref[...].astype(F32) + normalise_back(grad_h * gain, unit, scale)
    gmid_ref[...] = grad_middle
    gb = grad_middle.astype(BF)
    act_ref[:, ACT_GB : ACT_GB + D] = gb
    act_ref[:, ACT_COT : ACT_COT + D] = cot_ref[...]
    for j in range(TP):
        part = dot_nt(gb, w_out[pl.ds(starts[j], GW), :])
        pad = jnp.zeros((part.shape[0], 256 - GW), F32)
        gatts[j][...] = jnp.concatenate([pad, part], axis=1).astype(BF)
    result_ref[...] = middle + dot(mixed, w_down[...])


def up16(n):
    return -(-n // 16) * 16


def plan(shards):
    rows_d, rows_f = D // (4 * shards), FF // (4 * shards)
    return rows_d, rows_f, up16(rows_d), up16(rows_f)


def ffn_grads_kernel(shards, idx, own, got, gain_ref, *refs):
    ins = refs[:shards]
    mine_ref, other_ref = refs[shards : shards + 2]
    h_t, mixed_t, att_t, right = refs[shards + 2 :]
    z, x, c, y = idx[0], idx[1], idx[2], idx[3]
    rows_d, rows_f, pad_d, pad_f = plan(shards)
    n = own.shape[0]
    pieces, per = 4 * shards, GW // rows_d
    for i, act in enumerate((own, got)):
        at = slice(i * n, (i + 1) * n)
        h = act[:, ACT_H : ACT_H + D].T
        mixed = act[:, ACT_MIX : ACT_MIX + FF].T
        att = act[:, ACT_ATT : ACT_ATT + D].T
        for m in range(pieces):
            h_t[m, 0:rows_d, at] = h[m * rows_d : (m + 1) * rows_d]
            mixed_t[m, 0:rows_f, at] = mixed[m * rows_f : (m + 1) * rows_f]
            att_t[m, 0:rows_d, at] = att[m * rows_d : (m + 1) * rows_d]
        right[at, 0 : 2 * FF] = act[:, ACT_GU : ACT_GU + 2 * FF]
        right[at, 2 * FF : 2 * FF + D] = act[:, ACT_GB : ACT_GB + D]
        right[at, 2 * FF + D :] = act[:, ACT_COT : ACT_COT + D]
    for k in range(shards):
        piece = (lax.rem(y + k, shards) * 2 + c) * 2
        left = h_t[pl.ds(piece, 2)].reshape(2 * pad_d, 2 * n)
        grad = dot(left, right[:, 0 : 2 * FF]).astype(BF)
        for xx in range(2):
            for t in range(2 * FF // 128):
                ins[k][xx, t * pad_d : t * pad_d + rows_d, :] = grad[
                    xx * pad_d : xx * pad_d + rows_d, t * 128 : t * 128 + 128
                ]
    high = mine_ref.shape[1]
    gain = jnp.broadcast_to(gain_ref[0:1, :], (high - pad_f - pad_d, D)).astype(BF)
    for xx in range(2):
        for s in range(shards):
            piece = (s * 2 + c) * 2 + xx
            turned = lax.rem(piece // per - z + TP, TP) * per + lax.rem(piece, per)
            down = dot(mixed_t[piece], right[:, 2 * FF + D :]).astype(BF)
            out = dot(att_t[turned], right[:, 2 * FF : 2 * FF + D]).astype(BF)
            both = jnp.concatenate([down, out, gain], axis=0)

            @pl.when(x == xx)
            def _():
                mine_ref[s] = both

            @pl.when(x != xx)
            def _():
                other_ref[s] = both


def qkv_grads_kernel(shards, n_kv, idx, *refs):
    hs = refs[:n_kv]
    keep_ref, send_ref, dq_ref, w_ref, gains_ref, mine_ref, other_ref = refs[n_kv:]
    c = idx[2]
    total = None
    for i in range(n_kv):
        grads = (keep_ref if i < n_kv // 2 else send_ref)[i % (n_kv // 2)]
        part = dot(grads.T, hs[i][...])
        total = part if total is None else total + part
    grad = jnp.concatenate([total, dot(dq_ref[...].T, hs[0][...])], axis=0).T
    gain = gains_ref[...].T[:, 0:1]
    lane = lax.broadcasted_iota(jnp.int32, grad.shape, 1)
    by_gain = jnp.sum(grad * w_ref[...].astype(F32), axis=1, keepdims=True) / gain
    grad = jnp.where(lane < 3 * GW, grad, by_gain).astype(BF)
    height = plan(shards)[0]
    for s in range(shards):
        for cc in range(2):
            block = (s * 2 + cc) * 2 * height
            for xx in range(2):
                part = grad[block + xx * height : block + (xx + 1) * height]

                @pl.when(c == cc)
                def _():
                    mine_ref[s, xx] = part

                @pl.when(c != cc)
                def _():
                    other_ref[s, xx] = part


def h_one_grads_kernel(n_sum, idx, *refs):
    parts = refs[:n_sum]
    dq_ref, w_ref, gh_mine, gh_other = refs[n_sum:]
    rows = gh_mine.shape[1]
    for j in range(TP):
        at = slice(j * rows, (j + 1) * rows)
        total = parts[0][0, at, :].astype(F32)
        for part in parts[1:]:
            total += part[0, at, :].astype(F32)
        grad = jnp.concatenate([total.astype(BF), dq_ref[at, :]], axis=1)
        owner = lax.rem(idx[0] - j + TP, TP)
        target = gh_other if j % 2 else gh_mine
        target[owner // 2] = dot_nt(grad, w_ref[...]).astype(BF)


def tail_kernel(n_sum, idx, *refs):
    tok_ref, gmid_ref, gains_ref, out_ref = refs[n_sum:]
    unit, scale = normalise(tok_ref[...].astype(F32))
    total = 0.0
    for grad in refs[:n_sum]:
        grad = grad[idx[0] // 2] if len(grad.shape) == 3 else grad[...]
        total += grad.astype(F32)
    grad_unit = total * gains_ref[0:1, :]
    out_ref[...] = gmid_ref[...] + normalise_back(grad_unit, unit, scale)


def place_z(z, k):
    return lax.rem(z // 2 + k % 2, 2) * 2 + lax.rem(lax.rem(z, 2) + k // 2, 2)


def in_unpack_kernel(shards, idx, own, got, in_ref, held):
    rows_d, _, pad_d, _ = plan(shards)
    size = held.shape[0] // TP
    z, x, c = idx[0], idx[1], idx[2]
    for cr in range(2):
        for xr in range(2):
            for k in range(TP):
                at = pl.ds(pl.multiple_of(place_z(z, k) * size, size), size)
                held[at, :] = (got if cr else own)[xr, k].astype(F32)
            cc, xx = lax.rem(c + cr, 2), lax.rem(x + xr, 2)
            for t in range(2 * FF // 128):
                base = t * pad_d
                in_ref[cc, xx, :, t * 128 : t * 128 + 128] = held[base : base + rows_d, :]


def rest_unpack_kernel(shards, idx, own, got, out_ref, down_ref, gain_ref, held):
    rows_d, rows_f, pad_d, pad_f = plan(shards)
    size = held.shape[0] // TP
    z, x, c = idx[0], idx[1], idx[2]
    gain = None
    for cr in range(2):
        for xr in range(2):
            for k in range(TP):
                at = pl.ds(pl.multiple_of(place_z(z, k) * size, size), size)
                held[at, :] = (got if cr else own)[xr, k].astype(F32)
            cc, xx = lax.rem(c + cr, 2), lax.rem(x + xr, 2)
            down_ref[cc, xx] = held[0:rows_f, :]
            out_ref[cc, xx] = held[pad_f : pad_f + rows_d, :]
            if xr == 0:
                row = held[pad_f + pad_d : pad_f + pad_d + 8, :]
                gain = row if gain is None else gain + row
    part = gain_ref.shape[0]
    for s in range(shards):

        @pl.when(idx[3] == s)
        def _():
            gain_ref[...] = gain[0:1, s * part : (s + 1) * part].reshape(part)


def qkv_unpack_kernel(idx, own, got, out_ref, gain_ref, gain_s):
    z, x, c = idx[0], idx[1], idx[2]
    for cr in range(2):
        for xr in range(2):
            cc, xx = lax.rem(c + cr, 2), lax.rem(x + xr, 2)
            gain = None
            for g in range(TP):
                k = 2 * lax.rem(g % 2 + z, 2) + lax.rem(g // 2 + z // 2, 2)
                block = (got if cr else own)[xr, k].astype(F32)
                for source, place in ((0, 1), (1, 2), (2, 0)):
                    out_ref[cc, xx, :, place * D + g * GW : place * D + (g + 1) * GW] = block[
                        :, source * GW : (source + 1) * GW
                    ]
                tail = block[:, 512:640]
                gain = tail if gain is None else gain + tail
            height = gain.shape[0]
            at = pl.multiple_of((cc * 2 + xx) * height, height)
            gain_s[pl.ds(at, height), :] = gain
    gain_ref[...] = gain_s[...].T[64:65].reshape(gain_ref.shape)


def shift(value, axis, k):
    n = lax.axis_size(axis)
    return lax.ppermute(value, axis, [(i, (i + k) % n) for i in range(n)])


def gather(value, axis):
    return [value] + [shift(value, axis, k) for k in range(1, lax.axis_size(axis))]


def pick(value, index, dim):
    return lax.dynamic_index_in_dim(value, index, dim, keepdims=False)


def term(value, *views):
    return (value, views)


def take(index, dim):
    return lambda value: pick(value, index, dim)


def reshaped(*shape):
    return lambda value: value.reshape(shape)


def viewed(terms, view):
    return [(value, views + (view,)) for value, views in terms]


def reduce_step(order, terms, axis, dim):
    n, i = lax.axis_size(axis), lax.axis_index(axis)
    total = order.add(terms)
    got = [term(shift(pick(total, lax.rem(i + k, n), dim), axis, k)) for k in range(1, n)]
    return [term(pick(total, i, dim))] + got


def add(values):
    total = values[0].astype(F32)
    for value in values[1:]:
        total = total + value.astype(F32)
    return total.astype(BF)


def swap_z(value, bit):
    return lax.ppermute(value, "z", [(i, i ^ bit) for i in range(TP)])


def reduce_z(order, terms, bit):
    z = lax.axis_index("z")
    i, dim = (z % 2, 1) if bit == 1 else (z // 2, 0)
    total = order.add(terms)
    return [term(pick(total, i, dim)), term(swap_z(pick(total, 1 - i, dim), bit))]


def gather_z(order, value, bit):
    value = order.step(value)
    got = swap_z(value, bit)
    return jnp.stack([value, got]) if bit == 2 else jnp.concatenate([value, got])


def sum_over(value, axis):
    return add([value] + [shift(value, axis, k) for k in range(1, lax.axis_size(axis))])


def after(value, *others):
    return lax.optimization_barrier((value, *others))[0]


class Order:
    def __init__(self):
        self.last = None

    def __call__(self, values):
        if self.last is None:
            return values
        return lax.optimization_barrier((values, self.last))[0]

    def step(self, value):
        self.last = self(value)
        return self.last

    def add(self, terms):
        values = []
        for value, (_, views) in zip(self([t[0] for t in terms]), terms):
            for view in views:
                value = view(value)
            values.append(value)
        self.last = add(values)
        return self.last

    def run(self, body, outs, n_smem, ins, **more):
        got = call(body, outs, n_smem, self(list(ins)), **more)
        self.last = got[0]
        return got


def per_device(tokens, gain_one, w_qkv, w_out, gain_two, w_in, w_down, cotangent):
    tok, cot = tokens[0], cotangent[0]
    rows = tok.shape[0]
    many = TP * rows
    zo, z = lax.axis_index("zo"), lax.axis_index("z")
    x, c, y = lax.axis_index("x"), lax.axis_index("core"), lax.axis_index("shard")
    outer, shards = lax.axis_size("zo"), lax.axis_size("shard")
    part = w_qkv.shape[0]
    n_kv = 4 * outer
    keys = n_kv * many
    rows_d, rows_f, pad_d, pad_f = plan(shards)
    high_in, high = 2 * FF // 128 * pad_d, -(-(pad_f + pad_d + 16) // 64) * 64
    i32 = jnp.int32
    idx = jnp.stack([z, x, c, y]).astype(i32)
    order = Order()

    toks = gather(tok, "z")
    w_own, w_mine = order.run(
        group_kernel,
        [((part, WC), BF), ((part // 2 + 16, WC), BF)],
        1,
        [idx, w_qkv, gain_one, gain_two],
        hbm_ins=(1, 2, 3),
        name="group_columns",
    )
    w_slices = [w_own]
    for k in range(1, shards):
        w_slices.append(shift(w_mine, "shard", k))
        w_slices.append(shift(w_slices[-1], "core", 1))
    pack, pack_down = order.run(
        pack_kernel,
        [((2 * part, D), BF), ((down_half(down_half(w_down.shape[0])[0])[0], D), BF)],
        1,
        [idx, w_out, w_in, w_down],
        hbm_ins=(1, 2, 3),
        name="pack_weights",
    )
    downs = [shift(pack_down, "shard", k) for k in range(1, shards)]
    packs = [shift(pack, "shard", k) for k in range(1, shards)]

    freq = THETA ** (-jnp.arange(HEAD_DIM // 2, dtype=F32) * (2.0 / HEAD_DIM))
    owners = lax.rem(z - jnp.arange(TP, dtype=i32) + TP, TP)
    places = []
    for cr in range(2):
        for xr in range(2):
            for zr in range(outer):
                zz = lax.rem(zo - zr + outer, outer)
                place = ((zz * TP + owners) * 2 + lax.rem(x + xr, 2)) * 2 + lax.rem(c + cr, 2)
                places.append(place)
    first_place = jnp.concatenate(places) * rows
    freq = jnp.tile(freq, 4)[None, :]
    sign = jnp.where(jnp.arange(128) % 64 < 32, -1.0, 1.0).astype(F32)
    start = first_place.astype(F32)[:, None] * freq
    step = jnp.arange(rows, dtype=i32).astype(F32)[:, None] * freq
    cos_a, sin_a = jnp.cos(start)[:, None], jnp.sin(start)[:, None]
    cos_b, sin_b = jnp.cos(step)[None], jnp.sin(step)[None]
    cosine = (cos_a * cos_b - sin_a * sin_b).reshape(keys, 128)
    sine = ((sin_a * cos_b + cos_a * sin_b) * sign).reshape(keys, 128)

    query, kv, h_one, w_full, gains = order.run(
        functools.partial(front_kernel, shards),
        [
            ((many, 256), BF),
            ((many, 2 * GW), BF),
            ((many, D), BF),
            ((D, WC), BF),
            ((8, D), F32),
        ],
        1,
        [idx, *toks, *w_slices, w_mine, cosine, sine],
        hbm_ins=range(1, 1 + TP + len(w_slices) + 3),
        hbm_outs=(2, 3, 4),
        name="front",
    )

    near = gather(kv, "zo")
    near = near + [shift(v, "x", 1) for v in near]
    kv_core = shift(kv, "core", 1)
    close = (0, n_kv // 2)
    far = [i for i in range(n_kv) if i not in close]
    scratch = lambda count: [
        pltpu.VMEM((count * many, 2 * GW), BF),
        pltpu.VMEM((256, count * many), BF),
        pltpu.VMEM((256, many), BF),
    ]
    first = order.run(
        functools.partial(forward_kernel, 2, False),
        [((GW, many), F32), ((8, many), F32)],
        0,
        [query, kv, kv_core],
        scratch=scratch(2),
        name="attention_forward_near",
    )
    kvs = near + [kv_core] + [shift(after(v, *first), "core", 1) for v in near[1:]]
    downs = [jnp.stack([v, swap_z(v, 1)]) for v in downs]
    both_down = [v for p in downs for v in (p, shift(p, "core", 1))]
    first = [first[0], after(first[1], *both_down)]
    att = order.run(
        functools.partial(forward_kernel, len(far), True),
        [((rows, GW), BF)] * TP + [((GW, many), F32), ((8, many), F32)],
        0,
        [query, *[kvs[i] for i in far], *first],
        scratch=scratch(len(far)),
        hbm_outs=(TP, TP + 1),
        name="attention_forward_far",
    )
    att_blocks, (attended_t, lse) = att[:TP], att[TP:]
    h_near = gather(after(h_one, lse), "zo")
    h_near = h_near + [shift(v, "x", 1) for v in h_near]
    h_core = shift(after(h_one, lse), "core", 1)
    atts = [att_blocks[0]] + [shift(att_blocks[k], "z", -k) for k in range(1, TP)]

    packs = [after(p, lse) for p in packs]
    both = [v for p in packs for v in (p, shift(p, "core", 1))]
    mid = order.run(
        functools.partial(middle_kernel, len(both)),
        [((rows, D), F32), ((rows, D), F32), ((rows, ACT_ALL), BF), ((8, D), F32)]
        + [((rows, 256), BF)] * TP,
        1,
        [idx, *atts, tok, cot, after(gains, h_core), w_out, w_in, w_down, *both, *both_down],
        scratch=[
            pltpu.VMEM((D, D), BF),
            pltpu.VMEM((D, 2 * FF), BF),
            pltpu.VMEM((FF, D), BF),
            pltpu.SemaphoreType.DMA((3 + 6 * len(both),)),
        ],
        any_ins=range(1 + TP + 3, 1 + TP + 6 + 2 * len(both)),
        hbm_ins=(1 + TP, 2 + TP, 3 + TP),
        hbm_outs=(0, 1, 3),
        name="feed_forward",
    )
    result, grad_middle, act, gain_two_row = mid[:4]
    act = after(act, *h_near)
    gatts = mid[4:]
    gas = [gatts[0]] + [shift(gatts[k], "z", k) for k in range(1, TP)]

    hs = h_near + [h_core] + [shift(after(v, result), "core", 1) for v in h_near[1:]]
    gain_two_row = after(gain_two_row, *hs)
    ffn = order.run(
        functools.partial(ffn_grads_kernel, shards),
        [((2, high_in, 128), BF)] * shards
        + [((shards, high, D), BF)] * 2,
        1,
        [idx, act, shift(act, "core", 1), gain_two_row],
        scratch=[
            pltpu.VMEM((4 * shards, pad_d, 2 * rows), BF),
            pltpu.VMEM((4 * shards, pad_f, 2 * rows), BF),
            pltpu.VMEM((4 * shards, pad_d, 2 * rows), BF),
            pltpu.VMEM((2 * rows, 2 * FF + 2 * D), BF),
        ],
        hbm_outs=range(shards + 2),
        name="ffn_weight_grads",
    )
    f_in = [term(ffn[0])]
    f_in += [term(shift(after(ffn[k], *gas), "shard", k)) for k in range(1, shards)]
    f_rest = [term(ffn[shards]), term(shift(after(ffn[shards + 1], *gas), "x", 1))]

    dkv_keep, dkv_send, dq = order.run(
        functools.partial(backward_kernel, n_kv),
        [((n_kv // 2, many, 2 * GW), BF)] * 2 + [((many, 256), BF)],
        0,
        [query, *kvs, *gas, attended_t, lse, cosine, sine],
        scratch=[
            pltpu.VMEM((keys, 2 * GW), BF),
            pltpu.VMEM((256, keys), BF),
            pltpu.VMEM((256, many), BF),
            pltpu.VMEM((256, many), BF),
            pltpu.VMEM((many, 2 * GW), BF),
            pltpu.VMEM((many, 2 * GW), BF),
            pltpu.VMEM((keys, 2 * GW), F32),
            pltpu.VMEM((256, many), F32),
        ],
        hbm_ins=range(0, 1 + n_kv + TP + 4),
        name="attention_backward",
    )
    mine, other = order.run(
        functools.partial(qkv_grads_kernel, shards, n_kv),
        [((shards, 2, rows_d, WC), BF)] * 2,
        1,
        [idx, *hs, dkv_keep, dkv_send, dq, w_full, gains],
        hbm_ins=range(1, 1 + n_kv),
        name="qkv_weight_grads",
    )
    first_got = [t[0] for t in f_in[1:] + f_rest[1:]]
    mine, other, *_ = lax.optimization_barrier((mine, other, *first_got))
    order.last = mine
    terms = [term(dkv_keep), term(shift(after(dkv_send, mine), "core", 1))]
    terms = viewed(terms, reshaped(2, outer, many, 2 * GW))
    wq = [term(mine), term(shift(other, "core", 1))]

    def pair(value):
        return jnp.stack([value, shift(order.step(value), "x", 1)])

    f_in = reduce_step(order, f_in, "x", 0)
    f_rest = reduce_step(order, f_rest, "shard", 0)
    wq = reduce_step(order, wq, "shard", 0)
    f_in = reduce_z(order, viewed(f_in, reshaped(2, 2, high_in // TP, 128)), 1)
    f_rest = reduce_z(order, viewed(f_rest, reshaped(2, 2, high // TP, D)), 1)
    got = shift(order.add(viewed(terms, take(1, 0))), "x", 1)
    terms = viewed(terms, take(0, 0)) + [term(got)]
    wq = reduce_step(order, wq, "x", 0)
    f_in = reduce_z(order, f_in, 2)
    f_rest = reduce_z(order, f_rest, 2)
    wq = gather_z(order, sum_over(order.add(wq), "zo"), 2)
    f_in = gather_z(order, sum_over(order.add(f_in), "zo"), 2)
    f_rest = gather_z(order, sum_over(order.add(f_rest), "zo"), 2)

    wq = gather_z(order, wq, 1)
    f_in = gather_z(order, f_in, 1)
    f_rest = gather_z(order, f_rest, 1)
    if outer > 1:
        total = order.add(terms)
        sums = [total[0:1]] + [shift(total[k : k + 1], "zo", -k) for k in range(1, outer)]
    else:
        sums = [
            dkv_keep.reshape(2, many, 2 * GW),
            terms[1][0].reshape(2, many, 2 * GW),
            got.reshape(1, many, 2 * GW),
        ]
    gh, gh_other = order.run(
        functools.partial(h_one_grads_kernel, len(sums)),
        [((2, rows, D), BF)] * 2,
        1,
        [idx, *sums, dq, w_full],
        name="h_one_grads",
    )
    wq = pair(wq)
    f_in = pair(after(f_in, f_rest))
    gh = [term(gh), term(swap_z(order(gh_other), 1))]
    wq = order.step(wq)
    wq_got = shift(wq, "core", 1)
    f_rest = pair(f_rest)
    gh = reduce_z(order, gh, 2)
    g_qkv, grad_gain_one = order.run(
        qkv_unpack_kernel,
        [((2, 2, rows_d, 3 * D), F32), ((part,), F32)],
        1,
        [idx, wq, wq_got],
        scratch=[pltpu.VMEM((part, 128), F32)],
        name="qkv_unpack",
    )
    f_in = order.step(f_in)
    f_in_got = shift(f_in, "core", 1)
    f_rest = order.step(after(f_rest, gh[1][0]))
    f_rest_got = shift(f_rest, "core", 1)
    (g_in,) = order.run(
        functools.partial(in_unpack_kernel, shards),
        [((2, 2, rows_d, 2 * FF), F32)],
        1,
        [idx, f_in, f_in_got],
        scratch=[pltpu.VMEM((high_in, 128), F32)],
        name="w_in_unpack",
    )
    (grad_tokens,) = order.run(
        functools.partial(tail_kernel, len(gh)),
        [((rows, D), F32)],
        1,
        [idx, *[t[0] for t in gh], tok, grad_middle, gains],
        name="token_grads",
    )

    g_out, g_down, grad_gain_two = order.run(
        functools.partial(rest_unpack_kernel, shards),
        [
            ((2, 2, rows_d, D), F32),
            ((2, 2, rows_f, D), F32),
            ((part,), F32),
        ],
        1,
        [idx, f_rest, f_rest_got],
        scratch=[pltpu.VMEM((high, D), F32)],
        name="w_down_w_out_unpack",
    )
    return (
        result[None],
        grad_tokens[None],
        grad_gain_one,
        g_qkv.reshape(part, 3 * D),
        g_out.reshape(part, D),
        grad_gain_two,
        g_in.reshape(part, 2 * FF),
        g_down.reshape(w_down.shape[0], D),
    )


def solution(mesh):
    blocks = mesh.shape["ctx"]
    fine = Mesh(
        mesh.devices.reshape(blocks // (TP * 4), TP, 2, 2, mesh.shape["shard"]), CTX + ("shard",)
    )
    rows, split = P("shard", CTX, None), P("shard", None)
    return jax.shard_map(
        per_device,
        mesh=fine,
        in_specs=(rows, P("shard"), split, split, P("shard"), split, split, rows),
        out_specs=(rows, rows, P("shard"), split, split, P("shard"), split, split),
        check_vma=False,
    )
```

```python
import functools
import math

import jax
import jax.numpy as jnp
from jax import lax
from jax.experimental import pallas as pl
from jax.experimental.pallas import tpu as pltpu
from jax.sharding import Mesh, PartitionSpec as P

D = 768
HEADS = 12
HEAD_DIM = 64
FF = 1152
EPS = 1e-05
THETA = 160000.0

TP = 4
GH = HEADS // TP
GW = GH * HEAD_DIM
WC = 640
CTX = ("zo", "z", "x", "core")
BF = jnp.bfloat16
F32 = jnp.float32
VMEM_LIMIT = 32 * 1024 * 1024

KEY_AT = ((0, 0), (0, 1), (1, 0))
VALUE_AT = ((1, 1), (2, 0), (2, 1))


def dot(a, b):
    return jnp.dot(a, b, preferred_element_type=F32)


def dot_nt(a, b):
    return lax.dot_general(a, b, (((1,), (1,)), ((), ())), preferred_element_type=F32)


def dot_tn(a, b):
    return lax.dot_general(a, b, (((0,), (0,)), ((), ())), preferred_element_type=F32)


def call(body, outs, n_smem, ins, scratch=(), any_ins=(), hbm_ins=(), hbm_outs=(), name=None):
    specs, values = [], []
    for i, value in enumerate(ins):
        space = pltpu.SMEM if i < n_smem else (pl.ANY if i in any_ins else pltpu.VMEM)
        if i in hbm_ins:
            value = pltpu.with_memory_space_constraint(value, pltpu.HBM)
        specs.append(pl.BlockSpec(memory_space=space))
        values.append(value)
    shapes = []
    for i, (shape, kind) in enumerate(outs):
        shapes.append(pltpu.HBM(shape, kind) if i in hbm_outs else jax.ShapeDtypeStruct(shape, kind))
    return pl.pallas_call(
        body,
        out_shape=shapes,
        in_specs=specs,
        out_specs=[pl.BlockSpec(memory_space=pltpu.VMEM)] * len(outs),
        scratch_shapes=list(scratch),
        compiler_params=pltpu.CompilerParams(vmem_limit_bytes=VMEM_LIMIT),
        cost_estimate=pl.CostEstimate(flops=1, bytes_accessed=1, transcendentals=0),
        name=name,
    )(*values)


def normalise(values):
    mean = jnp.mean(values, axis=-1, keepdims=True)
    centred = values - mean
    spread = jnp.mean(centred * centred, axis=-1, keepdims=True)
    scale = lax.rsqrt(spread + EPS)
    return centred * scale, scale


def normalise_back(grad_unit, unit, scale):
    return scale * (
        grad_unit
        - jnp.mean(grad_unit, axis=-1, keepdims=True)
        - unit * jnp.mean(grad_unit * unit, axis=-1, keepdims=True)
    )


def turn(tile, cosine, signed_sine, first_half):
    swapped = jnp.where(first_half, pltpu.roll(tile, 96, 1), pltpu.roll(tile, 32, 1))
    return tile * cosine + swapped * signed_sine


def lane_masks(rows):
    lane = lax.broadcasted_iota(jnp.int32, (rows, 128), 1)
    return lax.rem(lane, 64) < 32, lane < 64


def group_kernel(idx, w_ref, one_ref, two_ref, own_ref, half_ref):
    height = w_ref.shape[0]
    half = height // 2
    for g in range(TP):

        @pl.when(idx[0] == g)
        def _():
            parts = [w_ref[:, p * D + g * GW : p * D + (g + 1) * GW] for p in (1, 2, 0)]
            parts.append(jnp.zeros((height, WC - 3 * GW), BF))
            own_ref[...] = jnp.concatenate(parts, axis=1)

    half_ref[0:half, :] = own_ref[pl.ds(pl.multiple_of(idx[2] * half, half), half), :]
    half_ref[half:, :] = jnp.zeros((16, WC), BF)
    half_ref[half : half + 1, 0:height] = one_ref[...].reshape(1, height)
    half_ref[half + 1 : half + 2, 0:height] = two_ref[...].reshape(1, height)


def pack_kernel(idx, out_ref, in_ref, down_ref, pack_ref, pack_down):
    c = idx[2]
    half = out_ref.shape[0] // 2
    at = pl.ds(pl.multiple_of(c * half, half), half)
    pack_ref[0:half, :] = out_ref[at, :]
    for b in range(3):
        pack_ref[(1 + b) * half : (2 + b) * half, :] = in_ref[at, b * D : (b + 1) * D]
    count, step = down_half(down_ref.shape[0])
    quarter, hop = down_half(count)
    at = pl.multiple_of(c * step + lax.rem(idx[0], 2) * hop, 16)
    pack_down[...] = down_ref[pl.ds(at, quarter), :]


def down_half(height):
    count = -(-height // 32) * 16
    return count, height - count


def front_kernel(shards, idx, *refs):
    toks = refs[:TP]
    n_w = 2 * shards - 1
    ws = refs[TP : TP + n_w]
    mine, cos_ref, sin_ref, q_ref, kv_ref, h_ref, w_ref, gains_ref = refs[TP + n_w :]
    c, y = idx[2], idx[3]
    rows = toks[0].shape[0]
    part = ws[0].shape[0]
    half = part // 2
    gains_ref[...] = jnp.zeros_like(gains_ref)
    for k in range(shards):
        start = lax.rem(y - k + shards, shards) * part
        at = pl.ds(pl.multiple_of(start, part), part)
        if k == 0:
            w_ref[at, :] = ws[0][...]
            continue
        at = pl.ds(pl.multiple_of(start + c * half, half), half)
        w_ref[at, :] = ws[2 * k - 1][0:half]
        at = pl.ds(pl.multiple_of(start + (1 - c) * half, half), half)
        w_ref[at, :] = ws[2 * k][0:half]
    for s in range(shards):

        @pl.when(y == s)
        def _():
            for k in range(shards):
                start = (s - k) % shards * part
                gains = (ws[2 * k - 1] if k else mine)[half : half + 2, 0:part]
                gains_ref[0:2, start : start + part] = gains.astype(F32)

    gain = gains_ref[0:1, :]
    first, low = lane_masks(rows)
    for j in range(TP):
        at = slice(j * rows, (j + 1) * rows)
        unit, _ = normalise(toks[j][...].astype(F32))
        h = (unit * gain).astype(BF)
        h_ref[at, :] = h
        out = dot(h, w_ref[...])
        cosine, sine = cos_ref[at, :], sin_ref[at, :]
        key_a = turn(out[:, 0:128], cosine, sine, first)
        mixed = out[:, 128:256]
        key_b = jnp.where(low, turn(mixed, cosine, sine, first), mixed)
        kv_ref[at, 0:128] = key_a.astype(BF)
        kv_ref[at, 128:256] = key_b.astype(BF)
        kv_ref[at, 256:384] = out[:, 256:384].astype(BF)
        query_a = turn(out[:, 384:512], cosine, sine, first)
        query_b = jnp.where(low, turn(out[:, 512:640], cosine, sine, first), 0.0)
        factor = HEAD_DIM ** (-0.5)
        q_ref[at, 0:128] = (query_a * factor).astype(BF)
        q_ref[at, 128:256] = (query_b * factor).astype(BF)


def half_rows(values_t, head):
    at = head * HEAD_DIM
    rows = values_t[at : at + HEAD_DIM]
    zeros = jnp.zeros_like(rows)
    return jnp.concatenate([rows, zeros] if head % 2 == 0 else [zeros, rows], axis=0)


def forward_kernel(n_kv, last, q_ref, *refs):
    kvs = refs[:n_kv]
    if last:
        before_ref, before_lse = refs[n_kv : n_kv + 2]
        atts = refs[n_kv + 2 : n_kv + 2 + TP]
    att_t_ref, lse_ref, kv_s, v_t, q_t = refs[-5:]
    rows = kvs[0].shape[0]
    block = math.gcd(rows, 256)
    for i, kv in enumerate(kvs):
        kv_s[i * rows : (i + 1) * rows, :] = kv[...]
        v_t[:, i * rows : (i + 1) * rows] = kv[:, 128:384].T
    q_t[...] = q_ref[...].T
    lse_ref[...] = jnp.zeros_like(lse_ref)
    for i in range(rows // block):
        at = slice(i * block, (i + 1) * block)
        for h in range(GH):
            tile = KEY_AT[h][0]
            keys = kv_s[:, tile * 128 : tile * 128 + 128]
            scores = dot(keys, half_rows(q_t[:, at], h))
            top = jnp.max(scores, axis=0, keepdims=True)
            weights = jnp.exp(scores - top)
            total = jnp.sum(weights, axis=0, keepdims=True)
            tile, half = VALUE_AT[h]
            values_t = v_t[(tile - 1) * 128 : tile * 128, :]
            out = dot(values_t, weights.astype(BF))[half * 64 : half * 64 + 64]
            head = slice(h * 64, h * 64 + 64)
            if last:
                old = before_lse[h : h + 1, at]
                high = jnp.maximum(old, top)
                share, own = jnp.exp(old - high), jnp.exp(top - high)
                total = total * own + share
                out = out * own + before_ref[head, at] * share
                top = high
            att_t_ref[head, at] = out / total
            lse_ref[h : h + 1, at] = top + jnp.log(total)
    if last:
        small = rows // TP
        for j in range(TP):
            atts[j][...] = att_t_ref[:, j * small : (j + 1) * small].T.astype(BF)


def backward_kernel(n_kv, q_ref, *refs):
    kvs = refs[:n_kv]
    gas = refs[n_kv : n_kv + TP]
    att_t_ref, lse_ref = refs[n_kv + TP : n_kv + TP + 2]
    tables = refs[n_kv + TP + 2 : n_kv + TP + 4]
    keep_ref, send_ref, dq_ref = refs[n_kv + TP + 4 : n_kv + TP + 7]
    kv_s, k_t, q_t, g_t, q_m, g_m, acc, dq_t = refs[n_kv + TP + 7 :]
    rows = kvs[0].shape[0]
    small = gas[0].shape[0]
    block = math.gcd(rows, 256)
    for i, kv in enumerate(kvs):
        kv_s[i * rows : (i + 1) * rows, :] = kv[...]
        k_t[:, i * rows : (i + 1) * rows] = kv[:, 0:256].T
    q_t[...] = q_ref[...].T
    _, low = lane_masks(small)
    for j in range(TP):
        at = slice(j * small, (j + 1) * small)
        g_t[:, at] = gas[j][...].T
        first, second = gas[j][:, 0:128], gas[j][:, 128:256].astype(F32)
        g_m[at, 0:128] = first
        g_m[at, 128:256] = jnp.where(low, second, 0.0).astype(BF)
        g_m[at, 256:384] = jnp.where(low, 0.0, second).astype(BF)
        both = q_ref[at, 0:128].astype(F32)
        q_m[at, 0:128] = jnp.where(low, both, 0.0).astype(BF)
        q_m[at, 128:256] = jnp.where(low, 0.0, both).astype(BF)
        q_m[at, 256:384] = q_ref[at, 128:256]
    dq_t[...] = jnp.zeros_like(dq_t)
    acc[...] = jnp.zeros_like(acc)
    for i in range(rows // block):
        at = slice(i * block, (i + 1) * block)
        for h in range(GH):
            ktile, khalf = KEY_AT[h]
            vtile = VALUE_AT[h][0]
            klanes = slice(ktile * 128, ktile * 128 + 128)
            vlanes = slice(vtile * 128, vtile * 128 + 128)
            scores = dot(kv_s[:, klanes], half_rows(q_t[:, at], h))
            probs = jnp.exp(scores - lse_ref[h : h + 1, at])
            grad_t = half_rows(g_t[:, at], h + 1)
            grad_probs = dot(kv_s[:, vlanes], grad_t)
            own = g_t[(h + 1) * 64 : (h + 2) * 64, at].astype(F32)
            inner = jnp.sum(
                own * att_t_ref[h * 64 : h * 64 + 64, at], axis=0, keepdims=True
            )
            grad_scores = (probs * (grad_probs - inner)).astype(BF)
            lanes = slice(h * 128, h * 128 + 128)
            acc[:, vlanes] += dot(probs.astype(BF), g_m[at, lanes])
            acc[:, klanes] += dot(grad_scores, q_m[at, lanes])
            part = dot(k_t[klanes, :], grad_scores)[khalf * 64 : khalf * 64 + 64]
            dq_t[h * 64 : h * 64 + 64, at] = part * HEAD_DIM ** (-0.5)
    first, low = lane_masks(rows)
    cosine, sine = tables[0][0:rows, :], -tables[1][0:rows, :]
    grad_q = dq_t[...].T
    for t in range(2):
        lanes = slice(t * 128, t * 128 + 128)
        dq_ref[:, lanes] = turn(grad_q[:, lanes], cosine, sine, first).astype(BF)
    for i in range(n_kv):
        at = slice(i * rows, (i + 1) * rows)
        cosine, sine = tables[0][at, :], -tables[1][at, :]
        target = keep_ref if i < n_kv // 2 else send_ref
        block = i % (n_kv // 2)
        grad = acc[at, 0:128]
        target[block, :, 0:128] = turn(grad, cosine, sine, first).astype(BF)
        grad = acc[at, 128:256]
        grad = jnp.where(low, turn(grad, cosine, sine, first), grad)
        target[block, :, 128:256] = grad.astype(BF)
        target[block, :, 256:384] = acc[at, 256:384].astype(BF)


ACT_H, ACT_MIX, ACT_GU, ACT_GB, ACT_ATT, ACT_COT, ACT_ALL = (
    0, D, D + FF, D + 3 * FF, 2 * D + 3 * FF, 3 * D + 3 * FF, 4 * D + 3 * FF
)


def middle_kernel(n_packs, idx, *refs):
    atts = refs[:TP]
    tok_ref, cot_ref, gains_ref, out_own, in_own, down_own = refs[TP : TP + 6]
    packs = refs[TP + 6 : TP + 6 + n_packs]
    down_packs = refs[TP + 6 + n_packs : TP + 6 + 2 * n_packs]
    rest = refs[TP + 6 + 2 * n_packs :]
    result_ref, gmid_ref, act_ref, gain_ref = rest[:4]
    gatts = rest[4 : 4 + TP]
    w_out, w_in, w_down, sems = rest[4 + TP :]
    half = out_own.shape[0] // 2
    count, step = down_half(down_own.shape[0])

    def rows(start, height):
        return pl.ds(pl.multiple_of(start, 16), height)

    z, c, y = idx[0], idx[2], idx[3]
    shards = n_packs // 2 + 1
    own, own_down = y * 2 * half, y * down_own.shape[0]
    outs = [pltpu.make_async_copy(out_own, w_out.at[rows(own, 2 * half), :], sems.at[0])]
    ins = [pltpu.make_async_copy(in_own, w_in.at[rows(own, 2 * half), :], sems.at[1])]
    target = w_down.at[rows(own_down, down_own.shape[0]), :]
    downs = [pltpu.make_async_copy(down_own, target, sems.at[2])]
    for i, pack in enumerate(packs):
        shard = lax.rem(y - (i // 2 + 1) + shards, shards)
        core = 1 - c if i % 2 else c
        at = rows((shard * 2 + core) * half, half)
        source = pack.at[0:half, :]
        outs.append(pltpu.make_async_copy(source, w_out.at[at, :], sems.at[3 + 6 * i]))
        for b in range(3):
            source = pack.at[(1 + b) * half : (2 + b) * half, :]
            target = w_in.at[at, b * D : (b + 1) * D]
            ins.append(pltpu.make_async_copy(source, target, sems.at[4 + 6 * i + b]))
        quarter, hop = down_half(count)
        for b in range(2):
            parity = lax.rem(z + b, 2)
            at = rows(shard * down_own.shape[0] + core * step + parity * hop, quarter)
            source = down_packs[i].at[b]
            downs.append(pltpu.make_async_copy(source, w_down.at[at, :], sems.at[7 + 6 * i + b]))
    apart = 4 * down_half(count)[0] == down_own.shape[0]
    for copy in outs + ins + (downs if apart else downs[:1]):
        copy.start()
    starts = [pl.multiple_of(lax.rem(z + j, TP) * GW, GW) for j in range(TP)]
    for copy in outs:
        copy.wait()
    middle = tok_ref[...].astype(F32)
    for j in range(TP):
        middle += dot(atts[j][...], w_out[pl.ds(starts[j], GW), :])
        act_ref[:, ACT_ATT + j * GW : ACT_ATT + (j + 1) * GW] = atts[j][...]
    gain = gains_ref[1:2, :]
    unit, scale = normalise(middle)
    h = (unit * gain).astype(BF)
    act_ref[:, ACT_H : ACT_H + D] = h
    for copy in ins:
        copy.wait()
    gate = dot(h, w_in[:, :FF])
    up = dot(h, w_in[:, FF:])
    phi = 0.5 * (1.0 + lax.erf(gate * math.sqrt(0.5)))
    active = gate * phi
    mixed = (active * up).astype(BF)
    act_ref[:, ACT_MIX : ACT_MIX + FF] = mixed
    for i, copy in enumerate(downs):
        if i and not apart:
            copy.start()
        copy.wait()
    grad_mixed = dot_nt(cot_ref[...], w_down[...])
    slope = phi + gate * (jnp.exp(-0.5 * gate * gate) * (1.0 / math.sqrt(2.0 * math.pi)))
    grad_gate = (grad_mixed * up * slope).astype(BF)
    grad_up = (grad_mixed * active).astype(BF)
    act_ref[:, ACT_GU : ACT_GU + FF] = grad_gate
    act_ref[:, ACT_GU + FF : ACT_GU + 2 * FF] = grad_up
    grad_h = dot_nt(grad_gate, w_in[:, :FF]) + dot_nt(grad_up, w_in[:, FF:])
    gain_ref[...] = jnp.broadcast_to(
        jnp.sum(grad_h * unit, axis=0, keepdims=True), gain_ref.shape
    )
    grad_middle = cot_ref[...].astype(F32) + normalise_back(grad_h * gain, unit, scale)
    gmid_ref[...] = grad_middle
    gb = grad_middle.astype(BF)
    act_ref[:, ACT_GB : ACT_GB + D] = gb
    act_ref[:, ACT_COT : ACT_COT + D] = cot_ref[...]
    for j in range(TP):
        part = dot_nt(gb, w_out[pl.ds(starts[j], GW), :])
        pad = jnp.zeros((part.shape[0], 256 - GW), F32)
        gatts[j][...] = jnp.concatenate([pad, part], axis=1).astype(BF)
    result_ref[...] = middle + dot(mixed, w_down[...])


def up16(n):
    return -(-n // 16) * 16


def plan(shards):
    rows_d, rows_f = D // (4 * shards), FF // (4 * shards)
    return rows_d, rows_f, up16(rows_d), up16(rows_f)


def ffn_grads_kernel(shards, idx, own, got, gain_ref, *refs):
    ins = refs[:shards]
    mine_ref, other_ref = refs[shards : shards + 2]
    h_t, mixed_t, att_t, right = refs[shards + 2 :]
    z, x, c, y = idx[0], idx[1], idx[2], idx[3]
    rows_d, rows_f, pad_d, pad_f = plan(shards)
    n = own.shape[0]
    pieces, per = 4 * shards, GW // rows_d
    for i, act in enumerate((own, got)):
        at = slice(i * n, (i + 1) * n)
        h = act[:, ACT_H : ACT_H + D].T
        mixed = act[:, ACT_MIX : ACT_MIX + FF].T
        att = act[:, ACT_ATT : ACT_ATT + D].T
        for m in range(pieces):
            h_t[m, 0:rows_d, at] = h[m * rows_d : (m + 1) * rows_d]
            mixed_t[m, 0:rows_f, at] = mixed[m * rows_f : (m + 1) * rows_f]
            att_t[m, 0:rows_d, at] = att[m * rows_d : (m + 1) * rows_d]
        right[at, 0 : 2 * FF] = act[:, ACT_GU : ACT_GU + 2 * FF]
        right[at, 2 * FF : 2 * FF + D] = act[:, ACT_GB : ACT_GB + D]
        right[at, 2 * FF + D :] = act[:, ACT_COT : ACT_COT + D]
    for k in range(shards):
        piece = (lax.rem(y + k, shards) * 2 + c) * 2
        left = h_t[pl.ds(piece, 2)].reshape(2 * pad_d, 2 * n)
        grad = dot(left, right[:, 0 : 2 * FF]).astype(BF)
        for xx in range(2):
            for t in range(2 * FF // 128):
                ins[k][xx, t * pad_d : t * pad_d + rows_d, :] = grad[
                    xx * pad_d : xx * pad_d + rows_d, t * 128 : t * 128 + 128
                ]
    high = mine_ref.shape[1]
    gain = jnp.broadcast_to(gain_ref[0:1, :], (high - pad_f - pad_d, D)).astype(BF)
    for xx in range(2):
        for s in range(shards):
            piece = (s * 2 + c) * 2 + xx
            turned = lax.rem(piece // per - z + TP, TP) * per + lax.rem(piece, per)
            down = dot(mixed_t[piece], right[:, 2 * FF + D :]).astype(BF)
            out = dot(att_t[turned], right[:, 2 * FF : 2 * FF + D]).astype(BF)
            both = jnp.concatenate([down, out, gain], axis=0)

            @pl.when(x == xx)
            def _():
                mine_ref[s] = both

            @pl.when(x != xx)
            def _():
                other_ref[s] = both


def qkv_grads_kernel(shards, n_kv, idx, *refs):
    hs = refs[:n_kv]
    keep_ref, send_ref, dq_ref, w_ref, gains_ref, mine_ref, other_ref = refs[n_kv:]
    c = idx[2]
    total = None
    for i in range(n_kv):
        grads = (keep_ref if i < n_kv // 2 else send_ref)[i % (n_kv // 2)]
        part = dot(grads.T, hs[i][...])
        total = part if total is None else total + part
    grad = jnp.concatenate([total, dot(dq_ref[...].T, hs[0][...])], axis=0).T
    gain = gains_ref[...].T[:, 0:1]
    lane = lax.broadcasted_iota(jnp.int32, grad.shape, 1)
    by_gain = jnp.sum(grad * w_ref[...].astype(F32), axis=1, keepdims=True) / gain
    grad = jnp.where(lane < 3 * GW, grad, by_gain).astype(BF)
    height = plan(shards)[0]
    for s in range(shards):
        for cc in range(2):
            block = (s * 2 + cc) * 2 * height
            for xx in range(2):
                part = grad[block + xx * height : block + (xx + 1) * height]

                @pl.when(c == cc)
                def _():
                    mine_ref[s, xx] = part

                @pl.when(c != cc)
                def _():
                    other_ref[s, xx] = part


def h_one_grads_kernel(n_sum, idx, *refs):
    parts = refs[:n_sum]
    dq_ref, w_ref, gh_mine, gh_other = refs[n_sum:]
    rows = gh_mine.shape[1]
    for j in range(TP):
        at = slice(j * rows, (j + 1) * rows)
        total = parts[0][0, at, :].astype(F32)
        for part in parts[1:]:
            total += part[0, at, :].astype(F32)
        grad = jnp.concatenate([total.astype(BF), dq_ref[at, :]], axis=1)
        owner = lax.rem(idx[0] - j + TP, TP)
        target = gh_other if j % 2 else gh_mine
        target[owner // 2] = dot_nt(grad, w_ref[...]).astype(BF)


def tail_kernel(n_sum, idx, *refs):
    tok_ref, gmid_ref, gains_ref, out_ref = refs[n_sum:]
    unit, scale = normalise(tok_ref[...].astype(F32))
    total = 0.0
    for grad in refs[:n_sum]:
        grad = grad[idx[0] // 2] if len(grad.shape) == 3 else grad[...]
        total += grad.astype(F32)
    grad_unit = total * gains_ref[0:1, :]
    out_ref[...] = gmid_ref[...] + normalise_back(grad_unit, unit, scale)


def place_z(z, k):
    return lax.rem(z // 2 + k % 2, 2) * 2 + lax.rem(lax.rem(z, 2) + k // 2, 2)


def in_unpack_kernel(shards, idx, own, got, in_ref, held):
    rows_d, _, pad_d, _ = plan(shards)
    size = held.shape[0] // TP
    z, x, c = idx[0], idx[1], idx[2]
    for cr in range(2):
        for xr in range(2):
            for k in range(TP):
                at = pl.ds(pl.multiple_of(place_z(z, k) * size, size), size)
                held[at, :] = (got if cr else own)[xr, k].astype(F32)
            cc, xx = lax.rem(c + cr, 2), lax.rem(x + xr, 2)
            for t in range(2 * FF // 128):
                base = t * pad_d
                in_ref[cc, xx, :, t * 128 : t * 128 + 128] = held[base : base + rows_d, :]


def rest_unpack_kernel(shards, idx, own, got, out_ref, down_ref, gain_ref, held):
    rows_d, rows_f, pad_d, pad_f = plan(shards)
    size = held.shape[0] // TP
    z, x, c = idx[0], idx[1], idx[2]
    gain = None
    for cr in range(2):
        for xr in range(2):
            for k in range(TP):
                at = pl.ds(pl.multiple_of(place_z(z, k) * size, size), size)
                held[at, :] = (got if cr else own)[xr, k].astype(F32)
            cc, xx = lax.rem(c + cr, 2), lax.rem(x + xr, 2)
            down_ref[cc, xx] = held[0:rows_f, :]
            out_ref[cc, xx] = held[pad_f : pad_f + rows_d, :]
            if xr == 0:
                row = held[pad_f + pad_d : pad_f + pad_d + 8, :]
                gain = row if gain is None else gain + row
    part = gain_ref.shape[0]
    for s in range(shards):

        @pl.when(idx[3] == s)
        def _():
            gain_ref[...] = gain[0:1, s * part : (s + 1) * part].reshape(part)


def qkv_unpack_kernel(idx, own, got, out_ref, gain_ref, gain_s):
    z, x, c = idx[0], idx[1], idx[2]
    for cr in range(2):
        for xr in range(2):
            cc, xx = lax.rem(c + cr, 2), lax.rem(x + xr, 2)
            gain = None
            for g in range(TP):
                k = 2 * lax.rem(g % 2 + z, 2) + lax.rem(g // 2 + z // 2, 2)
                block = (got if cr else own)[xr, k].astype(F32)
                for source, place in ((0, 1), (1, 2), (2, 0)):
                    out_ref[cc, xx, :, place * D + g * GW : place * D + (g + 1) * GW] = block[
                        :, source * GW : (source + 1) * GW
                    ]
                tail = block[:, 512:640]
                gain = tail if gain is None else gain + tail
            height = gain.shape[0]
            at = pl.multiple_of((cc * 2 + xx) * height, height)
            gain_s[pl.ds(at, height), :] = gain
    gain_ref[...] = gain_s[...].T[64:65].reshape(gain_ref.shape)


def shift(value, axis, k):
    n = lax.axis_size(axis)
    return lax.ppermute(value, axis, [(i, (i + k) % n) for i in range(n)])


def gather(value, axis):
    return [value] + [shift(value, axis, k) for k in range(1, lax.axis_size(axis))]


def pick(value, index, dim):
    return lax.dynamic_index_in_dim(value, index, dim, keepdims=False)


def term(value, *views):
    return (value, views)


def take(index, dim):
    return lambda value: pick(value, index, dim)


def reshaped(*shape):
    return lambda value: value.reshape(shape)


def viewed(terms, view):
    return [(value, views + (view,)) for value, views in terms]


def reduce_step(order, terms, axis, dim):
    n, i = lax.axis_size(axis), lax.axis_index(axis)
    total = order.add(terms)
    got = [term(shift(pick(total, lax.rem(i + k, n), dim), axis, k)) for k in range(1, n)]
    return [term(pick(total, i, dim))] + got


def add(values):
    total = values[0].astype(F32)
    for value in values[1:]:
        total = total + value.astype(F32)
    return total.astype(BF)


def swap_z(value, bit):
    return lax.ppermute(value, "z", [(i, i ^ bit) for i in range(TP)])


def reduce_z(order, terms, bit):
    z = lax.axis_index("z")
    i, dim = (z % 2, 1) if bit == 1 else (z // 2, 0)
    total = order.add(terms)
    return [term(pick(total, i, dim)), term(swap_z(pick(total, 1 - i, dim), bit))]


def gather_z(order, value, bit):
    value = order.step(value)
    got = swap_z(value, bit)
    return jnp.stack([value, got]) if bit == 2 else jnp.concatenate([value, got])


def sum_over(value, axis):
    return add([value] + [shift(value, axis, k) for k in range(1, lax.axis_size(axis))])


def after(value, *others):
    return lax.optimization_barrier((value, *others))[0]


class Order:
    def __init__(self):
        self.last = None

    def __call__(self, values):
        if self.last is None:
            return values
        return lax.optimization_barrier((values, self.last))[0]

    def step(self, value):
        self.last = self(value)
        return self.last

    def add(self, terms):
        values = []
        for value, (_, views) in zip(self([t[0] for t in terms]), terms):
            for view in views:
                value = view(value)
            values.append(value)
        self.last = add(values)
        return self.last

    def run(self, body, outs, n_smem, ins, **more):
        got = call(body, outs, n_smem, self(list(ins)), **more)
        self.last = got[0]
        return got


def per_device(tokens, gain_one, w_qkv, w_out, gain_two, w_in, w_down, cotangent):
    tok, cot = tokens[0], cotangent[0]
    rows = tok.shape[0]
    many = TP * rows
    zo, z = lax.axis_index("zo"), lax.axis_index("z")
    x, c, y = lax.axis_index("x"), lax.axis_index("core"), lax.axis_index("shard")
    outer, shards = lax.axis_size("zo"), lax.axis_size("shard")
    part = w_qkv.shape[0]
    n_kv = 4 * outer
    keys = n_kv * many
    rows_d, rows_f, pad_d, pad_f = plan(shards)
    high_in, high = 2 * FF // 128 * pad_d, -(-(pad_f + pad_d + 16) // 64) * 64
    i32 = jnp.int32
    idx = jnp.stack([z, x, c, y]).astype(i32)
    order = Order()

    toks = gather(tok, "z")
    w_own, w_mine = order.run(
        group_kernel,
        [((part, WC), BF), ((part // 2 + 16, WC), BF)],
        1,
        [idx, w_qkv, gain_one, gain_two],
        hbm_ins=(1, 2, 3),
        name="group_columns",
    )
    w_slices = [w_own]
    for k in range(1, shards):
        w_slices.append(shift(w_mine, "shard", k))
        w_slices.append(shift(w_slices[-1], "core", 1))
    pack, pack_down = order.run(
        pack_kernel,
        [((2 * part, D), BF), ((down_half(down_half(w_down.shape[0])[0])[0], D), BF)],
        1,
        [idx, w_out, w_in, w_down],
        hbm_ins=(1, 2, 3),
        name="pack_weights",
    )
    downs = [shift(pack_down, "shard", k) for k in range(1, shards)]
    packs = [shift(pack, "shard", k) for k in range(1, shards)]

    freq = THETA ** (-jnp.arange(HEAD_DIM // 2, dtype=F32) * (2.0 / HEAD_DIM))
    owners = lax.rem(z - jnp.arange(TP, dtype=i32) + TP, TP)
    places = []
    for cr in range(2):
        for xr in range(2):
            for zr in range(outer):
                zz = lax.rem(zo - zr + outer, outer)
                place = ((zz * TP + owners) * 2 + lax.rem(x + xr, 2)) * 2 + lax.rem(c + cr, 2)
                places.append(place)
    first_place = jnp.concatenate(places) * rows
    freq = jnp.tile(freq, 4)[None, :]
    sign = jnp.where(jnp.arange(128) % 64 < 32, -1.0, 1.0).astype(F32)
    start = first_place.astype(F32)[:, None] * freq
    step = jnp.arange(rows, dtype=i32).astype(F32)[:, None] * freq
    cos_a, sin_a = jnp.cos(start)[:, None], jnp.sin(start)[:, None]
    cos_b, sin_b = jnp.cos(step)[None], jnp.sin(step)[None]
    cosine = (cos_a * cos_b - sin_a * sin_b).reshape(keys, 128)
    sine = ((sin_a * cos_b + cos_a * sin_b) * sign).reshape(keys, 128)

    query, kv, h_one, w_full, gains = order.run(
        functools.partial(front_kernel, shards),
        [
            ((many, 256), BF),
            ((many, 2 * GW), BF),
            ((many, D), BF),
            ((D, WC), BF),
            ((8, D), F32),
        ],
        1,
        [idx, *toks, *w_slices, w_mine, cosine, sine],
        hbm_ins=range(1, 1 + TP + len(w_slices) + 3),
        hbm_outs=(2, 3, 4),
        name="front",
    )

    near = gather(kv, "zo")
    near = near + [shift(v, "x", 1) for v in near]
    kv_core = shift(kv, "core", 1)
    close = (0, n_kv // 2)
    far = [i for i in range(n_kv) if i not in close]
    scratch = lambda count: [
        pltpu.VMEM((count * many, 2 * GW), BF),
        pltpu.VMEM((256, count * many), BF),
        pltpu.VMEM((256, many), BF),
    ]
    first = order.run(
        functools.partial(forward_kernel, 2, False),
        [((GW, many), F32), ((8, many), F32)],
        0,
        [query, kv, kv_core],
        scratch=scratch(2),
        name="attention_forward_near",
    )
    kvs = near + [kv_core] + [shift(after(v, *first), "core", 1) for v in near[1:]]
    downs = [jnp.stack([v, swap_z(v, 1)]) for v in downs]
    both_down = [v for p in downs for v in (p, shift(p, "core", 1))]
    first = [first[0], after(first[1], *both_down)]
    att = order.run(
        functools.partial(forward_kernel, len(far), True),
        [((rows, GW), BF)] * TP + [((GW, many), F32), ((8, many), F32)],
        0,
        [query, *[kvs[i] for i in far], *first],
        scratch=scratch(len(far)),
        hbm_outs=(TP, TP + 1),
        name="attention_forward_far",
    )
    att_blocks, (attended_t, lse) = att[:TP], att[TP:]
    h_near = gather(after(h_one, lse), "zo")
    h_near = h_near + [shift(v, "x", 1) for v in h_near]
    h_core = shift(after(h_one, lse), "core", 1)
    atts = [att_blocks[0]] + [shift(att_blocks[k], "z", -k) for k in range(1, TP)]

    packs = [after(p, lse) for p in packs]
    both = [v for p in packs for v in (p, shift(p, "core", 1))]
    mid = order.run(
        functools.partial(middle_kernel, len(both)),
        [((rows, D), F32), ((rows, D), F32), ((rows, ACT_ALL), BF), ((8, D), F32)]
        + [((rows, 256), BF)] * TP,
        1,
        [idx, *atts, tok, cot, after(gains, h_core), w_out, w_in, w_down, *both, *both_down],
        scratch=[
            pltpu.VMEM((D, D), BF),
            pltpu.VMEM((D, 2 * FF), BF),
            pltpu.VMEM((FF, D), BF),
            pltpu.SemaphoreType.DMA((3 + 6 * len(both),)),
        ],
        any_ins=range(1 + TP + 3, 1 + TP + 6 + 2 * len(both)),
        hbm_ins=(1 + TP, 2 + TP, 3 + TP),
        hbm_outs=(0, 1, 3),
        name="feed_forward",
    )
    result, grad_middle, act, gain_two_row = mid[:4]
    act = after(act, *h_near)
    gatts = mid[4:]
    gas = [gatts[0]] + [shift(gatts[k], "z", k) for k in range(1, TP)]

    hs = h_near + [h_core] + [shift(after(v, result), "core", 1) for v in h_near[1:]]
    gain_two_row = after(gain_two_row, *hs)
    ffn = order.run(
        functools.partial(ffn_grads_kernel, shards),
        [((2, high_in, 128), BF)] * shards
        + [((shards, high, D), BF)] * 2,
        1,
        [idx, act, shift(act, "core", 1), gain_two_row],
        scratch=[
            pltpu.VMEM((4 * shards, pad_d, 2 * rows), BF),
            pltpu.VMEM((4 * shards, pad_f, 2 * rows), BF),
            pltpu.VMEM((4 * shards, pad_d, 2 * rows), BF),
            pltpu.VMEM((2 * rows, 2 * FF + 2 * D), BF),
        ],
        hbm_outs=range(shards + 2),
        name="ffn_weight_grads",
    )
    f_in = [term(ffn[0])]
    f_in += [term(shift(after(ffn[k], *gas), "shard", k)) for k in range(1, shards)]
    f_rest = [term(ffn[shards]), term(shift(after(ffn[shards + 1], *gas), "x", 1))]

    dkv_keep, dkv_send, dq = order.run(
        functools.partial(backward_kernel, n_kv),
        [((n_kv // 2, many, 2 * GW), BF)] * 2 + [((many, 256), BF)],
        0,
        [query, *kvs, *gas, attended_t, lse, cosine, sine],
        scratch=[
            pltpu.VMEM((keys, 2 * GW), BF),
            pltpu.VMEM((256, keys), BF),
            pltpu.VMEM((256, many), BF),
            pltpu.VMEM((256, many), BF),
            pltpu.VMEM((many, 2 * GW), BF),
            pltpu.VMEM((many, 2 * GW), BF),
            pltpu.VMEM((keys, 2 * GW), F32),
            pltpu.VMEM((256, many), F32),
        ],
        hbm_ins=range(0, 1 + n_kv + TP + 4),
        name="attention_backward",
    )
    mine, other = order.run(
        functools.partial(qkv_grads_kernel, shards, n_kv),
        [((shards, 2, rows_d, WC), BF)] * 2,
        1,
        [idx, *hs, dkv_keep, dkv_send, dq, w_full, gains],
        hbm_ins=range(1, 1 + n_kv),
        name="qkv_weight_grads",
    )
    first_got = [t[0] for t in f_in[1:] + f_rest[1:]]
    mine, other, *_ = lax.optimization_barrier((mine, other, *first_got))
    order.last = mine
    terms = [term(dkv_keep), term(shift(after(dkv_send, mine), "core", 1))]
    terms = viewed(terms, reshaped(2, outer, many, 2 * GW))
    wq = [term(mine), term(shift(other, "core", 1))]

    def pair(value):
        return jnp.stack([value, shift(order.step(value), "x", 1)])

    f_in = reduce_step(order, f_in, "x", 0)
    f_rest = reduce_step(order, f_rest, "shard", 0)
    wq = reduce_step(order, wq, "shard", 0)
    got = shift(order.add(viewed(terms, take(1, 0))), "x", 1)
    terms = viewed(terms, take(0, 0)) + [term(got)]
    f_in = reduce_z(order, viewed(f_in, reshaped(2, 2, high_in // TP, 128)), 1)
    f_rest = reduce_z(order, viewed(f_rest, reshaped(2, 2, high // TP, D)), 1)
    wq = reduce_step(order, wq, "x", 0)
    f_in = reduce_z(order, f_in, 2)
    f_rest = reduce_z(order, f_rest, 2)
    wq = gather_z(order, sum_over(order.add(wq), "zo"), 2)
    f_in = gather_z(order, sum_over(order.add(f_in), "zo"), 2)
    f_rest = gather_z(order, sum_over(order.add(f_rest), "zo"), 2)

    wq = gather_z(order, wq, 1)
    f_in = gather_z(order, f_in, 1)
    f_rest = gather_z(order, f_rest, 1)
    if outer > 1:
        total = order.add(terms)
        sums = [total[0:1]] + [shift(total[k : k + 1], "zo", -k) for k in range(1, outer)]
    else:
        sums = [
            dkv_keep.reshape(2, many, 2 * GW),
            terms[1][0].reshape(2, many, 2 * GW),
            got.reshape(1, many, 2 * GW),
        ]
    gh, gh_other = order.run(
        functools.partial(h_one_grads_kernel, len(sums)),
        [((2, rows, D), BF)] * 2,
        1,
        [idx, *sums, dq, w_full],
        name="h_one_grads",
    )
    wq = pair(wq)
    f_in = pair(after(f_in, f_rest))
    gh = [term(gh), term(swap_z(order(gh_other), 1))]
    wq = order.step(wq)
    wq_got = shift(wq, "core", 1)
    f_rest = pair(f_rest)
    gh = reduce_z(order, gh, 2)
    g_qkv, grad_gain_one = order.run(
        qkv_unpack_kernel,
        [((2, 2, rows_d, 3 * D), F32), ((part,), F32)],
        1,
        [idx, wq, wq_got],
        scratch=[pltpu.VMEM((part, 128), F32)],
        name="qkv_unpack",
    )
    f_in = order.step(f_in)
    f_in_got = shift(f_in, "core", 1)
    f_rest = order.step(after(f_rest, gh[1][0]))
    f_rest_got = shift(f_rest, "core", 1)
    (g_in,) = order.run(
        functools.partial(in_unpack_kernel, shards),
        [((2, 2, rows_d, 2 * FF), F32)],
        1,
        [idx, f_in, f_in_got],
        scratch=[pltpu.VMEM((high_in, 128), F32)],
        name="w_in_unpack",
    )
    (grad_tokens,) = order.run(
        functools.partial(tail_kernel, len(gh)),
        [((rows, D), F32)],
        1,
        [idx, *[t[0] for t in gh], tok, grad_middle, gains],
        name="token_grads",
    )

    g_out, g_down, grad_gain_two = order.run(
        functools.partial(rest_unpack_kernel, shards),
        [
            ((2, 2, rows_d, D), F32),
            ((2, 2, rows_f, D), F32),
            ((part,), F32),
        ],
        1,
        [idx, f_rest, f_rest_got],
        scratch=[pltpu.VMEM((high, D), F32)],
        name="w_down_w_out_unpack",
    )
    return (
        result[None],
        grad_tokens[None],
        grad_gain_one,
        g_qkv.reshape(part, 3 * D),
        g_out.reshape(part, D),
        grad_gain_two,
        g_in.reshape(part, 2 * FF),
        g_down.reshape(w_down.shape[0], D),
    )


def solution(mesh):
    blocks = mesh.shape["ctx"]
    fine = Mesh(
        mesh.devices.reshape(blocks // (TP * 4), TP, 2, 2, mesh.shape["shard"]), CTX + ("shard",)
    )
    rows, split = P("shard", CTX, None), P("shard", None)
    return jax.shard_map(
        per_device,
        mesh=fine,
        in_specs=(rows, P("shard"), split, split, P("shard"), split, split, rows),
        out_specs=(rows, rows, P("shard"), split, split, P("shard"), split, split),
        check_vma=False,
    )
```

```python
import functools
import math

import jax
import jax.numpy as jnp
from jax import lax
from jax.experimental import pallas as pl
from jax.experimental.pallas import tpu as pltpu
from jax.sharding import Mesh, PartitionSpec as P

D = 768
HEADS = 12
HEAD_DIM = 64
FF = 1152
EPS = 1e-05
THETA = 160000.0

TP = 4
GH = HEADS // TP
GW = GH * HEAD_DIM
WC = 640
CTX = ("zo", "z", "x", "core")
BF = jnp.bfloat16
F32 = jnp.float32
VMEM_LIMIT = 32 * 1024 * 1024

KEY_AT = ((0, 0), (0, 1), (1, 0))
VALUE_AT = ((1, 1), (2, 0), (2, 1))


def dot(a, b):
    return jnp.dot(a, b, preferred_element_type=F32)


def dot_nt(a, b):
    return lax.dot_general(a, b, (((1,), (1,)), ((), ())), preferred_element_type=F32)


def dot_tn(a, b):
    return lax.dot_general(a, b, (((0,), (0,)), ((), ())), preferred_element_type=F32)


def call(body, outs, n_smem, ins, scratch=(), any_ins=(), hbm_ins=(), hbm_outs=(), name=None):
    specs, values = [], []
    for i, value in enumerate(ins):
        space = pltpu.SMEM if i < n_smem else (pl.ANY if i in any_ins else pltpu.VMEM)
        if i in hbm_ins:
            value = pltpu.with_memory_space_constraint(value, pltpu.HBM)
        specs.append(pl.BlockSpec(memory_space=space))
        values.append(value)
    shapes = []
    for i, (shape, kind) in enumerate(outs):
        shapes.append(pltpu.HBM(shape, kind) if i in hbm_outs else jax.ShapeDtypeStruct(shape, kind))
    return pl.pallas_call(
        body,
        out_shape=shapes,
        in_specs=specs,
        out_specs=[pl.BlockSpec(memory_space=pltpu.VMEM)] * len(outs),
        scratch_shapes=list(scratch),
        compiler_params=pltpu.CompilerParams(vmem_limit_bytes=VMEM_LIMIT),
        cost_estimate=pl.CostEstimate(flops=1, bytes_accessed=1, transcendentals=0),
        name=name,
    )(*values)


def normalise(values):
    mean = jnp.mean(values, axis=-1, keepdims=True)
    centred = values - mean
    spread = jnp.mean(centred * centred, axis=-1, keepdims=True)
    scale = lax.rsqrt(spread + EPS)
    return centred * scale, scale


def normalise_back(grad_unit, unit, scale):
    return scale * (
        grad_unit
        - jnp.mean(grad_unit, axis=-1, keepdims=True)
        - unit * jnp.mean(grad_unit * unit, axis=-1, keepdims=True)
    )


def turn(tile, cosine, signed_sine, first_half):
    swapped = jnp.where(first_half, pltpu.roll(tile, 96, 1), pltpu.roll(tile, 32, 1))
    return tile * cosine + swapped * signed_sine


def lane_masks(rows):
    lane = lax.broadcasted_iota(jnp.int32, (rows, 128), 1)
    return lax.rem(lane, 64) < 32, lane < 64


def group_kernel(idx, w_ref, one_ref, two_ref, own_ref, half_ref):
    height = w_ref.shape[0]
    half = height // 2
    for g in range(TP):

        @pl.when(idx[0] == g)
        def _():
            parts = [w_ref[:, p * D + g * GW : p * D + (g + 1) * GW] for p in (1, 2, 0)]
            parts.append(jnp.zeros((height, WC - 3 * GW), BF))
            own_ref[...] = jnp.concatenate(parts, axis=1)

    half_ref[0:half, :] = own_ref[pl.ds(pl.multiple_of(idx[2] * half, half), half), :]
    half_ref[half:, :] = jnp.zeros((16, WC), BF)
    half_ref[half : half + 1, 0:height] = one_ref[...].reshape(1, height)
    half_ref[half + 1 : half + 2, 0:height] = two_ref[...].reshape(1, height)


def pack_kernel(idx, out_ref, in_ref, down_ref, pack_ref, pack_down):
    c = idx[2]
    half = out_ref.shape[0] // 2
    at = pl.ds(pl.multiple_of(c * half, half), half)
    pack_ref[0:half, :] = out_ref[at, :]
    for b in range(3):
        pack_ref[(1 + b) * half : (2 + b) * half, :] = in_ref[at, b * D : (b + 1) * D]
    count, step = down_half(down_ref.shape[0])
    quarter, hop = down_half(count)
    at = pl.multiple_of(c * step + lax.rem(idx[0], 2) * hop, 16)
    pack_down[...] = down_ref[pl.ds(at, quarter), :]


def down_half(height):
    count = -(-height // 32) * 16
    return count, height - count


def front_kernel(shards, idx, *refs):
    toks = refs[:TP]
    n_w = 2 * shards - 1
    ws = refs[TP : TP + n_w]
    mine, cos_ref, sin_ref, q_ref, kv_ref, h_ref, w_ref, gains_ref = refs[TP + n_w :]
    c, y = idx[2], idx[3]
    rows = toks[0].shape[0]
    part = ws[0].shape[0]
    half = part // 2
    gains_ref[...] = jnp.zeros_like(gains_ref)
    for k in range(shards):
        start = lax.rem(y - k + shards, shards) * part
        at = pl.ds(pl.multiple_of(start, part), part)
        if k == 0:
            w_ref[at, :] = ws[0][...]
            continue
        at = pl.ds(pl.multiple_of(start + c * half, half), half)
        w_ref[at, :] = ws[2 * k - 1][0:half]
        at = pl.ds(pl.multiple_of(start + (1 - c) * half, half), half)
        w_ref[at, :] = ws[2 * k][0:half]
    for s in range(shards):

        @pl.when(y == s)
        def _():
            for k in range(shards):
                start = (s - k) % shards * part
                gains = (ws[2 * k - 1] if k else mine)[half : half + 2, 0:part]
                gains_ref[0:2, start : start + part] = gains.astype(F32)

    gain = gains_ref[0:1, :]
    first, low = lane_masks(rows)
    for j in range(TP):
        at = slice(j * rows, (j + 1) * rows)
        unit, _ = normalise(toks[j][...].astype(F32))
        h = (unit * gain).astype(BF)
        h_ref[at, :] = h
        out = dot(h, w_ref[...])
        cosine, sine = cos_ref[at, :], sin_ref[at, :]
        key_a = turn(out[:, 0:128], cosine, sine, first)
        mixed = out[:, 128:256]
        key_b = jnp.where(low, turn(mixed, cosine, sine, first), mixed)
        kv_ref[at, 0:128] = key_a.astype(BF)
        kv_ref[at, 128:256] = key_b.astype(BF)
        kv_ref[at, 256:384] = out[:, 256:384].astype(BF)
        query_a = turn(out[:, 384:512], cosine, sine, first)
        query_b = jnp.where(low, turn(out[:, 512:640], cosine, sine, first), 0.0)
        factor = HEAD_DIM ** (-0.5)
        q_ref[at, 0:128] = (query_a * factor).astype(BF)
        q_ref[at, 128:256] = (query_b * factor).astype(BF)


def half_rows(values_t, head):
    at = head * HEAD_DIM
    rows = values_t[at : at + HEAD_DIM]
    zeros = jnp.zeros_like(rows)
    return jnp.concatenate([rows, zeros] if head % 2 == 0 else [zeros, rows], axis=0)


def fold(values):
    half = values.shape[0] // 2
    rest = values[:, 128:192]
    return jnp.concatenate([values[:, 0:128], jnp.concatenate([rest[:half], rest[half:]], axis=1)])


def unfold(values):
    rows = values.shape[0] * 2 // 3
    rest = values[rows:]
    rest = jnp.concatenate([rest[:, 0:64], rest[:, 64:128]])
    return jnp.concatenate([values[:rows], rest], axis=1)


def forward_kernel(n_kv, last, q_ref, *refs):
    kvs = refs[:n_kv]
    if last:
        before_ref, before_lse = refs[n_kv : n_kv + 2]
        atts = refs[n_kv + 2 : n_kv + 2 + TP]
    att_t_ref, lse_ref, kv_s, v_t, q_t = refs[-5:]
    rows = kvs[0].shape[0]
    block = math.gcd(rows, 256)
    for i, kv in enumerate(kvs):
        kv_s[i * rows : (i + 1) * rows, :] = kv[...]
        v_t[:, i * rows : (i + 1) * rows] = kv[:, 128:384].T
    q_t[...] = q_ref[...].T
    lse_ref[...] = jnp.zeros_like(lse_ref)
    for i in range(rows // block):
        at = slice(i * block, (i + 1) * block)
        for h in range(GH):
            tile = KEY_AT[h][0]
            keys = kv_s[:, tile * 128 : tile * 128 + 128]
            scores = dot(keys, half_rows(q_t[:, at], h))
            top = jnp.max(scores, axis=0, keepdims=True)
            weights = jnp.exp(scores - top)
            total = jnp.sum(weights, axis=0, keepdims=True)
            tile, half = VALUE_AT[h]
            values_t = v_t[(tile - 1) * 128 : tile * 128, :]
            out = dot(values_t, weights.astype(BF))[half * 64 : half * 64 + 64]
            head = slice(h * 64, h * 64 + 64)
            if last:
                old = before_lse[h : h + 1, at]
                high = jnp.maximum(old, top)
                share, own = jnp.exp(old - high), jnp.exp(top - high)
                total = total * own + share
                out = out * own + before_ref[head, at] * share
                top = high
            att_t_ref[head, at] = out / total
            lse_ref[h : h + 1, at] = top + jnp.log(total)
    if last:
        small = rows // TP
        for j in range(TP):
            atts[j][...] = fold(att_t_ref[:, j * small : (j + 1) * small].T.astype(BF))


def backward_kernel(n_kv, q_ref, *refs):
    kvs = refs[:n_kv]
    gas = refs[n_kv : n_kv + TP]
    att_t_ref, lse_ref = refs[n_kv + TP : n_kv + TP + 2]
    tables = refs[n_kv + TP + 2 : n_kv + TP + 4]
    keep_ref, send_ref, dq_ref = refs[n_kv + TP + 4 : n_kv + TP + 7]
    kv_s, k_t, q_t, g_t, q_m, g_m, acc, dq_t = refs[n_kv + TP + 7 :]
    rows = kvs[0].shape[0]
    small = gas[0].shape[0]
    block = math.gcd(rows, 256)
    for i, kv in enumerate(kvs):
        kv_s[i * rows : (i + 1) * rows, :] = kv[...]
        k_t[:, i * rows : (i + 1) * rows] = kv[:, 0:256].T
    q_t[...] = q_ref[...].T
    _, low = lane_masks(small)
    for j in range(TP):
        at = slice(j * small, (j + 1) * small)
        g_t[:, at] = gas[j][...].T
        first, second = gas[j][:, 0:128], gas[j][:, 128:256].astype(F32)
        g_m[at, 0:128] = first
        g_m[at, 128:256] = jnp.where(low, second, 0.0).astype(BF)
        g_m[at, 256:384] = jnp.where(low, 0.0, second).astype(BF)
        both = q_ref[at, 0:128].astype(F32)
        q_m[at, 0:128] = jnp.where(low, both, 0.0).astype(BF)
        q_m[at, 128:256] = jnp.where(low, 0.0, both).astype(BF)
        q_m[at, 256:384] = q_ref[at, 128:256]
    dq_t[...] = jnp.zeros_like(dq_t)
    acc[...] = jnp.zeros_like(acc)
    for i in range(rows // block):
        at = slice(i * block, (i + 1) * block)
        for h in range(GH):
            ktile, khalf = KEY_AT[h]
            vtile = VALUE_AT[h][0]
            klanes = slice(ktile * 128, ktile * 128 + 128)
            vlanes = slice(vtile * 128, vtile * 128 + 128)
            scores = dot(kv_s[:, klanes], half_rows(q_t[:, at], h))
            probs = jnp.exp(scores - lse_ref[h : h + 1, at])
            grad_t = half_rows(g_t[:, at], h + 1)
            grad_probs = dot(kv_s[:, vlanes], grad_t)
            own = g_t[(h + 1) * 64 : (h + 2) * 64, at].astype(F32)
            inner = jnp.sum(
                own * att_t_ref[h * 64 : h * 64 + 64, at], axis=0, keepdims=True
            )
            grad_scores = (probs * (grad_probs - inner)).astype(BF)
            lanes = slice(h * 128, h * 128 + 128)
            acc[:, vlanes] += dot(probs.astype(BF), g_m[at, lanes])
            acc[:, klanes] += dot(grad_scores, q_m[at, lanes])
            part = dot(k_t[klanes, :], grad_scores)[khalf * 64 : khalf * 64 + 64]
            dq_t[h * 64 : h * 64 + 64, at] = part * HEAD_DIM ** (-0.5)
    first, low = lane_masks(rows)
    cosine, sine = tables[0][0:rows, :], -tables[1][0:rows, :]
    grad_q = dq_t[...].T
    for t in range(2):
        lanes = slice(t * 128, t * 128 + 128)
        dq_ref[:, lanes] = turn(grad_q[:, lanes], cosine, sine, first).astype(BF)
    for i in range(n_kv):
        at = slice(i * rows, (i + 1) * rows)
        cosine, sine = tables[0][at, :], -tables[1][at, :]
        target = keep_ref if i < n_kv // 2 else send_ref
        block = i % (n_kv // 2)
        grad = acc[at, 0:128]
        target[block, :, 0:128] = turn(grad, cosine, sine, first).astype(BF)
        grad = acc[at, 128:256]
        grad = jnp.where(low, turn(grad, cosine, sine, first), grad)
        target[block, :, 128:256] = grad.astype(BF)
        target[block, :, 256:384] = acc[at, 256:384].astype(BF)


ACT_H, ACT_MIX, ACT_GU, ACT_GB, ACT_ATT, ACT_COT, ACT_ALL = (
    0, D, D + FF, D + 3 * FF, 2 * D + 3 * FF, 3 * D + 3 * FF, 4 * D + 3 * FF
)


def middle_kernel(n_packs, idx, *refs):
    atts = refs[:TP]
    tok_ref, cot_ref, gains_ref, out_own, in_own, down_own = refs[TP : TP + 6]
    packs = refs[TP + 6 : TP + 6 + n_packs]
    down_packs = refs[TP + 6 + n_packs : TP + 6 + 2 * n_packs]
    rest = refs[TP + 6 + 2 * n_packs :]
    result_ref, gmid_ref, act_ref, gain_ref = rest[:4]
    gatts = rest[4 : 4 + TP]
    w_out, w_in, w_down, sems = rest[4 + TP :]
    half = out_own.shape[0] // 2
    count, step = down_half(down_own.shape[0])

    def rows(start, height):
        return pl.ds(pl.multiple_of(start, 16), height)

    z, c, y = idx[0], idx[2], idx[3]
    shards = n_packs // 2 + 1
    own, own_down = y * 2 * half, y * down_own.shape[0]
    outs = [pltpu.make_async_copy(out_own, w_out.at[rows(own, 2 * half), :], sems.at[0])]
    ins = [pltpu.make_async_copy(in_own, w_in.at[rows(own, 2 * half), :], sems.at[1])]
    target = w_down.at[rows(own_down, down_own.shape[0]), :]
    downs = [pltpu.make_async_copy(down_own, target, sems.at[2])]
    for i, pack in enumerate(packs):
        shard = lax.rem(y - (i // 2 + 1) + shards, shards)
        core = 1 - c if i % 2 else c
        at = rows((shard * 2 + core) * half, half)
        source = pack.at[0:half, :]
        outs.append(pltpu.make_async_copy(source, w_out.at[at, :], sems.at[3 + 6 * i]))
        for b in range(3):
            source = pack.at[(1 + b) * half : (2 + b) * half, :]
            target = w_in.at[at, b * D : (b + 1) * D]
            ins.append(pltpu.make_async_copy(source, target, sems.at[4 + 6 * i + b]))
        quarter, hop = down_half(count)
        for b in range(2):
            parity = lax.rem(z + b, 2)
            at = rows(shard * down_own.shape[0] + core * step + parity * hop, quarter)
            source = down_packs[i].at[b]
            downs.append(pltpu.make_async_copy(source, w_down.at[at, :], sems.at[7 + 6 * i + b]))
    apart = 4 * down_half(count)[0] == down_own.shape[0]
    for copy in outs + ins + (downs if apart else downs[:1]):
        copy.start()
    starts = [pl.multiple_of(lax.rem(z + j, TP) * GW, GW) for j in range(TP)]
    for copy in outs:
        copy.wait()
    middle = tok_ref[...].astype(F32)
    for j in range(TP):
        att = unfold(atts[j][...])
        middle += dot(att, w_out[pl.ds(starts[j], GW), :])
        act_ref[:, ACT_ATT + j * GW : ACT_ATT + (j + 1) * GW] = att
    gain = gains_ref[1:2, :]
    unit, scale = normalise(middle)
    h = (unit * gain).astype(BF)
    act_ref[:, ACT_H : ACT_H + D] = h
    for copy in ins:
        copy.wait()
    gate = dot(h, w_in[:, :FF])
    up = dot(h, w_in[:, FF:])
    phi = 0.5 * (1.0 + lax.erf(gate * math.sqrt(0.5)))
    active = gate * phi
    mixed = (active * up).astype(BF)
    act_ref[:, ACT_MIX : ACT_MIX + FF] = mixed
    for i, copy in enumerate(downs):
        if i and not apart:
            copy.start()
        copy.wait()
    grad_mixed = dot_nt(cot_ref[...], w_down[...])
    slope = phi + gate * (jnp.exp(-0.5 * gate * gate) * (1.0 / math.sqrt(2.0 * math.pi)))
    grad_gate = (grad_mixed * up * slope).astype(BF)
    grad_up = (grad_mixed * active).astype(BF)
    act_ref[:, ACT_GU : ACT_GU + FF] = grad_gate
    act_ref[:, ACT_GU + FF : ACT_GU + 2 * FF] = grad_up
    grad_h = dot_nt(grad_gate, w_in[:, :FF]) + dot_nt(grad_up, w_in[:, FF:])
    gain_ref[...] = jnp.broadcast_to(
        jnp.sum(grad_h * unit, axis=0, keepdims=True), gain_ref.shape
    )
    grad_middle = cot_ref[...].astype(F32) + normalise_back(grad_h * gain, unit, scale)
    gmid_ref[...] = grad_middle
    gb = grad_middle.astype(BF)
    act_ref[:, ACT_GB : ACT_GB + D] = gb
    act_ref[:, ACT_COT : ACT_COT + D] = cot_ref[...]
    for j in range(TP):
        part = dot_nt(gb, w_out[pl.ds(starts[j], GW), :])
        pad = jnp.zeros((part.shape[0], 256 - GW), F32)
        gatts[j][...] = jnp.concatenate([pad, part], axis=1).astype(BF)
    result_ref[...] = middle + dot(mixed, w_down[...])


def up16(n):
    return -(-n // 16) * 16


def plan(shards):
    rows_d, rows_f = D // (4 * shards), FF // (4 * shards)
    return rows_d, rows_f, up16(rows_d), up16(rows_f)


def ffn_grads_kernel(shards, idx, own, got, gain_ref, *refs):
    ins = refs[:shards]
    mine_ref, other_ref = refs[shards : shards + 2]
    h_t, mixed_t, att_t, right = refs[shards + 2 :]
    z, x, c, y = idx[0], idx[1], idx[2], idx[3]
    rows_d, rows_f, pad_d, pad_f = plan(shards)
    n = own.shape[0]
    pieces, per = 4 * shards, GW // rows_d
    for i, act in enumerate((own, got)):
        at = slice(i * n, (i + 1) * n)
        h = act[:, ACT_H : ACT_H + D].T
        mixed = act[:, ACT_MIX : ACT_MIX + FF].T
        att = act[:, ACT_ATT : ACT_ATT + D].T
        for m in range(pieces):
            h_t[m, 0:rows_d, at] = h[m * rows_d : (m + 1) * rows_d]
            mixed_t[m, 0:rows_f, at] = mixed[m * rows_f : (m + 1) * rows_f]
            att_t[m, 0:rows_d, at] = att[m * rows_d : (m + 1) * rows_d]
        right[at, 0 : 2 * FF] = act[:, ACT_GU : ACT_GU + 2 * FF]
        right[at, 2 * FF : 2 * FF + D] = act[:, ACT_GB : ACT_GB + D]
        right[at, 2 * FF + D :] = act[:, ACT_COT : ACT_COT + D]
    for k in range(shards):
        piece = (lax.rem(y + k, shards) * 2 + c) * 2
        left = h_t[pl.ds(piece, 2)].reshape(2 * pad_d, 2 * n)
        grad = dot(left, right[:, 0 : 2 * FF]).astype(BF)
        for xx in range(2):
            for t in range(2 * FF // 128):
                ins[k][xx, t * pad_d : t * pad_d + rows_d, :] = grad[
                    xx * pad_d : xx * pad_d + rows_d, t * 128 : t * 128 + 128
                ]
    high = mine_ref.shape[1]
    gain = jnp.broadcast_to(gain_ref[0:1, :], (high - pad_f - pad_d, D)).astype(BF)
    for xx in range(2):
        for s in range(shards):
            piece = (s * 2 + c) * 2 + xx
            turned = lax.rem(piece // per - z + TP, TP) * per + lax.rem(piece, per)
            down = dot(mixed_t[piece], right[:, 2 * FF + D :]).astype(BF)
            out = dot(att_t[turned], right[:, 2 * FF : 2 * FF + D]).astype(BF)
            both = jnp.concatenate([down, out, gain], axis=0)

            @pl.when(x == xx)
            def _():
                mine_ref[s] = both

            @pl.when(x != xx)
            def _():
                other_ref[s] = both


def qkv_grads_kernel(shards, n_kv, idx, *refs):
    hs = refs[:n_kv]
    keep_ref, send_ref, dq_ref, w_ref, gains_ref, mine_ref, other_ref = refs[n_kv:]
    c = idx[2]
    total = None
    for i in range(n_kv):
        grads = (keep_ref if i < n_kv // 2 else send_ref)[i % (n_kv // 2)]
        part = dot(grads.T, hs[i][...])
        total = part if total is None else total + part
    grad = jnp.concatenate([total, dot(dq_ref[...].T, hs[0][...])], axis=0).T
    gain = gains_ref[...].T[:, 0:1]
    lane = lax.broadcasted_iota(jnp.int32, grad.shape, 1)
    by_gain = jnp.sum(grad * w_ref[...].astype(F32), axis=1, keepdims=True) / gain
    grad = jnp.where(lane < 3 * GW, grad, by_gain).astype(BF)
    height = plan(shards)[0]
    for s in range(shards):
        for cc in range(2):
            block = (s * 2 + cc) * 2 * height
            for xx in range(2):
                part = grad[block + xx * height : block + (xx + 1) * height]

                @pl.when(c == cc)
                def _():
                    mine_ref[s, xx] = part

                @pl.when(c != cc)
                def _():
                    other_ref[s, xx] = part


def h_one_grads_kernel(n_sum, idx, *refs):
    parts = refs[:n_sum]
    dq_ref, w_ref, gh_mine, gh_other = refs[n_sum:]
    rows = gh_mine.shape[1]
    for j in range(TP):
        at = slice(j * rows, (j + 1) * rows)
        total = parts[0][0, at, :].astype(F32)
        for part in parts[1:]:
            total += part[0, at, :].astype(F32)
        grad = jnp.concatenate([total.astype(BF), dq_ref[at, :]], axis=1)
        owner = lax.rem(idx[0] - j + TP, TP)
        target = gh_other if j % 2 else gh_mine
        target[owner // 2] = dot_nt(grad, w_ref[...]).astype(BF)


def tail_kernel(n_sum, idx, *refs):
    tok_ref, gmid_ref, gains_ref, out_ref = refs[n_sum:]
    unit, scale = normalise(tok_ref[...].astype(F32))
    total = 0.0
    for grad in refs[:n_sum]:
        grad = grad[idx[0] // 2] if len(grad.shape) == 3 else grad[...]
        total += grad.astype(F32)
    grad_unit = total * gains_ref[0:1, :]
    out_ref[...] = gmid_ref[...] + normalise_back(grad_unit, unit, scale)


def place_z(z, k):
    return lax.rem(z // 2 + k % 2, 2) * 2 + lax.rem(lax.rem(z, 2) + k // 2, 2)


def in_unpack_kernel(shards, idx, own, got, in_ref, held):
    rows_d, _, pad_d, _ = plan(shards)
    size = held.shape[0] // TP
    z, x, c = idx[0], idx[1], idx[2]
    for cr in range(2):
        for xr in range(2):
            for k in range(TP):
                at = pl.ds(pl.multiple_of(place_z(z, k) * size, size), size)
                held[at, :] = (got if cr else own)[xr, k].astype(F32)
            cc, xx = lax.rem(c + cr, 2), lax.rem(x + xr, 2)
            for t in range(2 * FF // 128):
                base = t * pad_d
                in_ref[cc, xx, :, t * 128 : t * 128 + 128] = held[base : base + rows_d, :]


def rest_unpack_kernel(shards, idx, own, got, out_ref, down_ref, gain_ref, held):
    rows_d, rows_f, pad_d, pad_f = plan(shards)
    size = held.shape[0] // TP
    z, x, c = idx[0], idx[1], idx[2]
    gain = None
    for cr in range(2):
        for xr in range(2):
            for k in range(TP):
                at = pl.ds(pl.multiple_of(place_z(z, k) * size, size), size)
                held[at, :] = (got if cr else own)[xr, k].astype(F32)
            cc, xx = lax.rem(c + cr, 2), lax.rem(x + xr, 2)
            down_ref[cc, xx] = held[0:rows_f, :]
            out_ref[cc, xx] = held[pad_f : pad_f + rows_d, :]
            if xr == 0:
                row = held[pad_f + pad_d : pad_f + pad_d + 8, :]
                gain = row if gain is None else gain + row
    part = gain_ref.shape[0]
    for s in range(shards):

        @pl.when(idx[3] == s)
        def _():
            gain_ref[...] = gain[0:1, s * part : (s + 1) * part].reshape(part)


def qkv_unpack_kernel(idx, own, got, out_ref, gain_ref, gain_s):
    z, x, c = idx[0], idx[1], idx[2]
    for cr in range(2):
        for xr in range(2):
            cc, xx = lax.rem(c + cr, 2), lax.rem(x + xr, 2)
            gain = None
            for g in range(TP):
                k = 2 * lax.rem(g % 2 + z, 2) + lax.rem(g // 2 + z // 2, 2)
                block = (got if cr else own)[xr, k].astype(F32)
                for source, place in ((0, 1), (1, 2), (2, 0)):
                    out_ref[cc, xx, :, place * D + g * GW : place * D + (g + 1) * GW] = block[
                        :, source * GW : (source + 1) * GW
                    ]
                tail = block[:, 512:640]
                gain = tail if gain is None else gain + tail
            height = gain.shape[0]
            at = pl.multiple_of((cc * 2 + xx) * height, height)
            gain_s[pl.ds(at, height), :] = gain
    gain_ref[...] = gain_s[...].T[64:65].reshape(gain_ref.shape)


def shift(value, axis, k):
    n = lax.axis_size(axis)
    return lax.ppermute(value, axis, [(i, (i + k) % n) for i in range(n)])


def gather(value, axis):
    return [value] + [shift(value, axis, k) for k in range(1, lax.axis_size(axis))]


def pick(value, index, dim):
    return lax.dynamic_index_in_dim(value, index, dim, keepdims=False)


def term(value, *views):
    return (value, views)


def take(index, dim):
    return lambda value: pick(value, index, dim)


def reshaped(*shape):
    return lambda value: value.reshape(shape)


def viewed(terms, view):
    return [(value, views + (view,)) for value, views in terms]


def reduce_step(order, terms, axis, dim):
    n, i = lax.axis_size(axis), lax.axis_index(axis)
    total = order.add(terms)
    got = [term(shift(pick(total, lax.rem(i + k, n), dim), axis, k)) for k in range(1, n)]
    return [term(pick(total, i, dim))] + got


def add(values):
    total = values[0].astype(F32)
    for value in values[1:]:
        total = total + value.astype(F32)
    return total.astype(BF)


def swap_z(value, bit):
    return lax.ppermute(value, "z", [(i, i ^ bit) for i in range(TP)])


def reduce_z(order, terms, bit):
    z = lax.axis_index("z")
    i, dim = (z % 2, 1) if bit == 1 else (z // 2, 0)
    total = order.add(terms)
    return [term(pick(total, i, dim)), term(swap_z(pick(total, 1 - i, dim), bit))]


def gather_z(order, value, bit):
    value = order.step(value)
    got = swap_z(value, bit)
    return jnp.stack([value, got]) if bit == 2 else jnp.concatenate([value, got])


def sum_over(value, axis):
    return add([value] + [shift(value, axis, k) for k in range(1, lax.axis_size(axis))])


def after(value, *others):
    return lax.optimization_barrier((value, *others))[0]


class Order:
    def __init__(self):
        self.last = None

    def __call__(self, values):
        if self.last is None:
            return values
        return lax.optimization_barrier((values, self.last))[0]

    def step(self, value):
        self.last = self(value)
        return self.last

    def add(self, terms):
        values = []
        for value, (_, views) in zip(self([t[0] for t in terms]), terms):
            for view in views:
                value = view(value)
            values.append(value)
        self.last = add(values)
        return self.last

    def run(self, body, outs, n_smem, ins, **more):
        got = call(body, outs, n_smem, self(list(ins)), **more)
        self.last = got[0]
        return got


def per_device(tokens, gain_one, w_qkv, w_out, gain_two, w_in, w_down, cotangent):
    tok, cot = tokens[0], cotangent[0]
    rows = tok.shape[0]
    many = TP * rows
    zo, z = lax.axis_index("zo"), lax.axis_index("z")
    x, c, y = lax.axis_index("x"), lax.axis_index("core"), lax.axis_index("shard")
    outer, shards = lax.axis_size("zo"), lax.axis_size("shard")
    part = w_qkv.shape[0]
    n_kv = 4 * outer
    keys = n_kv * many
    rows_d, rows_f, pad_d, pad_f = plan(shards)
    high_in, high = 2 * FF // 128 * pad_d, -(-(pad_f + pad_d + 16) // 64) * 64
    i32 = jnp.int32
    idx = jnp.stack([z, x, c, y]).astype(i32)
    order = Order()

    toks = gather(tok, "z")
    w_own, w_mine = order.run(
        group_kernel,
        [((part, WC), BF), ((part // 2 + 16, WC), BF)],
        1,
        [idx, w_qkv, gain_one, gain_two],
        hbm_ins=(1, 2, 3),
        name="group_columns",
    )
    w_slices = [w_own]
    for k in range(1, shards):
        w_slices.append(shift(w_mine, "shard", k))
        w_slices.append(shift(w_slices[-1], "core", 1))
    pack, pack_down = order.run(
        pack_kernel,
        [((2 * part, D), BF), ((down_half(down_half(w_down.shape[0])[0])[0], D), BF)],
        1,
        [idx, w_out, w_in, w_down],
        hbm_ins=(1, 2, 3),
        name="pack_weights",
    )
    downs = [shift(pack_down, "shard", k) for k in range(1, shards)]
    packs = [shift(pack, "shard", k) for k in range(1, shards)]

    freq = THETA ** (-jnp.arange(HEAD_DIM // 2, dtype=F32) * (2.0 / HEAD_DIM))
    owners = lax.rem(z - jnp.arange(TP, dtype=i32) + TP, TP)
    places = []
    for cr in range(2):
        for xr in range(2):
            for zr in range(outer):
                zz = lax.rem(zo - zr + outer, outer)
                place = ((zz * TP + owners) * 2 + lax.rem(x + xr, 2)) * 2 + lax.rem(c + cr, 2)
                places.append(place)
    first_place = jnp.concatenate(places) * rows
    freq = jnp.tile(freq, 4)[None, :]
    sign = jnp.where(jnp.arange(128) % 64 < 32, -1.0, 1.0).astype(F32)
    start = first_place.astype(F32)[:, None] * freq
    step = jnp.arange(rows, dtype=i32).astype(F32)[:, None] * freq
    cos_a, sin_a = jnp.cos(start)[:, None], jnp.sin(start)[:, None]
    cos_b, sin_b = jnp.cos(step)[None], jnp.sin(step)[None]
    cosine = (cos_a * cos_b - sin_a * sin_b).reshape(keys, 128)
    sine = ((sin_a * cos_b + cos_a * sin_b) * sign).reshape(keys, 128)

    query, kv, h_one, w_full, gains = order.run(
        functools.partial(front_kernel, shards),
        [
            ((many, 256), BF),
            ((many, 2 * GW), BF),
            ((many, D), BF),
            ((D, WC), BF),
            ((8, D), F32),
        ],
        1,
        [idx, *toks, *w_slices, w_mine, cosine, sine],
        hbm_ins=range(1, 1 + TP + len(w_slices) + 3),
        hbm_outs=(2, 3, 4),
        name="front",
    )

    near = gather(kv, "zo")
    near = near + [shift(v, "x", 1) for v in near]
    kv_core = shift(kv, "core", 1)
    close = (0, n_kv // 2)
    far = [i for i in range(n_kv) if i not in close]
    scratch = lambda count: [
        pltpu.VMEM((count * many, 2 * GW), BF),
        pltpu.VMEM((256, count * many), BF),
        pltpu.VMEM((256, many), BF),
    ]
    first = order.run(
        functools.partial(forward_kernel, 2, False),
        [((GW, many), F32), ((8, many), F32)],
        0,
        [query, kv, kv_core],
        scratch=scratch(2),
        name="attention_forward_near",
    )
    kvs = near + [kv_core] + [shift(after(v, *first), "core", 1) for v in near[1:]]
    downs = [jnp.stack([v, swap_z(v, 1)]) for v in downs]
    both_down = [v for p in downs for v in (p, shift(p, "core", 1))]
    first = [first[0], after(first[1], *both_down)]
    att = order.run(
        functools.partial(forward_kernel, len(far), True),
        [((rows * 3 // 2, 128), BF)] * TP + [((GW, many), F32), ((8, many), F32)],
        0,
        [query, *[kvs[i] for i in far], *first],
        scratch=scratch(len(far)),
        hbm_outs=(TP, TP + 1),
        name="attention_forward_far",
    )
    att_blocks, (attended_t, lse) = att[:TP], att[TP:]
    h_near = gather(after(h_one, lse), "zo")
    h_near = h_near + [shift(v, "x", 1) for v in h_near]
    h_core = shift(after(h_one, lse), "core", 1)
    atts = [att_blocks[0]] + [shift(att_blocks[k], "z", -k) for k in range(1, TP)]

    packs = [after(p, lse) for p in packs]
    both = [v for p in packs for v in (p, shift(p, "core", 1))]
    mid = order.run(
        functools.partial(middle_kernel, len(both)),
        [((rows, D), F32), ((rows, D), F32), ((rows, ACT_ALL), BF), ((8, D), F32)]
        + [((rows, 256), BF)] * TP,
        1,
        [idx, *atts, tok, cot, after(gains, h_core), w_out, w_in, w_down, *both, *both_down],
        scratch=[
            pltpu.VMEM((D, D), BF),
            pltpu.VMEM((D, 2 * FF), BF),
            pltpu.VMEM((FF, D), BF),
            pltpu.SemaphoreType.DMA((3 + 6 * len(both),)),
        ],
        any_ins=range(1 + TP + 3, 1 + TP + 6 + 2 * len(both)),
        hbm_ins=(1 + TP, 2 + TP, 3 + TP),
        hbm_outs=(0, 1, 3),
        name="feed_forward",
    )
    result, grad_middle, act, gain_two_row = mid[:4]
    act = after(act, *h_near)
    gatts = mid[4:]
    gas = [gatts[0]] + [shift(gatts[k], "z", k) for k in range(1, TP)]

    hs = h_near + [h_core] + [shift(after(v, result), "core", 1) for v in h_near[1:]]
    gain_two_row = after(gain_two_row, *hs)
    ffn = order.run(
        functools.partial(ffn_grads_kernel, shards),
        [((2, high_in, 128), BF)] * shards
        + [((shards, high, D), BF)] * 2,
        1,
        [idx, act, shift(act, "core", 1), gain_two_row],
        scratch=[
            pltpu.VMEM((4 * shards, pad_d, 2 * rows), BF),
            pltpu.VMEM((4 * shards, pad_f, 2 * rows), BF),
            pltpu.VMEM((4 * shards, pad_d, 2 * rows), BF),
            pltpu.VMEM((2 * rows, 2 * FF + 2 * D), BF),
        ],
        hbm_outs=range(shards + 2),
        name="ffn_weight_grads",
    )
    f_in = [term(ffn[0])]
    f_in += [term(shift(after(ffn[k], *gas), "shard", k)) for k in range(1, shards)]
    f_rest = [term(ffn[shards]), term(shift(after(ffn[shards + 1], *gas), "x", 1))]

    dkv_keep, dkv_send, dq = order.run(
        functools.partial(backward_kernel, n_kv),
        [((n_kv // 2, many, 2 * GW), BF)] * 2 + [((many, 256), BF)],
        0,
        [query, *kvs, *gas, attended_t, lse, cosine, sine],
        scratch=[
            pltpu.VMEM((keys, 2 * GW), BF),
            pltpu.VMEM((256, keys), BF),
            pltpu.VMEM((256, many), BF),
            pltpu.VMEM((256, many), BF),
            pltpu.VMEM((many, 2 * GW), BF),
            pltpu.VMEM((many, 2 * GW), BF),
            pltpu.VMEM((keys, 2 * GW), F32),
            pltpu.VMEM((256, many), F32),
        ],
        hbm_ins=range(0, 1 + n_kv + TP + 4),
        name="attention_backward",
    )
    mine, other = order.run(
        functools.partial(qkv_grads_kernel, shards, n_kv),
        [((shards, 2, rows_d, WC), BF)] * 2,
        1,
        [idx, *hs, dkv_keep, dkv_send, dq, w_full, gains],
        hbm_ins=range(1, 1 + n_kv),
        name="qkv_weight_grads",
    )
    first_got = [t[0] for t in f_in[1:] + f_rest[1:]]
    mine, other, *_ = lax.optimization_barrier((mine, other, *first_got))
    order.last = mine
    terms = [term(dkv_keep), term(shift(after(dkv_send, mine), "core", 1))]
    terms = viewed(terms, reshaped(2, outer, many, 2 * GW))
    wq = [term(mine), term(shift(other, "core", 1))]

    def pair(value):
        return jnp.stack([value, shift(order.step(value), "x", 1)])

    f_in = reduce_step(order, f_in, "x", 0)
    f_rest = reduce_step(order, f_rest, "shard", 0)
    wq = reduce_step(order, wq, "shard", 0)
    got = shift(order.add(viewed(terms, take(1, 0))), "x", 1)
    terms = viewed(terms, take(0, 0)) + [term(got)]
    f_in = reduce_z(order, viewed(f_in, reshaped(2, 2, high_in // TP, 128)), 1)
    f_rest = reduce_z(order, viewed(f_rest, reshaped(2, 2, high // TP, D)), 1)
    wq = reduce_step(order, wq, "x", 0)
    f_in = reduce_z(order, f_in, 2)
    f_rest = reduce_z(order, f_rest, 2)
    wq = gather_z(order, sum_over(order.add(wq), "zo"), 2)
    f_in = gather_z(order, sum_over(order.add(f_in), "zo"), 2)
    f_rest = gather_z(order, sum_over(order.add(f_rest), "zo"), 2)

    wq = gather_z(order, wq, 1)
    f_in = gather_z(order, f_in, 1)
    f_rest = gather_z(order, f_rest, 1)
    if outer > 1:
        total = order.add(terms)
        sums = [total[0:1]] + [shift(total[k : k + 1], "zo", -k) for k in range(1, outer)]
    else:
        sums = [
            dkv_keep.reshape(2, many, 2 * GW),
            terms[1][0].reshape(2, many, 2 * GW),
            got.reshape(1, many, 2 * GW),
        ]
    gh, gh_other = order.run(
        functools.partial(h_one_grads_kernel, len(sums)),
        [((2, rows, D), BF)] * 2,
        1,
        [idx, *sums, dq, w_full],
        name="h_one_grads",
    )
    wq = pair(wq)
    f_in = pair(after(f_in, f_rest))
    gh = [term(gh), term(swap_z(order(gh_other), 1))]
    wq = order.step(wq)
    wq_got = shift(wq, "core", 1)
    f_rest = pair(f_rest)
    gh = reduce_z(order, gh, 2)
    g_qkv, grad_gain_one = order.run(
        qkv_unpack_kernel,
        [((2, 2, rows_d, 3 * D), F32), ((part,), F32)],
        1,
        [idx, wq, wq_got],
        scratch=[pltpu.VMEM((part, 128), F32)],
        name="qkv_unpack",
    )
    f_in = order.step(f_in)
    f_in_got = shift(f_in, "core", 1)
    f_rest = order.step(after(f_rest, gh[1][0]))
    f_rest_got = shift(f_rest, "core", 1)
    (g_in,) = order.run(
        functools.partial(in_unpack_kernel, shards),
        [((2, 2, rows_d, 2 * FF), F32)],
        1,
        [idx, f_in, f_in_got],
        scratch=[pltpu.VMEM((high_in, 128), F32)],
        name="w_in_unpack",
    )
    (grad_tokens,) = order.run(
        functools.partial(tail_kernel, len(gh)),
        [((rows, D), F32)],
        1,
        [idx, *[t[0] for t in gh], tok, grad_middle, gains],
        name="token_grads",
    )

    g_out, g_down, grad_gain_two = order.run(
        functools.partial(rest_unpack_kernel, shards),
        [
            ((2, 2, rows_d, D), F32),
            ((2, 2, rows_f, D), F32),
            ((part,), F32),
        ],
        1,
        [idx, f_rest, f_rest_got],
        scratch=[pltpu.VMEM((high, D), F32)],
        name="w_down_w_out_unpack",
    )
    return (
        result[None],
        grad_tokens[None],
        grad_gain_one,
        g_qkv.reshape(part, 3 * D),
        g_out.reshape(part, D),
        grad_gain_two,
        g_in.reshape(part, 2 * FF),
        g_down.reshape(w_down.shape[0], D),
    )


def solution(mesh):
    blocks = mesh.shape["ctx"]
    fine = Mesh(
        mesh.devices.reshape(blocks // (TP * 4), TP, 2, 2, mesh.shape["shard"]), CTX + ("shard",)
    )
    rows, split = P("shard", CTX, None), P("shard", None)
    return jax.shard_map(
        per_device,
        mesh=fine,
        in_specs=(rows, P("shard"), split, split, P("shard"), split, split, rows),
        out_specs=(rows, rows, P("shard"), split, split, P("shard"), split, split),
        check_vma=False,
    )
```
